512 devices in a mesh: dp: 32 (over z, y_hi, core), space: 16 (over y_lo, x).
Axes of the slice: x: 4, y: 8 (y_hi: 2, y_lo: 4; y = y_hi * 4 + y_lo), z: 8, core: 2. Of those that a mesh axis runs over, the one named last changes fastest.
Arguments:
- state: bfloat16 [32, 16, 32, 32, 256], P('dp', 'space'), may hold values from -6 to 6
- cotangent: bfloat16 [32, 16, 32, 32, 256], P('dp', 'space'), may hold values from -0.01953125 to 0.01953125
- kernel: bfloat16 [49, 256], replicated, may hold values from -0.875 to 0.875
- ln_gain: float32 [256], replicated, may hold values from 0.5 to 1.5
- w_in: bfloat16 [256, 1024], replicated, may hold values from -0.375 to 0.375
- w_out: bfloat16 [1024, 256], replicated, may hold values from -0.1875 to 0.1875
- layer_scale: float32 [256], replicated, may hold values from 0.5 to 1.5
- neighbours: int32 [16, 8], replicated, may hold values from -1 to 15, as said below
- codes: int32 [16, 8], replicated, may hold values from 0 to 3
Outputs:
- kernel_grad: float32 [49, 256], replicated
- gain_grad: float32 [256], replicated
- scale_grad: float32 [256], replicated
- in_grad: bfloat16 [256, 1024], replicated
- out_grad: bfloat16 [1024, 256], replicated
The draws below stay inside these ranges and needn't reach their ends.
Inputs may be any that keep to these rules, and one draw needn't show every extreme that they name: `neighbours`: slots 0 to 3 name the tiles across a tile's sides clockwise from the top, slots 4 to 7 those across its corners, corner q lying between sides q - 1 and q; -1 marks a corner with no tile, which happens only in slots 4 to 7.
All inputs are finite; a program needn't handle non-finite values.
Results may differ from the reference program's by a relative error of at most 0.0072.
Values may be sent and summed in bfloat16 or wider, within the bound.
A program may use at most 64 MiB of HBM per device.

```python
import jax
import jax.numpy as jnp
from jax import lax

C = 256
HID = 1024
S = 32
TILES = 16
SAMPLES = 32


def draw_neighbours(key, part):
    key = jax.random.fold_in(key, 11)
    key_ids, key_gaps = jax.random.split(key)
    table = jax.random.randint(key_ids, (TILES, 8), 0, TILES)
    table = table.at[:, 0].set((jnp.arange(TILES) + 1) % TILES)
    absent = jax.random.randint(key_gaps, (TILES, 4), 0, 8) == 0
    corners = jnp.where(absent, -1, table[:, 4:])
    table = table.at[:, 4:].set(corners).at[0, 4].set(-1)
    return table.astype(jnp.int32)


def draw_codes(key, part):
    key = jax.random.fold_in(key, 23)
    table = jax.random.randint(key, (TILES, 8), 0, 4)
    table = table.at[0, 0].set(0).at[0, 1].set(3)
    return table.astype(jnp.int32)


def block_scale(key, extent, cuts, low, largest):
    factor_of = 1.0
    for axis_at, shards_of in cuts:
        heights = jax.random.uniform(jax.random.fold_in(jax.random.fold_in(key, 6), axis_at), (shards_of,), jnp.float32, low / len(cuts), largest / len(cuts))
        factor_of = factor_of * jnp.repeat(jnp.exp(heights), extent[axis_at] // shards_of).reshape((-1,) + (1,) * (len(extent) - 1 - axis_at))
    return factor_of


def noise(key, shape, spread, bound, shards=(), kind=jnp.bfloat16):
    factor_of = block_scale(key, shape, shards, -0.22, 0.18) if shards else 1.0
    array = jax.random.normal(key, shape, jnp.float32) * spread * factor_of
    return jnp.minimum(jnp.maximum(array, -bound), bound).astype(kind)


def setup_inputs(seed: int = 0) -> dict:
    arg_keys = jax.random.split(jax.random.key(seed), 10)
    return {
        "state": noise(arg_keys[0], (SAMPLES, TILES, S, S, C), 1.0, 6.0, ((0, 32), (1, 16))),
        "cotangent": noise(arg_keys[1], (SAMPLES, TILES, S, S, C), ((SAMPLES * TILES * S * S) ** -0.5), 0.01953125, ((0, 32), (1, 16))),
        "kernel": noise(arg_keys[2], (49, C), 49 ** -0.5, 0.875),
        "ln_gain": jnp.clip(jax.random.uniform(arg_keys[3], (C,), jnp.float32, 0.5, 1.5), 0.5, 1.5),
        "w_in": noise(arg_keys[4], (C, HID), C ** -0.5, 0.375),
        "w_out": noise(arg_keys[5], (HID, C), HID ** -0.5, 0.1875),
        "layer_scale": jnp.clip(jax.random.uniform(arg_keys[6], (C,), jnp.float32, 0.5, 1.5), 0.5, 1.5),
        "neighbours": draw_neighbours(jax.random.fold_in(arg_keys[9], 71), 0),
        "codes": draw_codes(jax.random.fold_in(arg_keys[9], 71), 0),
    }


EPSILON = 1e-06

def side_strips(tile):
    return jnp.stack([jnp.rot90(tile, turn, axes=(0, 1))[:3] for turn in range(4)])

def build_frame(tile, pieces, blocks):
    frame = jnp.pad(tile, ((3, 3), (3, 3), (0, 0)))
    for turn in range(4):
        turned = jnp.rot90(frame, turn, axes=(0, 1))
        turned = turned.at[0:3, 3:-3].set(pieces[turn]).at[0:3, 0:3].set(blocks[turn])
        frame = jnp.rot90(turned, -turn, axes=(0, 1))
    return frame

def facing_pieces(strips_all, tile_ids, tile_codes):
    present = tile_ids >= 0
    picked = strips_all[jnp.maximum(tile_ids, 0), tile_codes]
    pieces = picked[:, :4, ::-1, ::-1]
    corner = picked[:, 4:, :, :3][:, :, ::-1, ::-1]
    blocks = jnp.where(present[:, 4:, None, None, None], corner, jnp.zeros_like(corner))
    return (pieces, blocks)

def inner_rows(left, right):
    return lax.dot_general(left, right, (((0,), (0,)), ((), ())), preferred_element_type=jnp.float32)

def inner_cols(left, right):
    return lax.dot_general(left, right, (((1,), (1,)), ((), ())), preferred_element_type=jnp.float32)

def gelu_tanh(value):
    return jax.nn.gelu(value, approximate=True)

def block_grads(tiles, frames, cotan, kernel, ln_gain, w_in, w_out, layer_scale):
    side = tiles.shape[1]
    width = tiles.shape[3]
    depthwise = jnp.zeros(tiles.shape, jnp.float32)
    for offset in range(49):
        row_at, col_at = (offset // 7, offset % 7)
        window = frames[:, row_at:row_at + side, col_at:col_at + side].astype(jnp.float32)
        depthwise = depthwise + window * kernel[offset].astype(jnp.float32)
    flat = depthwise.reshape(-1, width)
    centered = flat - lax.optimization_barrier(jnp.mean(flat, axis=-1, keepdims=True))
    inverse = lax.rsqrt(lax.optimization_barrier(jnp.mean(centered * centered, axis=-1, keepdims=True)) + EPSILON)
    normed = centered * inverse
    scaled = (normed * ln_gain).astype(jnp.bfloat16)
    pre_act = jnp.dot(scaled, w_in, preferred_element_type=jnp.float32)
    hidden = gelu_tanh(pre_act).astype(jnp.bfloat16)
    output = jnp.dot(hidden, w_out, preferred_element_type=jnp.float32)
    upstream = cotan.reshape(-1, width).astype(jnp.float32)
    scale_grad = lax.optimization_barrier(jnp.sum(upstream * output, axis=0))
    branch = (upstream * layer_scale).astype(jnp.bfloat16)
    out_grad = inner_rows(hidden, branch)
    hidden_grad = inner_cols(branch, w_out)
    _, pullback = jax.vjp(gelu_tanh, pre_act)
    pre_grad = pullback(hidden_grad)[0].astype(jnp.bfloat16)
    in_grad = inner_rows(scaled, pre_grad)
    scaled_grad = inner_cols(pre_grad, w_in)
    gain_grad = lax.optimization_barrier(jnp.sum(scaled_grad * normed, axis=0))
    normed_grad = scaled_grad * ln_gain
    depth_grad = (normed_grad - lax.optimization_barrier(jnp.mean(normed_grad, axis=-1, keepdims=True)) - normed * lax.optimization_barrier(jnp.mean(normed_grad * normed, axis=-1, keepdims=True))) * inverse
    depth_grad = depth_grad.reshape(tiles.shape)
    kernel_rows = []
    for offset in range(49):
        row_at, col_at = (offset // 7, offset % 7)
        window = frames[:, row_at:row_at + side, col_at:col_at + side].astype(jnp.float32)
        kernel_rows.append(lax.optimization_barrier(jnp.sum(depth_grad * window, axis=(0, 1, 2))))
    return (jnp.stack(kernel_rows), gain_grad, scale_grad, in_grad, out_grad)

def reference(state, cotangent, kernel, ln_gain, w_in, w_out, layer_scale, neighbours, codes):
    width = state.shape[-1]
    hidden_width = w_in.shape[1]

    def one_sample(carry, pair):
        tiles, cotan = pair
        strips = jax.vmap(side_strips)(tiles)
        pieces, blocks = facing_pieces(strips, neighbours, codes)
        frames = jax.vmap(build_frame)(tiles, pieces, blocks)
        grads = block_grads(tiles, frames, cotan, kernel, ln_gain, w_in, w_out, layer_scale)
        return (tuple((total + term for total, term in zip(carry, grads))), None)
    start = (jnp.zeros((49, width), jnp.float32), jnp.zeros((width,), jnp.float32), jnp.zeros((width,), jnp.float32), jnp.zeros((width, hidden_width), jnp.float32), jnp.zeros((hidden_width, width), jnp.float32))
    totals, _ = lax.scan(one_sample, start, (state, cotangent))
    kernel_grad, gain_grad, scale_grad, in_grad, out_grad = totals
    return (kernel_grad, gain_grad, scale_grad, in_grad.astype(jnp.bfloat16), out_grad.astype(jnp.bfloat16))
```

```python
import jax
import jax.numpy as jnp
from jax import lax
from jax.experimental import pallas as pl
from jax.experimental.pallas import tpu as pltpu
from jax.sharding import PartitionSpec as P

EPSILON = 1e-06
MESH = pl.DeviceIdType.MESH
F32 = jnp.float32
BF16 = jnp.bfloat16

CORES, NX, NY_LO, NY_HI, NZ = 2, 4, 4, 2, 8
NY = NY_LO * NY_HI

S = 32
C = 256
HID = 1024
PIX = S * S
PITCH = 40
ROWS = 38


class Place:
    def __init__(self):
        dp = lax.axis_index("dp")
        space = lax.axis_index("space")
        self.core = lax.rem(dp, CORES)
        self.y_hi = lax.rem(dp // CORES, NY_HI)
        self.z = dp // (CORES * NY_HI)
        self.x = lax.rem(space, NX)
        self.y_lo = space // NX
        self.y = self.y_hi * NY_LO + self.y_lo
        self.dp = dp
        self.space = space

    def at(self, core=None, x=None, y=None, z=None):
        core = self.core if core is None else core
        x = self.x if x is None else x
        y = self.y if y is None else y
        z = self.z if z is None else z
        dp = (z * NY_HI + y // NY_LO) * CORES + core
        return {"dp": dp, "space": lax.rem(y, NY_LO) * NX + x}


def greet(devices):
    barrier = pltpu.get_barrier_semaphore()
    for device in devices:
        pl.semaphore_signal(barrier, inc=1, device_id=device, device_id_type=MESH)
    pl.semaphore_wait(barrier, len(devices))


class Copies:
    def __init__(self, send_sems, recv_sems):
        self.send_sems = send_sems
        self.recv_sems = recv_sems
        self.used = 0
        self.started = []

    def send(self, src, dst, device):
        copy = pltpu.make_async_remote_copy(
            src_ref=src,
            dst_ref=dst,
            send_sem=self.send_sems.at[self.used],
            recv_sem=self.recv_sems.at[self.used],
            device_id=device,
            device_id_type=MESH,
        )
        copy.start()
        self.used += 1
        self.started.append(copy)
        return copy

    def finish(self):
        for copy in self.started:
            copy.wait_send()


def rim_kernel(ids, codes, x_ref, sides, corners, xf, gath, out_s, out_c, in_s, in_c, cf, ss, rs):
    me = Place()
    y_lo, x = me.y_lo, me.x
    base = me.y_hi * NY_LO
    turn = reversal()
    xf[...] = x_ref[...].astype(F32)
    for r in range(3):
        gath[y_lo, 0, r] = x_ref[r]
        gath[y_lo, 2, r] = flip(turn, x_ref[S - 1 - r])
        gath[y_lo, 1, r] = xf[:, S - 1 - r, :].astype(BF16)
        gath[y_lo, 3, r] = flip(turn, xf[:, r, :].astype(BF16))
    along_y = [me.at(y=base + lax.rem(y_lo + k, NY_LO)) for k in range(1, NY_LO)]
    along_x = [me.at(x=lax.rem(x + k, NX)) for k in range(1, NX)]
    greet(along_y + along_x)
    net = Copies(ss, rs)
    first = [net.send(gath.at[y_lo], gath.at[y_lo], device) for device in along_y]
    for copy in first:
        copy.wait_recv()
    second = []
    for k in (2, 1, 3, 0):
        target = y_lo * NX + lax.rem(x + k, NX)
        for s in range(8):
            n = jnp.maximum(ids[target, s], 0)
            row = n // NX
            e = codes[target, s]
            if s < 4:
                piece = gath[row, e]
                if k:
                    out_s[k - 1, s] = piece
                else:
                    in_s[x, s] = piece
            else:
                piece = gath[row, e, :, 0:16, :].astype(F32)
                for r in range(3):
                    cf[pl.ds(16 * (s - 4) + 4 * r, 4), :] = piece[r, 0:4]
        if k:
            out_c[k - 1] = cf[...].astype(BF16)
            second.append(net.send(out_s.at[k - 1], in_s.at[x], along_x[k - 1]))
            second.append(net.send(out_c.at[k - 1], in_c.at[x], along_x[k - 1]))
        else:
            in_c[x] = cf[...].astype(BF16)
    for copy in second:
        copy.wait_recv()
    for s in range(8):
        n = ids[me.space, s]
        col = lax.rem(jnp.maximum(n, 0), NX)
        if s < 4:
            sides[s] = in_s[col, s]
        else:
            piece = in_c[col, pl.ds(16 * (s - 4), 16)]
            corners[s - 4] = jnp.where(n >= 0, piece, jnp.zeros_like(piece))
    net.finish()


def reversal():
    row = lax.broadcasted_iota(jnp.int32, (S, S), 0)
    col = lax.broadcasted_iota(jnp.int32, (S, S), 1)
    return jnp.where(row + col == S - 1, 1.0, 0.0).astype(BF16)


def flip(turn, rows):
    return jnp.dot(turn, rows, preferred_element_type=F32).astype(rows.dtype)


def exchange_rims(tile, neighbours, codes):
    copies = 3 + 6
    return pl.pallas_call(
        rim_kernel,
        out_shape=(
            jax.ShapeDtypeStruct((4, 3, S, C), BF16),
            jax.ShapeDtypeStruct((4, 16, C), BF16),
        ),
        in_specs=[
            pl.BlockSpec(memory_space=pltpu.SMEM),
            pl.BlockSpec(memory_space=pltpu.SMEM),
            pl.BlockSpec(memory_space=pltpu.VMEM),
        ],
        out_specs=(pl.BlockSpec(memory_space=pltpu.VMEM), pl.BlockSpec(memory_space=pltpu.VMEM)),
        scratch_shapes=[
            pltpu.VMEM((S, S, C), F32),
            pltpu.VMEM((NY_LO, 4, 3, S, C), BF16),
            pltpu.VMEM((NX - 1, 4, 3, S, C), BF16),
            pltpu.VMEM((NX - 1, 64, C), BF16),
            pltpu.VMEM((NX, 4, 3, S, C), BF16),
            pltpu.VMEM((NX, 64, C), BF16),
            pltpu.VMEM((64, C), F32),
            pltpu.SemaphoreType.DMA((copies,)),
            pltpu.SemaphoreType.DMA((copies,)),
        ],
        compiler_params=pltpu.CompilerParams(
            collective_id=0, has_side_effects=True, vmem_limit_bytes=32 * 2**20
        ),
    )(neighbours, codes, tile)


def build_frame(x_ref, sides, corners, fr, cf):
    turn = reversal()

    def interior(i, carry):
        fr[3 + i, 3 : 3 + S, :] = x_ref[i].astype(F32)
        return carry

    lax.fori_loop(0, S, interior, 0)
    for r in range(3):
        fr[r, 3 : 3 + S, :] = flip(turn, sides[0, 2 - r]).astype(F32)
        fr[3 : 3 + S, 35 + r, :] = flip(turn, sides[1, r]).astype(F32)
        fr[35 + r, 3 : 3 + S, :] = sides[2, r].astype(F32)
        fr[3 : 3 + S, r, :] = sides[3, 2 - r].astype(F32)
    cf[...] = corners[...].astype(F32)
    for i in range(3):
        for j in range(3):
            fr[i, j, :] = cf[0, 4 * (2 - i) + 2 - j, :]
            fr[i, 35 + j, :] = cf[1, 4 * j + 2 - i, :]
            fr[35 + i, 35 + j, :] = cf[2, 4 * i + j, :]
            fr[35 + i, j, :] = cf[3, 4 * (2 - j) + i, :]


def shift_frame(fr, fb):
    def one_row(i, carry):
        for b in range(7):
            fb[b, i] = fr[i, b : b + S, :]
        return carry

    lax.fori_loop(0, ROWS, one_row, 0)


def lanes(g):
    return (
        pl.ds(pl.multiple_of((g // 2) * 8, 8), 8),
        pl.ds(pl.multiple_of(lax.rem(g, 2) * 128, 128), 128),
    )


def depthwise(fb, taps, dw):
    def step(g, carry):
        cols, chans = lanes(g)
        acc = [None] * S
        for b in range(7):
            k = [jnp.broadcast_to(taps[pl.ds(7 * a + b, 1), chans], (8, 128)) for a in range(7)]
            for i in range(ROWS):
                f = fb[b, i, cols, chans]
                for a in range(7):
                    at = i - a
                    if 0 <= at < S:
                        term = f * k[a]
                        acc[at] = term if acc[at] is None else acc[at] + term
        for i in range(S):
            dw[i, cols, chans] = acc[i]
        return carry

    lax.fori_loop(0, 8, step, 0)


def correlate(fb, dg, kg):
    def step(g, carry):
        cols, chans = lanes(g)
        d = [dg[i, cols, chans] for i in range(S)]
        for b in range(7):
            acc = [None] * 7
            for i in range(ROWS):
                f = fb[b, i, cols, chans]
                for a in range(7):
                    at = i - a
                    if 0 <= at < S:
                        term = f * d[at]
                        acc[a] = term if acc[a] is None else acc[a] + term
            for a in range(7):
                kg[7 * a + b, :, chans] += acc[a]
        return carry

    kg[...] = jnp.zeros_like(kg)
    lax.fori_loop(0, 8, step, 0)


def gelu_and_slope(v):
    root = 0.7978845608028654
    square = v * v
    inner = v * (root + (root * 0.044715) * square)
    t = jnp.tanh(inner)
    half = 0.5 * (1.0 + t)
    slope = half + (0.5 * v) * (1.0 - t * t) * (root + (3.0 * root * 0.044715) * square)
    return v * half, slope


def nt(left, right):
    return lax.dot_general(left, right, (((1,), (1,)), ((), ())), preferred_element_type=F32)


def block_kernel(
    x_ref, cot, taps_in, gain, w_in, w_in_t, w_out, layer, sides, corners,
    big, small,
    fr, cf, fb, taps, dw, inv, scaled, scaled_t, branch, pre, hg, hid, pg, sg_t, kg,
):
    build_frame(x_ref, sides, corners, fr, cf)
    shift_frame(fr, fb)
    taps[...] = taps_in[...].astype(F32)
    depthwise(fb, taps, dw)

    def norm(q, carry):
        rows = pl.ds(q * 4, 4)
        flat = pl.ds(pl.multiple_of(q * 128, 128), 128)
        v = dw[rows].reshape(128, C)
        mean = jnp.mean(v, axis=-1, keepdims=True)
        v = v - mean
        inverse = lax.rsqrt(jnp.mean(v * v, axis=-1, keepdims=True) + EPSILON)
        normed = v * inverse
        inv[flat] = jnp.broadcast_to(inverse, (128, 128))
        dw[rows] = normed.reshape(4, S, C)
        scaled[flat] = (normed * gain[...]).astype(BF16)
        branch[flat] = (cot[flat].astype(F32) * layer[...]).astype(BF16)
        return carry

    lax.fori_loop(0, 8, norm, 0)
    scaled_t[...] = scaled[...].T

    scale_grad = jnp.zeros((1, C), F32)
    for h in range(HID // 256):
        part = slice(256 * h, 256 * h + 256)
        pre[...] = jnp.dot(w_in_t[part], scaled_t[...], preferred_element_type=F32)
        hg[...] = nt(w_out[part], branch[...])

        def act(q, carry):
            rows = pl.ds(pl.multiple_of(q * 16, 16), 16)
            out = pl.ds(pl.multiple_of(256 * h + q * 16, 16), 16)
            value, slope = gelu_and_slope(pre[rows])
            hid[rows] = value.astype(BF16)
            pg[out] = (hg[rows] * slope).astype(BF16)
            return carry

        lax.fori_loop(0, 16, act, 0)
        g = jnp.dot(hid[...], cot[...], preferred_element_type=F32)
        big[part] = (g * layer[...]).astype(BF16)
        scale_grad += jnp.sum(g * w_out[part].astype(F32), axis=0, keepdims=True)
        big[slice(HID + 256 * h, HID + 256 * h + 256)] = nt(scaled_t[...], pg[part]).astype(BF16)
    sg_t[...] = jnp.dot(w_in[...], pg[...], preferred_element_type=F32)

    gain_grad = jnp.zeros((1, C), F32)
    for q in range(8):
        rows = slice(4 * q, 4 * q + 4)
        flat = slice(128 * q, 128 * q + 128)
        normed = dw[rows].reshape(128, C)
        sg = sg_t[:, flat].T
        gain_grad += jnp.sum(sg * normed, axis=0, keepdims=True)
        g = sg * gain[...]
        mean = jnp.mean(g, axis=-1, keepdims=True)
        along = jnp.mean(g * normed, axis=-1, keepdims=True)
        inverse = inv[flat]
        grad = (g - mean - normed * along) * jnp.concatenate([inverse, inverse], axis=1)
        dw[rows] = grad.reshape(4, S, C)
    correlate(fb, dw, kg)
    small[0:49] = jnp.sum(kg[...], axis=1)
    small[49:50] = gain_grad
    small[50:51] = scale_grad
    small[51:64] = jnp.zeros((13, C), F32)


def own_grads(tile, cot, kernel, ln_gain, w_in, w_out, layer_scale, sides, corners):
    vmem = pl.BlockSpec(memory_space=pltpu.VMEM)
    return pl.pallas_call(
        block_kernel,
        out_shape=(
            jax.ShapeDtypeStruct((2 * HID, C), BF16),
            jax.ShapeDtypeStruct((64, C), F32),
        ),
        in_specs=[vmem] * 10,
        out_specs=(vmem, vmem),
        scratch_shapes=[
            pltpu.VMEM((ROWS, PITCH, C), F32),
            pltpu.VMEM((4, 16, C), F32),
            pltpu.VMEM((7, ROWS, S, C), F32),
            pltpu.VMEM((49, C), F32),
            pltpu.VMEM((S, S, C), F32),
            pltpu.VMEM((PIX, 128), F32),
            pltpu.VMEM((PIX, C), BF16),
            pltpu.VMEM((C, PIX), BF16),
            pltpu.VMEM((PIX, C), BF16),
            pltpu.VMEM((256, PIX), F32),
            pltpu.VMEM((256, PIX), F32),
            pltpu.VMEM((256, PIX), BF16),
            pltpu.VMEM((HID, PIX), BF16),
            pltpu.VMEM((C, PIX), F32),
            pltpu.VMEM((49, 8, C), F32),
        ],
        compiler_params=pltpu.CompilerParams(vmem_limit_bytes=48 * 2**20),
    )(
        tile, cot, kernel, ln_gain.reshape(1, C), w_in, w_in.T, w_out,
        layer_scale.reshape(1, C), sides, corners,
    )


def sum_kernel(
    big, small, kg_out, gain_out, scale_out, in_out, out_out,
    r0, s1, r1, s2, r2, s3, r3, fin, q0, t1, q1, t2, q2, t3, q3, sfin, ss, rs,
):
    me = Place()
    core, x, y, z = me.core, me.x, me.y, me.z
    other = 1 - core
    mate = me.at(core=other)
    along_x = [me.at(x=lax.rem(x + k, NX)) for k in range(1, NX)]
    along_y = [me.at(y=lax.rem(y + k, NY)) for k in range(1, NY)]
    along_z = [me.at(z=lax.rem(z + k, NZ)) for k in range(1, NZ)]
    greet([mate] + along_x + along_y + along_z)
    net = Copies(ss, rs)
    far_first = (4, 3, 5, 2, 6, 1, 7)

    halves = []
    small_half = net.send(
        small.at[pl.ds(pl.multiple_of(other * 32, 32), 32)], q0, mate
    )
    order = (2, 1, 3, 0)
    for k in order:
        at = lax.rem(x + k, NX)
        halves.append(
            net.send(
                big.at[pl.ds(pl.multiple_of(other * HID + at * 256, 256), 256)], r0.at[at], mate
            )
        )
    small_half.wait_recv()
    t1[...] = (small[pl.ds(pl.multiple_of(core * 32, 32), 32)] + q0[...]).reshape(NX, 8, C)
    small_x = [
        net.send(t1.at[lax.rem(x + k, NX)], q1.at[k - 1], along_x[k - 1]) for k in range(1, NX)
    ]
    big_x = []
    for k, copy in zip(order, halves):
        at = lax.rem(x + k, NX)
        copy.wait_recv()
        own = big[pl.ds(pl.multiple_of(core * HID + at * 256, 256), 256)]
        s1[at] = (own.astype(F32) + r0[at].astype(F32)).astype(BF16)
        if k:
            big_x.append(net.send(s1.at[at], r1.at[k - 1], along_x[k - 1]))

    for copy in small_x:
        copy.wait_recv()
    t2[...] = t1[x] + q1[0] + q1[1] + q1[2]
    q2[y] = t2[...]
    small_y = [net.send(t2, q2.at[y], along_y[k - 1]) for k in far_first]
    for copy in big_x:
        copy.wait_recv()
    total = s1[x].astype(F32)
    for k in range(NX - 1):
        total += r1[k].astype(F32)
    s2[...] = total.astype(BF16).reshape(NY, 32, C)
    big_y = [
        net.send(s2.at[lax.rem(y + k, NY)], r2.at[k - 1], along_y[k - 1]) for k in far_first
    ]
    for copy in small_y:
        copy.wait_recv()
    t3[...] = jnp.sum(q2[...], axis=0)
    q3[z] = t3[...]
    small_z = [net.send(t3, q3.at[z], along_z[k - 1]) for k in far_first]
    for copy in big_y:
        copy.wait_recv()
    total = s2[y].astype(F32)
    for k in range(NY - 1):
        total += r2[k].astype(F32)
    s3[...] = total.astype(BF16)
    r3[z] = s3[...]
    big_z = [net.send(s3, r3.at[z], along_z[k - 1]) for k in far_first]
    for copy in small_z:
        copy.wait_recv()
    sfin[core, x] = jnp.sum(q3[...], axis=0)
    small_back = [net.send(sfin.at[core, x], sfin.at[core, x], device) for device in along_x]
    for copy in big_z:
        copy.wait_recv()
    total = r3[0].astype(F32)
    for k in range(1, NZ):
        total += r3[k].astype(F32)
    fin[core, x, y] = total.astype(BF16)

    back_y = [
        net.send(fin.at[core, x, y], fin.at[core, x, y], along_y[k - 1]) for k in far_first
    ]
    for copy in small_back:
        copy.wait_recv()
    small_mate = net.send(sfin.at[core], sfin.at[core], mate)
    for copy in back_y:
        copy.wait_recv()
    back_x = [
        net.send(fin.at[core, x], fin.at[core, x], along_x[k - 1]) for k in (2, 1, 3)
    ]
    back_mate = [net.send(fin.at[core, x], fin.at[core, x], mate)]
    for k, copy in zip((2, 1, 3), back_x):
        copy.wait_recv()
        at = lax.rem(x + NX - k, NX)
        back_mate.append(net.send(fin.at[core, at], fin.at[core, at], mate))
    small_mate.wait_recv()
    rows = sfin[...].reshape(64, C)
    kg_out[...] = rows[0:49]
    gain_out[...] = rows[49:50]
    scale_out[...] = rows[50:51]
    for copy in back_mate:
        copy.wait_recv()
    out_out[...] = fin[0].reshape(HID, C)
    for q in range(NX):
        in_out[:, 256 * q : 256 * q + 256] = fin[1, q].reshape(256, C)
    net.finish()


def sum_grads(big, small):
    vmem = pl.BlockSpec(memory_space=pltpu.VMEM)
    copies = 1 + 4 + 3 + 3 + 7 * 5 + 3 + 1 + 3 + 4
    return pl.pallas_call(
        sum_kernel,
        out_shape=(
            jax.ShapeDtypeStruct((49, C), F32),
            jax.ShapeDtypeStruct((1, C), F32),
            jax.ShapeDtypeStruct((1, C), F32),
            jax.ShapeDtypeStruct((C, HID), BF16),
            jax.ShapeDtypeStruct((HID, C), BF16),
        ),
        in_specs=[vmem, vmem],
        out_specs=(vmem,) * 5,
        scratch_shapes=[
            pltpu.VMEM((NX, 256, C), BF16),
            pltpu.VMEM((NX, 256, C), BF16),
            pltpu.VMEM((NX - 1, 256, C), BF16),
            pltpu.VMEM((NY, 32, C), BF16),
            pltpu.VMEM((NY - 1, 32, C), BF16),
            pltpu.VMEM((32, C), BF16),
            pltpu.VMEM((NZ, 32, C), BF16),
            pltpu.VMEM((2, NX, NY, 32, C), BF16),
            pltpu.VMEM((32, C), F32),
            pltpu.VMEM((NX, 8, C), F32),
            pltpu.VMEM((NX - 1, 8, C), F32),
            pltpu.VMEM((8, C), F32),
            pltpu.VMEM((NY, 8, C), F32),
            pltpu.VMEM((8, C), F32),
            pltpu.VMEM((NZ, 8, C), F32),
            pltpu.VMEM((2, NX, 8, C), F32),
            pltpu.SemaphoreType.DMA((copies,)),
            pltpu.SemaphoreType.DMA((copies,)),
        ],
        compiler_params=pltpu.CompilerParams(
            collective_id=1, has_side_effects=True, vmem_limit_bytes=32 * 2**20
        ),
    )(big, small)


def on_device(state, cotangent, kernel, ln_gain, w_in, w_out, layer_scale, neighbours, codes):
    tile = state.reshape(S, S, C)
    cot = cotangent.reshape(PIX, C)
    sides, corners = exchange_rims(tile, neighbours, codes)
    big, small = own_grads(
        tile, cot, kernel, ln_gain, w_in, w_out, layer_scale, sides, corners
    )
    kernel_grad, gain_grad, scale_grad, in_grad, out_grad = sum_grads(big, small)
    return (kernel_grad, gain_grad.reshape(C), scale_grad.reshape(C), in_grad, out_grad)


def solution(mesh):
    placed = (P("dp", "space", None, None, None),) * 2 + (P(),) * 7
    return jax.shard_map(
        on_device, mesh=mesh, in_specs=placed, out_specs=(P(),) * 5, check_vma=False
    )
```

```python
import jax
import jax.numpy as jnp
from jax import lax
from jax.experimental import pallas as pl
from jax.experimental.pallas import tpu as pltpu
from jax.sharding import PartitionSpec as P

EPSILON = 1e-06
MESH = pl.DeviceIdType.MESH
F32 = jnp.float32
BF16 = jnp.bfloat16

CORES, NX, NY_LO, NY_HI, NZ = 2, 4, 4, 2, 8
NY = NY_LO * NY_HI

S = 32
C = 256
HID = 1024
PIX = S * S
PITCH = 40
ROWS = 38


class Place:
    def __init__(self):
        dp = lax.axis_index("dp")
        space = lax.axis_index("space")
        self.core = lax.rem(dp, CORES)
        self.y_hi = lax.rem(dp // CORES, NY_HI)
        self.z = dp // (CORES * NY_HI)
        self.x = lax.rem(space, NX)
        self.y_lo = space // NX
        self.y = self.y_hi * NY_LO + self.y_lo
        self.dp = dp
        self.space = space

    def at(self, core=None, x=None, y=None, z=None):
        core = self.core if core is None else core
        x = self.x if x is None else x
        y = self.y if y is None else y
        z = self.z if z is None else z
        dp = (z * NY_HI + y // NY_LO) * CORES + core
        return {"dp": dp, "space": lax.rem(y, NY_LO) * NX + x}


def greet(devices):
    barrier = pltpu.get_barrier_semaphore()
    for device in devices:
        pl.semaphore_signal(barrier, inc=1, device_id=device, device_id_type=MESH)
    pl.semaphore_wait(barrier, len(devices))


class Copies:
    def __init__(self, send_sems, recv_sems):
        self.send_sems = send_sems
        self.recv_sems = recv_sems
        self.used = 0
        self.started = []

    def send(self, src, dst, device):
        copy = pltpu.make_async_remote_copy(
            src_ref=src,
            dst_ref=dst,
            send_sem=self.send_sems.at[self.used],
            recv_sem=self.recv_sems.at[self.used],
            device_id=device,
            device_id_type=MESH,
        )
        copy.start()
        self.used += 1
        self.started.append(copy)
        return copy

    def finish(self):
        for copy in self.started:
            copy.wait_send()


HALF = C // 2


def own_strips(x_ref, xf, gath_y, gath_x, me):
    turn = reversal()
    xf[...] = x_ref[...].astype(F32)

    def put(side, r, rows):
        gath_y[me.y_lo, side, r] = rows[:, :HALF]
        gath_x[me.x, side, r] = rows[:, HALF:]

    for r in range(3):
        put(0, r, x_ref[r])
        put(2, r, flip(turn, x_ref[S - 1 - r]))
        put(1, r, xf[:, S - 1 - r, :].astype(BF16))
        put(3, r, flip(turn, xf[:, r, :].astype(BF16)))


class Rims:
    def __init__(self, net, ids, codes, gath, out_s, out_c, in_s, in_c, cf, gather_at, choose_at, gather_to, choose_to, tile_at, split):
        self.net = net
        self.ids, self.codes = ids, codes
        self.gath, self.out_s, self.out_c, self.in_s, self.in_c, self.cf = gath, out_s, out_c, in_s, in_c, cf
        self.gather_at, self.choose_at = gather_at, choose_at
        self.gather_to, self.choose_to = gather_to, choose_to
        self.tile_at, self.split = tile_at, split

    def gather(self):
        at = self.gather_at
        self.first = [
            self.net.send(self.gath.at[at], self.gath.at[at], self.gather_to[k - 1])
            for k in (2, 1, 3)
        ]

    def choose(self):
        for copy in self.first:
            copy.wait_recv()
        self.second = []
        at = self.choose_at
        for k in (2, 1, 3, 0):
            target = self.tile_at(lax.rem(at + k, 4))
            for s in range(8):
                row, _ = self.split(jnp.maximum(self.ids[target, s], 0))
                e = self.codes[target, s]
                if s < 4:
                    piece = self.gath[row, e]
                    if k:
                        self.out_s[k - 1, s] = piece
                    else:
                        self.in_s[at, s] = piece
                else:
                    piece = self.gath[row, e, :, 0:16, :].astype(F32)
                    for r in range(3):
                        self.cf[pl.ds(16 * (s - 4) + 4 * r, 4), :] = piece[r, 0:4]
            packed = self.cf[...].astype(BF16)
            if k:
                self.out_c[k - 1] = packed
                to = self.choose_to[k - 1]
                self.second.append(self.net.send(self.out_s.at[k - 1], self.in_s.at[at], to))
                self.second.append(self.net.send(self.out_c.at[k - 1], self.in_c.at[at], to))
            else:
                self.in_c[at] = packed

    def take(self, sides, corners, chans, space):
        for copy in self.second:
            copy.wait_recv()
        for s in range(8):
            n = self.ids[space, s]
            _, col = self.split(jnp.maximum(n, 0))
            if s < 4:
                sides[s, :, :, chans] = self.in_s[col, s]
            else:
                piece = self.in_c[col, pl.ds(16 * (s - 4), 16)]
                corners[s - 4, :, chans] = jnp.where(n >= 0, piece, jnp.zeros_like(piece))


def both_rims(net, me, ids, codes, along_y, along_x, bufs_y, bufs_x):
    by_y = Rims(
        net, ids, codes, *bufs_y, me.y_lo, me.x, along_y, along_x,
        lambda x: me.y_lo * NX + x, lambda n: (n // NX, lax.rem(n, NX)),
    )
    by_x = Rims(
        net, ids, codes, *bufs_x, me.x, me.y_lo, along_x, along_y,
        lambda y: y * NX + me.x, lambda n: (lax.rem(n, NX), n // NX),
    )
    return by_y, by_x


def rim_partners(me):
    base = me.y_hi * NY_LO
    along_y = [me.at(y=base + lax.rem(me.y_lo + k, NY_LO)) for k in range(1, NY_LO)]
    along_x = [me.at(x=lax.rem(me.x + k, NX)) for k in range(1, NX)]
    return along_y, along_x


RIM_COPIES = 2 * 9


def rim_scratch():
    half = [
        pltpu.VMEM((4, 4, 3, S, HALF), BF16),
        pltpu.VMEM((3, 4, 3, S, HALF), BF16),
        pltpu.VMEM((3, 64, HALF), BF16),
        pltpu.VMEM((4, 4, 3, S, HALF), BF16),
        pltpu.VMEM((4, 64, HALF), BF16),
        pltpu.VMEM((64, HALF), F32),
    ]
    return half * 2


def reversal():
    row = lax.broadcasted_iota(jnp.int32, (S, S), 0)
    col = lax.broadcasted_iota(jnp.int32, (S, S), 1)
    return jnp.where(row + col == S - 1, 1.0, 0.0).astype(BF16)


def flip(turn, rows):
    return jnp.dot(turn, rows, preferred_element_type=F32).astype(rows.dtype)


INNER = S - 6
IN_PIX = INNER * S
IN_PAD = 896
EDGE = 3 * S
SIDE_AT = 2 * EDGE
OUT_PIX = SIDE_AT + INNER * 8
OUT_PAD = 512


def frame_inside(xf, fr):
    fr[...] = jnp.zeros_like(fr)

    def one_row(i, carry):
        fr[3 + i, 3 : 3 + S, :] = xf[i]
        return carry

    lax.fori_loop(0, S, one_row, 0)


def frame_rims(sides, corners, fr, cf):
    turn = reversal()
    for r in range(3):
        fr[r, 3 : 3 + S, :] = flip(turn, sides[0, 2 - r]).astype(F32)
        fr[3 : 3 + S, 35 + r, :] = flip(turn, sides[1, r]).astype(F32)
        fr[35 + r, 3 : 3 + S, :] = sides[2, r].astype(F32)
        fr[3 : 3 + S, r, :] = sides[3, 2 - r].astype(F32)
    cf[...] = corners[...].astype(F32)
    for i in range(3):
        for j in range(3):
            fr[i, j, :] = cf[0, 4 * (2 - i) + 2 - j, :]
            fr[i, 35 + j, :] = cf[1, 4 * j + 2 - i, :]
            fr[35 + i, 35 + j, :] = cf[2, 4 * i + j, :]
            fr[35 + i, j, :] = cf[3, 4 * (2 - j) + i, :]


def shift_rows(fr, fb, first, count):
    def one_row(i, carry):
        for b in range(7):
            fb[b, first + i] = fr[first + i, b : b + S, :]
        return carry

    lax.fori_loop(0, count, one_row, 0)


def shift_sides(fr, fs):
    fs[...] = jnp.zeros_like(fs)

    def one_row(i, carry):
        for b in range(7):
            fs[b, i, 0:3, :] = fr[3 + i, b : b + 3, :]
            fs[b, i, 3:6, :] = fr[3 + i, 29 + b : 32 + b, :]
        return carry

    lax.fori_loop(0, S, one_row, 0)


def lanes(g):
    return (
        pl.ds(pl.multiple_of((g // 2) * 8, 8), 8),
        pl.ds(pl.multiple_of(lax.rem(g, 2) * 128, 128), 128),
    )


def convolve(load, taps, chans, count, put):
    acc = [None] * count
    for b in range(7):
        k = [jnp.broadcast_to(taps[pl.ds(7 * a + b, 1), chans], (8, 128)) for a in range(7)]
        for i in range(count + 6):
            f = load(b, i)
            for a in range(7):
                at = i - a
                if 0 <= at < count:
                    term = f * k[a]
                    acc[at] = term if acc[at] is None else acc[at] + term
    for i in range(count):
        put(i, acc[i])


def correlate(load, d, kg, chans):
    count = len(d)
    for b in range(7):
        acc = [None] * 7
        for i in range(count + 6):
            f = load(b, i)
            for a in range(7):
                at = i - a
                if 0 <= at < count:
                    term = f * d[at]
                    acc[a] = term if acc[a] is None else acc[a] + term
        for a in range(7):
            kg[7 * a + b, :, chans] += acc[a]


def normalise(v):
    mean = jnp.mean(v, axis=-1, keepdims=True)
    v = v - mean
    inverse = lax.rsqrt(jnp.mean(v * v, axis=-1, keepdims=True) + EPSILON)
    return v * inverse, inverse


def norm_backward(sg, normed, inverse, gain):
    g = sg * gain
    mean = jnp.mean(g, axis=-1, keepdims=True)
    along = jnp.mean(g * normed, axis=-1, keepdims=True)
    return (g - mean - normed * along) * jnp.concatenate([inverse, inverse], axis=1)


def gelu_and_slope(v):
    root = 0.7978845608028654
    square = v * v
    inner = v * (root + (root * 0.044715) * square)
    t = jnp.tanh(inner)
    half = 0.5 * (1.0 + t)
    slope = half + (0.5 * v) * (1.0 - t * t) * (root + (3.0 * root * 0.044715) * square)
    return v * half, slope


def dot(left, right):
    return jnp.dot(left, right, preferred_element_type=F32)


class Inside:
    def __init__(self, w, fb, bufs):
        self.w, self.fb = w, fb
        (self.normed, self.inv, self.scaled, self.cot, self.branch, self.scaled_t, self.cot_t,
         self.pre, self.hg, self.hid, self.pg, self.sg) = bufs

    def depthwise(self):
        def step(g, carry):
            cols, chans = lanes(g)

            def put(i, value):
                self.normed[i, cols, chans] = value

            convolve(lambda b, i: self.fb[b, 3 + i, cols, chans], self.w.taps, chans, INNER, put)
            return carry

        lax.fori_loop(0, 8, step, 0)

    def norm(self):
        w = self.w
        col = lax.rem(lax.broadcasted_iota(jnp.int32, (64, C), 0), S)
        here = (col >= 3) & (col < S - 3)

        def step(q, carry):
            rows = pl.ds(q * 2, 2)
            flat = pl.ds(pl.multiple_of(q * 64, 64), 64)
            normed, inverse = normalise(self.normed[rows].reshape(64, C))
            self.inv[flat] = jnp.broadcast_to(inverse, (64, 128))
            self.normed[rows] = normed.reshape(2, S, C)
            self.scaled[flat] = (normed * w.gain[...]).astype(BF16)
            cot = w.cot[pl.ds(pl.multiple_of(3 * S + q * 64, 32), 64)].astype(F32)
            cot = jnp.where(here, cot, jnp.zeros_like(cot))
            self.cot[flat] = cot.astype(BF16)
            self.branch[flat] = (cot * w.layer[...]).astype(BF16)
            return carry

        lax.fori_loop(0, INNER // 2, step, 0)
        rest = slice(IN_PIX, IN_PAD)
        none = jnp.zeros((IN_PAD - IN_PIX, C), BF16)
        self.scaled[rest] = none
        self.cot[rest] = none
        self.hid[rest] = none
        for h in range(4):
            self.pg[rest, 256 * h : 256 * h + 256] = none
        self.scaled_t[...] = self.scaled[...].T
        self.cot_t[...] = self.cot[...].T

    def hidden(self, h, gacc, iacc):
        w = self.w
        part = slice(256 * h, 256 * h + 256)
        self.pre[...] = dot(self.scaled[0:IN_PIX], w.w_in[:, part])
        self.hg[...] = dot(self.branch[...], w.w_out_t[:, part])

        def act(q, carry):
            rows = pl.ds(pl.multiple_of(q * 32, 32), 32)
            value, slope = gelu_and_slope(self.pre[rows])
            self.hid[rows] = value.astype(BF16)
            self.pg[rows, part] = (self.hg[rows] * slope).astype(BF16)
            return carry

        lax.fori_loop(0, IN_PIX // 32, act, 0)
        gacc[:, part] = dot(self.cot_t[...], self.hid[...])
        iacc[:, part] = dot(self.scaled_t[...], self.pg[:, part])

    def backward(self, gain_acc):
        w = self.w
        self.sg[...] = dot(self.pg[0:IN_PIX], w.w_in_t[...])

        def step(q, total):
            rows = pl.ds(q * 2, 2)
            flat = pl.ds(pl.multiple_of(q * 64, 64), 64)
            normed = self.normed[rows].reshape(64, C)
            sg = self.sg[flat]
            grad = norm_backward(sg, normed, self.inv[flat], w.gain[...])
            self.normed[rows] = grad.reshape(2, S, C)
            return total + jnp.sum((sg * normed).reshape(8, 8, C), axis=0)

        gain_acc[...] = lax.fori_loop(0, INNER // 2, step, jnp.zeros((8, C), F32))

    def kernel_grad(self, kg):
        def step(g, carry):
            cols, chans = lanes(g)
            d = [self.normed[i, cols, chans] for i in range(INNER)]
            correlate(lambda b, i: self.fb[b, 3 + i, cols, chans], d, kg, chans)
            return carry

        lax.fori_loop(0, 8, step, 0)


class Border:
    def __init__(self, w, fb, fs, bufs):
        self.w, self.fb, self.fs = w, fb, fs
        (self.normed, self.inv, self.scaled, self.cot, self.branch, self.scaled_t, self.cot_t,
         self.pre, self.hg, self.hid, self.pg, self.sg, self.cf) = bufs

    def cotangent(self):
        w = self.w
        self.cf[...] = jnp.zeros_like(self.cf)
        self.cf[0:EDGE] = w.cot[0:EDGE].astype(F32)
        self.cf[EDGE : 2 * EDGE] = w.cot[PIX - EDGE : PIX].astype(F32)
        for i in range(INNER):
            row = w.cot[(3 + i) * S : (4 + i) * S].astype(F32)
            at = SIDE_AT + 8 * i
            self.cf[at : at + 3] = row[0:3]
            self.cf[at + 3 : at + 6] = row[29:32]
        self.cot[...] = self.cf[...].astype(BF16)
        self.branch[...] = (self.cf[...] * w.layer[...]).astype(BF16)
        self.cot_t[...] = self.cot[...].T
        rest = slice(OUT_PIX, OUT_PAD)
        none = jnp.zeros((OUT_PAD - OUT_PIX, C), BF16)
        self.scaled[rest] = none
        for h in range(4):
            self.hid[rest, 256 * h : 256 * h + 256] = none
            self.pg[rest, 256 * h : 256 * h + 256] = none

    def depthwise(self):
        for chans in (slice(0, 128), slice(128, 256)):

            def put_side(i, value):
                self.normed[SIDE_AT + 8 * i : SIDE_AT + 8 * i + 8, chans] = value

            convolve(lambda b, i: self.fs[b, i, :, chans], self.w.taps, chans, INNER, put_side)
            for first, at in ((0, 0), (S - 3, EDGE)):
                for j in range(0, S, 8):

                    def put(i, value):
                        self.normed[at + S * i + j : at + S * i + j + 8, chans] = value

                    convolve(
                        lambda b, i: self.fb[b, first + i, j : j + 8, chans],
                        self.w.taps, chans, 3, put,
                    )

    def norm(self):
        w = self.w
        for at in range(0, OUT_PIX, 80):
            rows = slice(at, at + 80)
            normed, inverse = normalise(self.normed[rows])
            self.inv[rows] = jnp.broadcast_to(inverse, (80, 128))
            self.normed[rows] = normed
            self.scaled[rows] = (normed * w.gain[...]).astype(BF16)
        self.scaled_t[...] = self.scaled[...].T

    def products(self, h):
        part = slice(256 * h, 256 * h + 256)
        self.pre[h % 2] = dot(self.scaled[0:OUT_PIX], self.w.w_in[:, part])
        self.hg[h % 2] = dot(self.branch[0:OUT_PIX], self.w.w_out_t[:, part])

    def hidden(self):
        self.products(0)
        for h in range(4):
            if h < 3:
                self.products(h + 1)
            part = slice(256 * h, 256 * h + 256)
            for at in range(0, OUT_PIX, 16):
                rows = slice(at, at + 16)
                value, slope = gelu_and_slope(self.pre[h % 2, rows])
                self.hid[rows, part] = value.astype(BF16)
                self.pg[rows, part] = (self.hg[h % 2, rows] * slope).astype(BF16)

    def out_grad(self, gacc, big):
        w = self.w
        scale = jnp.zeros((1, C), F32)
        for h in range(4):
            part = slice(256 * h, 256 * h + 256)
            g = (gacc[:, part] + dot(self.cot_t[...], self.hid[:, part])).T
            big[part] = (g * w.layer[...]).astype(BF16)
            scale += jnp.sum(g * w.w_out[part].astype(F32), axis=0, keepdims=True)
        return scale

    def in_grad(self, iacc, big):
        for h in range(4):
            part = slice(256 * h, 256 * h + 256)
            total = iacc[:, part] + dot(self.scaled_t[...], self.pg[:, part])
            big[HID + 256 * h : HID + 256 * h + 256] = total.astype(BF16)

    def scaled_grad(self):
        self.sg[...] = dot(self.pg[0:OUT_PIX], self.w.w_in_t[...])

    def backward(self, gain_acc):
        total = gain_acc[...]
        for at in range(0, OUT_PIX, 80):
            rows = slice(at, at + 80)
            normed = self.normed[rows]
            sg = self.sg[rows]
            total += jnp.sum((sg * normed).reshape(10, 8, C), axis=0)
            self.normed[rows] = norm_backward(sg, normed, self.inv[rows], self.w.gain[...])
        return jnp.sum(total, axis=0, keepdims=True)

    def kernel_grad(self, kg):
        for chans in (slice(0, 128), slice(128, 256)):
            d = [self.normed[SIDE_AT + 8 * i : SIDE_AT + 8 * i + 8, chans] for i in range(INNER)]
            correlate(lambda b, i: self.fs[b, i, :, chans], d, kg, chans)
            for b in range(7):
                acc = [None] * 7
                for first, at in ((0, 0), (S - 3, EDGE)):
                    for j in range(0, S, 8):
                        d = [
                            self.normed[at + S * i + j : at + S * i + j + 8, chans]
                            for i in range(3)
                        ]
                        for i in range(9):
                            f = self.fb[b, first + i, j : j + 8, chans]
                            for a in range(7):
                                if 0 <= i - a < 3:
                                    term = f * d[i - a]
                                    acc[a] = term if acc[a] is None else acc[a] + term
                for a in range(7):
                    kg[7 * a + b, :, chans] += acc[a]


class Weights:
    def __init__(self, bufs):
        (self.taps, self.taps_in, self.gain, self.layer, self.w_in, self.w_in_t, self.w_out,
         self.w_out_t, self.cot) = bufs


def weight_scratch():
    return [
        pltpu.VMEM((49, C), F32),
        pltpu.VMEM((49, C), BF16),
        pltpu.VMEM((1, C), F32),
        pltpu.VMEM((1, C), F32),
        pltpu.VMEM((C, HID), BF16),
        pltpu.VMEM((HID, C), BF16),
        pltpu.VMEM((HID, C), BF16),
        pltpu.VMEM((C, HID), BF16),
        pltpu.VMEM((PIX, C), BF16),
    ]


def inside_scratch():
    return [
        pltpu.VMEM((INNER, S, C), F32),
        pltpu.VMEM((IN_PIX, 128), F32),
        pltpu.VMEM((IN_PAD, C), BF16),
        pltpu.VMEM((IN_PAD, C), BF16),
        pltpu.VMEM((IN_PIX, C), BF16),
        pltpu.VMEM((C, IN_PAD), BF16),
        pltpu.VMEM((C, IN_PAD), BF16),
        pltpu.VMEM((IN_PIX, 256), F32),
        pltpu.VMEM((IN_PIX, 256), F32),
        pltpu.VMEM((IN_PAD, 256), BF16),
        pltpu.VMEM((IN_PAD, HID), BF16),
        pltpu.VMEM((IN_PIX, C), F32),
    ]


def border_scratch():
    return [
        pltpu.VMEM((OUT_PIX, C), F32),
        pltpu.VMEM((OUT_PIX, 128), F32),
        pltpu.VMEM((OUT_PAD, C), BF16),
        pltpu.VMEM((OUT_PAD, C), BF16),
        pltpu.VMEM((OUT_PAD, C), BF16),
        pltpu.VMEM((C, OUT_PAD), BF16),
        pltpu.VMEM((C, OUT_PAD), BF16),
        pltpu.VMEM((2, OUT_PIX, 256), F32),
        pltpu.VMEM((2, OUT_PIX, 256), F32),
        pltpu.VMEM((OUT_PAD, HID), BF16),
        pltpu.VMEM((OUT_PAD, HID), BF16),
        pltpu.VMEM((OUT_PIX, C), F32),
        pltpu.VMEM((OUT_PAD, C), F32),
    ]


FAR_FIRST = (4, 3, 5, 2, 6, 1, 7)


def added(first, rest, count):
    total = first.astype(F32)
    for k in range(count):
        total += rest[k].astype(F32)
    return total


class OutSum:
    def __init__(self, net, me, peers, big, bufs):
        self.net, self.me, self.peers, self.big = net, me, peers, big
        self.r0, self.s1, self.r1, self.s2, self.r2, self.s3, self.r3, self.fin = bufs

    def start(self):
        half = pl.ds(pl.multiple_of((1 - self.me.core) * 512, 512), 512)
        self.c0 = self.net.send(self.big.at[half], self.r0, self.peers.mate)

    def over_z(self):
        self.c0.wait_recv()
        own = self.big[pl.ds(pl.multiple_of(self.me.core * 512, 512), 512)]
        self.s1[...] = added(own, [self.r0[...]], 1).astype(BF16).reshape(NZ, 64, C)
        z = self.me.z
        self.c1 = [
            self.net.send(self.s1.at[lax.rem(z + k, NZ)], self.r1.at[k - 1], self.peers.z[k - 1])
            for k in FAR_FIRST
        ]

    def over_x(self):
        for copy in self.c1:
            copy.wait_recv()
        total = added(self.s1[self.me.z], self.r1, NZ - 1)
        self.s2[...] = total.astype(BF16).reshape(NX, 16, C)
        x = self.me.x
        self.c2 = [
            self.net.send(self.s2.at[lax.rem(x + k, NX)], self.r2.at[k - 1], self.peers.x[k - 1])
            for k in (2, 1, 3)
        ]

    def over_y(self):
        for copy in self.c2:
            copy.wait_recv()
        self.s3[...] = added(self.s2[self.me.x], self.r2, NX - 1).astype(BF16)
        y = self.me.y
        self.r3[y] = self.s3[...]
        self.c3 = [self.net.send(self.s3, self.r3.at[y], self.peers.y[k - 1]) for k in FAR_FIRST]

    def back_x(self):
        for copy in self.c3:
            copy.wait_recv()
        me = self.me
        total = added(self.r3[0], [self.r3[k] for k in range(1, NY)], NY - 1)
        self.fin[me.core, me.z, me.x] = total.astype(BF16)
        mine = self.fin.at[me.core, me.z, me.x]
        self.c4 = [self.net.send(mine, mine, self.peers.x[k - 1]) for k in (2, 1, 3)]

    def back_z(self):
        for copy in self.c4:
            copy.wait_recv()
        mine = self.fin.at[self.me.core, self.me.z]
        self.c5 = [self.net.send(mine, mine, self.peers.z[k - 1]) for k in FAR_FIRST]

    def back_core(self):
        for copy in self.c5:
            copy.wait_recv()
        mine = self.fin.at[self.me.core]
        self.c6 = self.net.send(mine, mine, self.peers.mate)

    def finish(self):
        self.c6.wait_recv()
        return self.fin[...].reshape(HID, C)


class InSum:
    def __init__(self, net, me, peers, big, bufs):
        self.net, self.me, self.peers, self.big = net, me, peers, big
        self.r0, self.s1, self.r1, self.s2, self.r2, self.s3, self.r3, self.fin = bufs

    def start(self):
        half = pl.ds(pl.multiple_of(HID + (1 - self.me.core) * 512, 512), 512)
        self.c0 = self.net.send(self.big.at[half], self.r0, self.peers.mate)

    def over_x(self):
        self.c0.wait_recv()
        own = self.big[pl.ds(pl.multiple_of(HID + self.me.core * 512, 512), 512)]
        self.s1[...] = added(own, [self.r0[...]], 1).astype(BF16).reshape(NX, 128, C)
        x = self.me.x
        self.c1 = [
            self.net.send(self.s1.at[lax.rem(x + k, NX)], self.r1.at[k - 1], self.peers.x[k - 1])
            for k in (2, 1, 3)
        ]

    def over_y(self):
        for copy in self.c1:
            copy.wait_recv()
        total = added(self.s1[self.me.x], self.r1, NX - 1)
        self.s2[...] = total.astype(BF16).reshape(NY, 16, C)
        y = self.me.y
        self.c2 = [
            self.net.send(self.s2.at[lax.rem(y + k, NY)], self.r2.at[k - 1], self.peers.y[k - 1])
            for k in FAR_FIRST
        ]

    def over_z(self):
        for copy in self.c2:
            copy.wait_recv()
        self.s3[...] = added(self.s2[self.me.y], self.r2, NY - 1).astype(BF16)
        z = self.me.z
        self.r3[z] = self.s3[...]
        self.c3 = [self.net.send(self.s3, self.r3.at[z], self.peers.z[k - 1]) for k in FAR_FIRST]

    def back_y(self):
        for copy in self.c3:
            copy.wait_recv()
        me = self.me
        total = added(self.r3[0], [self.r3[k] for k in range(1, NZ)], NZ - 1)
        self.fin[me.core, me.x, me.y] = total.astype(BF16)
        mine = self.fin.at[me.core, me.x, me.y]
        self.c4 = [self.net.send(mine, mine, self.peers.y[k - 1]) for k in FAR_FIRST]

    def back_x(self):
        for copy in self.c4:
            copy.wait_recv()
        mine = self.fin.at[self.me.core, self.me.x]
        self.c5 = [self.net.send(mine, mine, self.peers.x[k - 1]) for k in (2, 1, 3)]

    def back_core(self):
        for copy in self.c5:
            copy.wait_recv()
        mine = self.fin.at[self.me.core]
        self.c6 = self.net.send(mine, mine, self.peers.mate)

    def finish(self):
        self.c6.wait_recv()
        return self.fin[...].reshape(HID, C)


class SmallSum:
    def __init__(self, net, me, peers, small, bufs):
        self.net, self.me, self.peers, self.small = net, me, peers, small
        self.r0, self.s1, self.r1, self.s2, self.r2, self.s3, self.r3, self.fin = bufs

    def start(self):
        half = pl.ds(pl.multiple_of((1 - self.me.core) * 32, 32), 32)
        self.c0 = self.net.send(self.small.at[half], self.r0, self.peers.mate)

    def over_x(self):
        self.c0.wait_recv()
        own = self.small[pl.ds(pl.multiple_of(self.me.core * 32, 32), 32)]
        self.s1[...] = (own + self.r0[...]).reshape(NX, 8, C)
        x = self.me.x
        self.c1 = [
            self.net.send(self.s1.at[lax.rem(x + k, NX)], self.r1.at[k - 1], self.peers.x[k - 1])
            for k in (2, 1, 3)
        ]

    def over_y(self):
        for copy in self.c1:
            copy.wait_recv()
        self.s2[...] = added(self.s1[self.me.x], self.r1, NX - 1)
        y = self.me.y
        self.r2[y] = self.s2[...]
        self.c2 = [self.net.send(self.s2, self.r2.at[y], self.peers.y[k - 1]) for k in FAR_FIRST]

    def over_z(self):
        for copy in self.c2:
            copy.wait_recv()
        self.s3[...] = jnp.sum(self.r2[...], axis=0)
        z = self.me.z
        self.r3[z] = self.s3[...]
        self.c3 = [self.net.send(self.s3, self.r3.at[z], self.peers.z[k - 1]) for k in FAR_FIRST]

    def back_x(self):
        for copy in self.c3:
            copy.wait_recv()
        me = self.me
        self.fin[me.core, me.x] = jnp.sum(self.r3[...], axis=0)
        mine = self.fin.at[me.core, me.x]
        self.c4 = [self.net.send(mine, mine, self.peers.x[k - 1]) for k in (2, 1, 3)]

    def back_core(self):
        for copy in self.c4:
            copy.wait_recv()
        mine = self.fin.at[self.me.core]
        self.c5 = self.net.send(mine, mine, self.peers.mate)

    def finish(self):
        self.c5.wait_recv()
        return self.fin[...].reshape(64, C)


class Peers:
    def __init__(self, me):
        self.mate = me.at(core=1 - me.core)
        self.x = [me.at(x=lax.rem(me.x + k, NX)) for k in range(1, NX)]
        self.y = [me.at(y=lax.rem(me.y + k, NY)) for k in range(1, NY)]
        self.z = [me.at(z=lax.rem(me.z + k, NZ)) for k in range(1, NZ)]

    def all(self):
        return [self.mate] + self.x + self.y + self.z


SUM_COPIES = (1 + 7 + 3 + 7 + 3 + 7 + 1) + (1 + 3 + 7 + 7 + 7 + 3 + 1) + (1 + 3 + 7 + 7 + 3 + 1)


def sum_scratch():
    return [
        pltpu.VMEM((512, C), BF16),
        pltpu.VMEM((NZ, 64, C), BF16),
        pltpu.VMEM((NZ - 1, 64, C), BF16),
        pltpu.VMEM((NX, 16, C), BF16),
        pltpu.VMEM((NX - 1, 16, C), BF16),
        pltpu.VMEM((16, C), BF16),
        pltpu.VMEM((NY, 16, C), BF16),
        pltpu.VMEM((2, NZ, NX, 16, C), BF16),
        pltpu.VMEM((512, C), BF16),
        pltpu.VMEM((NX, 128, C), BF16),
        pltpu.VMEM((NX - 1, 128, C), BF16),
        pltpu.VMEM((NY, 16, C), BF16),
        pltpu.VMEM((NY - 1, 16, C), BF16),
        pltpu.VMEM((16, C), BF16),
        pltpu.VMEM((NZ, 16, C), BF16),
        pltpu.VMEM((2, NX, NY, 16, C), BF16),
        pltpu.VMEM((32, C), F32),
        pltpu.VMEM((NX, 8, C), F32),
        pltpu.VMEM((NX - 1, 8, C), F32),
        pltpu.VMEM((8, C), F32),
        pltpu.VMEM((NY, 8, C), F32),
        pltpu.VMEM((8, C), F32),
        pltpu.VMEM((NZ, 8, C), F32),
        pltpu.VMEM((2, NX, 8, C), F32),
    ]


def sum_sums(outs, ins, smalls, kg_out, gain_out, scale_out, in_out, out_out):
    smalls.over_x()
    smalls.over_y()
    ins.over_y()
    outs.over_x()
    smalls.over_z()
    ins.over_z()
    outs.over_y()
    smalls.back_x()
    ins.back_y()
    outs.back_x()
    smalls.back_core()
    outs.back_z()
    ins.back_x()
    rows = smalls.finish()
    kg_out[...] = rows[0:49]
    gain_out[...] = rows[49:50]
    scale_out[...] = rows[50:51]
    ins.back_core()
    outs.back_core()
    rows = ins.finish()
    for q in range(HID // C):
        in_out[:, 256 * q : 256 * q + 256] = rows[256 * q : 256 * q + 256]
    out_out[...] = outs.finish()


def shared_scratch():
    return [
        pltpu.SMEM((16, 8), jnp.int32),
        pltpu.SMEM((16, 8), jnp.int32),
        pltpu.VMEM((S, S, C), BF16),
        pltpu.VMEM((S, S, C), F32),
        pltpu.VMEM((ROWS, PITCH, C), F32),
        pltpu.VMEM((7, ROWS, S, C), F32),
        pltpu.VMEM((7, S, 8, C), F32),
        pltpu.VMEM((4, 3, S, C), BF16),
        pltpu.VMEM((4, 16, C), BF16),
        pltpu.VMEM((4, 16, C), F32),
        pltpu.VMEM((C, HID), F32),
        pltpu.VMEM((C, HID), F32),
        pltpu.VMEM((49, 8, C), F32),
        pltpu.VMEM((8, C), F32),
        pltpu.VMEM((2 * HID, C), BF16),
        pltpu.VMEM((64, C), F32),
    ]


def split_refs(refs, *lists):
    refs = list(refs)
    parts = []
    for scratch in lists:
        parts.append(refs[: len(scratch)])
        refs = refs[len(scratch) :]
    return parts + [refs]


def block_kernel(
    ids_in, codes_in, x_in, cot_in, taps_in, gain_in, layer_in, w_in_in, w_out_in,
    kg_out, gain_out, scale_out, in_out, out_out, *rest,
):
    shared, weights, rims, inner, outer, sums, sems = split_refs(
        rest, shared_scratch(), weight_scratch(), rim_scratch(), inside_scratch(),
        border_scratch(), sum_scratch(),
    )
    ids, codes, xb, xf, fr, fb, fs, sides, corners, cf, gacc, iacc, kg, gain_acc, big, small = shared
    ss, rs, ls = sems
    w = Weights(weights)
    me = Place()
    peers = Peers(me)
    along_y, along_x = rim_partners(me)
    partners = peers.all() + along_y

    barrier = pltpu.get_barrier_semaphore()
    for device in partners:
        pl.semaphore_signal(barrier, inc=1, device_id=device, device_id_type=MESH)
    loads = [
        pltpu.make_async_copy(src, dst, ls.at[i])
        for i, (src, dst) in enumerate(
            (
                (x_in, xb), (ids_in, ids), (codes_in, codes), (taps_in, w.taps_in),
                (gain_in, w.gain), (layer_in, w.layer), (w_in_in, w.w_in), (w_out_in, w.w_out),
                (cot_in, w.cot),
            )
        )
    ]
    for load in loads:
        load.start()
    loads[0].wait()
    own_strips(xb, xf, rims[0], rims[6], me)
    pl.semaphore_wait(barrier, len(partners))

    net = Copies(ss, rs)
    by_y, by_x = both_rims(net, me, ids, codes, along_y, along_x, rims[:6], rims[6:])
    by_y.gather()
    by_x.gather()
    for load in loads[1:]:
        load.wait()

    inside = Inside(w, fb, inner)
    border = Border(w, fb, fs, outer)
    frame_inside(xf, fr)
    shift_rows(fr, fb, 3, S)
    w.taps[...] = w.taps_in[...].astype(F32)
    by_x.choose()
    inside.depthwise()
    w.w_out_t[...] = w.w_out[...].T
    w.w_in_t[...] = w.w_in[...].T
    inside.norm()
    by_y.choose()
    border.cotangent()
    for h in range(4):
        inside.hidden(h, gacc, iacc)
    inside.backward(gain_acc)
    kg[...] = jnp.zeros_like(kg)
    inside.kernel_grad(kg)

    by_y.take(sides, corners, slice(0, HALF), me.space)
    by_x.take(sides, corners, slice(HALF, C), me.space)
    frame_rims(sides, corners, fr, cf)
    shift_rows(fr, fb, 0, 9)
    shift_rows(fr, fb, S - 3, 9)
    shift_sides(fr, fs)
    border.depthwise()
    border.norm()
    border.hidden()
    outs = OutSum(net, me, peers, big, sums[0:8])
    ins = InSum(net, me, peers, big, sums[8:16])
    smalls = SmallSum(net, me, peers, small, sums[16:24])
    scale = border.out_grad(gacc, big)
    outs.start()
    border.in_grad(iacc, big)
    ins.start()
    border.scaled_grad()
    outs.over_z()
    ins.over_x()
    gain = border.backward(gain_acc)
    border.kernel_grad(kg)
    small[0:49] = jnp.sum(kg[...], axis=1)
    small[49:50] = gain
    small[50:51] = scale
    small[51:64] = jnp.zeros((13, C), F32)
    smalls.start()
    sum_sums(outs, ins, smalls, kg_out, gain_out, scale_out, in_out, out_out)
    net.finish()


def block_grads(neighbours, codes, tile, cot, kernel, ln_gain, layer_scale, w_in, w_out):
    vmem = pl.BlockSpec(memory_space=pltpu.VMEM)
    copies = RIM_COPIES + SUM_COPIES
    return pl.pallas_call(
        block_kernel,
        out_shape=(
            jax.ShapeDtypeStruct((49, C), F32),
            jax.ShapeDtypeStruct((1, C), F32),
            jax.ShapeDtypeStruct((1, C), F32),
            jax.ShapeDtypeStruct((C, HID), BF16),
            jax.ShapeDtypeStruct((HID, C), BF16),
        ),
        in_specs=[pl.BlockSpec(memory_space=pl.ANY)] * 9,
        out_specs=(vmem,) * 5,
        scratch_shapes=shared_scratch() + weight_scratch() + rim_scratch() + inside_scratch()
        + border_scratch() + sum_scratch()
        + [pltpu.SemaphoreType.DMA((copies,))] * 2 + [pltpu.SemaphoreType.DMA((9,))],
        compiler_params=pltpu.CompilerParams(
            collective_id=0, has_side_effects=True, vmem_limit_bytes=60 * 2**20
        ),
    )(
        neighbours, codes, tile, cot, kernel, ln_gain.reshape(1, C), layer_scale.reshape(1, C),
        w_in, w_out,
    )


def on_device(state, cotangent, kernel, ln_gain, w_in, w_out, layer_scale, neighbours, codes):
    kernel_grad, gain_grad, scale_grad, in_grad, out_grad = block_grads(
        neighbours, codes, state.reshape(S, S, C), cotangent.reshape(PIX, C), kernel, ln_gain,
        layer_scale, w_in, w_out,
    )
    return (kernel_grad, gain_grad.reshape(C), scale_grad.reshape(C), in_grad, out_grad)


def solution(mesh):
    placed = (P("dp", "space", None, None, None),) * 2 + (P(),) * 7
    return jax.shard_map(
        on_device, mesh=mesh, in_specs=placed, out_specs=(P(),) * 5, check_vma=False
    )
```

```python
import jax
import jax.numpy as jnp
from jax import lax
from jax.experimental import pallas as pl
from jax.experimental.pallas import tpu as pltpu
from jax.sharding import PartitionSpec as P

EPSILON = 1e-06
MESH = pl.DeviceIdType.MESH
F32 = jnp.float32
BF16 = jnp.bfloat16

CORES, NX, NY_LO, NY_HI, NZ = 2, 4, 4, 2, 8
NY = NY_LO * NY_HI

S = 32
C = 256
HID = 1024
PIX = S * S
PITCH = 40
ROWS = 38


class Place:
    def __init__(self):
        dp = lax.axis_index("dp")
        space = lax.axis_index("space")
        self.core = lax.rem(dp, CORES)
        self.y_hi = lax.rem(dp // CORES, NY_HI)
        self.z = dp // (CORES * NY_HI)
        self.x = lax.rem(space, NX)
        self.y_lo = space // NX
        self.y = self.y_hi * NY_LO + self.y_lo
        self.dp = dp
        self.space = space

    def at(self, core=None, x=None, y=None, z=None):
        core = self.core if core is None else core
        x = self.x if x is None else x
        y = self.y if y is None else y
        z = self.z if z is None else z
        dp = (z * NY_HI + y // NY_LO) * CORES + core
        return {"dp": dp, "space": lax.rem(y, NY_LO) * NX + x}


def greet(devices):
    barrier = pltpu.get_barrier_semaphore()
    for device in devices:
        pl.semaphore_signal(barrier, inc=1, device_id=device, device_id_type=MESH)
    pl.semaphore_wait(barrier, len(devices))


class Copies:
    def __init__(self, send_sems, recv_sems):
        self.send_sems = send_sems
        self.recv_sems = recv_sems
        self.used = 0
        self.started = []

    def send(self, src, dst, device):
        copy = pltpu.make_async_remote_copy(
            src_ref=src,
            dst_ref=dst,
            send_sem=self.send_sems.at[self.used],
            recv_sem=self.recv_sems.at[self.used],
            device_id=device,
            device_id_type=MESH,
        )
        copy.start()
        self.used += 1
        self.started.append(copy)
        return copy

    def finish(self):
        for copy in self.started:
            copy.wait_send()


HALF = C // 2


def own_strips(x_ref, xf, gath_y, gath_x, me):
    turn = reversal()
    xf[...] = x_ref[...].astype(F32)

    def put(side, r, rows):
        gath_y[me.y_lo, side, r] = rows[:, :HALF]
        gath_x[me.x, side, r] = rows[:, HALF:]

    for r in range(3):
        put(0, r, x_ref[r])
        put(2, r, flip(turn, x_ref[S - 1 - r]))
        put(1, r, xf[:, S - 1 - r, :].astype(BF16))
        put(3, r, flip(turn, xf[:, r, :].astype(BF16)))


class Rims:
    def __init__(self, net, ids, codes, gath, out_s, out_c, in_s, in_c, cf, gather_at, choose_at, gather_to, choose_to, tile_at, split):
        self.net = net
        self.ids, self.codes = ids, codes
        self.gath, self.out_s, self.out_c, self.in_s, self.in_c, self.cf = gath, out_s, out_c, in_s, in_c, cf
        self.gather_at, self.choose_at = gather_at, choose_at
        self.gather_to, self.choose_to = gather_to, choose_to
        self.tile_at, self.split = tile_at, split

    def gather(self):
        at = self.gather_at
        self.first = [
            self.net.send(self.gath.at[at], self.gath.at[at], self.gather_to[k - 1])
            for k in (2, 1, 3)
        ]

    def choose(self):
        for copy in self.first:
            copy.wait_recv()
        self.second = []
        at = self.choose_at
        for k in (2, 1, 3, 0):
            target = self.tile_at(lax.rem(at + k, 4))
            for s in range(8):
                row, _ = self.split(jnp.maximum(self.ids[s, target], 0))
                e = self.codes[s, target]
                if s < 4:
                    piece = self.gath[row, e]
                    if k:
                        self.out_s[k - 1, s] = piece
                    else:
                        self.in_s[at, s] = piece
                else:
                    piece = self.gath[row, e, :, 0:16, :].astype(F32)
                    for r in range(3):
                        self.cf[pl.ds(16 * (s - 4) + 4 * r, 4), :] = piece[r, 0:4]
            packed = self.cf[...].astype(BF16)
            if k:
                self.out_c[k - 1] = packed
                to = self.choose_to[k - 1]
                self.second.append(self.net.send(self.out_s.at[k - 1], self.in_s.at[at], to))
                self.second.append(self.net.send(self.out_c.at[k - 1], self.in_c.at[at], to))
            else:
                self.in_c[at] = packed

    def take(self, sides, corners, chans, space):
        for copy in self.second:
            copy.wait_recv()
        for s in range(8):
            n = self.ids[s, space]
            _, col = self.split(jnp.maximum(n, 0))
            if s < 4:
                sides[s, :, :, chans] = self.in_s[col, s]
            else:
                piece = self.in_c[col, pl.ds(16 * (s - 4), 16)]
                corners[s - 4, :, chans] = jnp.where(n >= 0, piece, jnp.zeros_like(piece))


def both_rims(net, me, ids, codes, along_y, along_x, bufs_y, bufs_x):
    by_y = Rims(
        net, ids, codes, *bufs_y, me.y_lo, me.x, along_y, along_x,
        lambda x: me.y_lo * NX + x, lambda n: (n // NX, lax.rem(n, NX)),
    )
    by_x = Rims(
        net, ids, codes, *bufs_x, me.x, me.y_lo, along_x, along_y,
        lambda y: y * NX + me.x, lambda n: (lax.rem(n, NX), n // NX),
    )
    return by_y, by_x


def rim_partners(me):
    base = me.y_hi * NY_LO
    along_y = [me.at(y=base + lax.rem(me.y_lo + k, NY_LO)) for k in range(1, NY_LO)]
    along_x = [me.at(x=lax.rem(me.x + k, NX)) for k in range(1, NX)]
    return along_y, along_x


RIM_COPIES = 2 * 9


def rim_scratch():
    half = [
        pltpu.VMEM((4, 4, 3, S, HALF), BF16),
        pltpu.VMEM((3, 4, 3, S, HALF), BF16),
        pltpu.VMEM((3, 64, HALF), BF16),
        pltpu.VMEM((4, 4, 3, S, HALF), BF16),
        pltpu.VMEM((4, 64, HALF), BF16),
        pltpu.VMEM((64, HALF), F32),
    ]
    return half * 2


def reversal():
    row = lax.broadcasted_iota(jnp.int32, (S, S), 0)
    col = lax.broadcasted_iota(jnp.int32, (S, S), 1)
    return jnp.where(row + col == S - 1, 1.0, 0.0).astype(BF16)


def flip(turn, rows):
    return jnp.dot(turn, rows, preferred_element_type=F32).astype(rows.dtype)


INNER = S - 6
IN_PIX = INNER * S
IN_PAD = 896
EDGE = 3 * S
SIDE_AT = 2 * EDGE
OUT_PIX = SIDE_AT + INNER * 8
OUT_PAD = 512


def frame_inside(xf, fr):
    fr[...] = jnp.zeros_like(fr)

    def one_row(i, carry):
        fr[3 + i, 3 : 3 + S, :] = xf[i]
        return carry

    lax.fori_loop(0, S, one_row, 0)


def frame_rims(sides, corners, fr, cf):
    turn = reversal()
    for r in range(3):
        fr[r, 3 : 3 + S, :] = flip(turn, sides[0, 2 - r]).astype(F32)
        fr[3 : 3 + S, 35 + r, :] = flip(turn, sides[1, r]).astype(F32)
        fr[35 + r, 3 : 3 + S, :] = sides[2, r].astype(F32)
        fr[3 : 3 + S, r, :] = sides[3, 2 - r].astype(F32)
    cf[...] = corners[...].astype(F32)
    for i in range(3):
        for j in range(3):
            fr[i, j, :] = cf[0, 4 * (2 - i) + 2 - j, :]
            fr[i, 35 + j, :] = cf[1, 4 * j + 2 - i, :]
            fr[35 + i, 35 + j, :] = cf[2, 4 * i + j, :]
            fr[35 + i, j, :] = cf[3, 4 * (2 - j) + i, :]


def shift_rows(fr, fb, first, count):
    def one_row(i, carry):
        for b in range(7):
            fb[b, first + i] = fr[first + i, b : b + S, :]
        return carry

    lax.fori_loop(0, count, one_row, 0)


def shift_sides(fr, fs):
    fs[...] = jnp.zeros_like(fs)

    def one_row(i, carry):
        for b in range(7):
            fs[b, i, 0:3, :] = fr[3 + i, b : b + 3, :]
            fs[b, i, 3:6, :] = fr[3 + i, 29 + b : 32 + b, :]
        return carry

    lax.fori_loop(0, S, one_row, 0)


def lanes(g):
    return (
        pl.ds(pl.multiple_of((g // 2) * 8, 8), 8),
        pl.ds(pl.multiple_of(lax.rem(g, 2) * 128, 128), 128),
    )


def convolve(load, taps, chans, count, put):
    acc = [None] * count
    for b in range(7):
        k = [jnp.broadcast_to(taps[pl.ds(7 * a + b, 1), chans], (8, 128)) for a in range(7)]
        for i in range(count + 6):
            f = load(b, i)
            for a in range(7):
                at = i - a
                if 0 <= at < count:
                    term = f * k[a]
                    acc[at] = term if acc[at] is None else acc[at] + term
    for i in range(count):
        put(i, acc[i])


def correlate(load, d, kg, chans):
    count = len(d)
    for b in range(7):
        acc = [None] * 7
        for i in range(count + 6):
            f = load(b, i)
            for a in range(7):
                at = i - a
                if 0 <= at < count:
                    term = f * d[at]
                    acc[a] = term if acc[a] is None else acc[a] + term
        for a in range(7):
            kg[7 * a + b, :, chans] += acc[a]


def normalise(v):
    mean = jnp.mean(v, axis=-1, keepdims=True)
    v = v - mean
    inverse = lax.rsqrt(jnp.mean(v * v, axis=-1, keepdims=True) + EPSILON)
    return v * inverse, inverse


def norm_backward(sg, normed, inverse, gain):
    g = sg * gain
    mean = jnp.mean(g, axis=-1, keepdims=True)
    along = jnp.mean(g * normed, axis=-1, keepdims=True)
    return (g - mean - normed * along) * jnp.concatenate([inverse, inverse], axis=1)


def gelu_and_slope(v):
    root = 0.7978845608028654
    square = v * v
    inner = v * (root + (root * 0.044715) * square)
    t = jnp.tanh(inner)
    half = 0.5 * (1.0 + t)
    slope = half + (0.5 * v) * (1.0 - t * t) * (root + (3.0 * root * 0.044715) * square)
    return v * half, slope


def dot(left, right):
    return jnp.dot(left, right, preferred_element_type=F32)


class Inside:
    def __init__(self, w, fb, bufs):
        self.w, self.fb = w, fb
        (self.normed, self.inv, self.scaled, self.cot, self.branch, self.scaled_t, self.cot_t,
         self.pre, self.hg, self.hid, self.pg, self.sg) = bufs

    def depthwise(self):
        def step(g, carry):
            cols, chans = lanes(g)

            def put(i, value):
                self.normed[i, cols, chans] = value

            convolve(lambda b, i: self.fb[b, 3 + i, cols, chans], self.w.taps, chans, INNER, put)
            return carry

        lax.fori_loop(0, 8, step, 0)

    def norm(self):
        w = self.w
        col = lax.rem(lax.broadcasted_iota(jnp.int32, (64, C), 0), S)
        here = (col >= 3) & (col < S - 3)

        def step(q, carry):
            rows = pl.ds(q * 2, 2)
            flat = pl.ds(pl.multiple_of(q * 64, 64), 64)
            normed, inverse = normalise(self.normed[rows].reshape(64, C))
            self.inv[flat] = jnp.broadcast_to(inverse, (64, 128))
            self.normed[rows] = normed.reshape(2, S, C)
            self.scaled[flat] = (normed * w.gain[...]).astype(BF16)
            cot = w.cot[pl.ds(pl.multiple_of(3 * S + q * 64, 32), 64)].astype(F32)
            cot = jnp.where(here, cot, jnp.zeros_like(cot))
            self.cot[flat] = cot.astype(BF16)
            self.branch[flat] = (cot * w.layer[...]).astype(BF16)
            return carry

        lax.fori_loop(0, INNER // 2, step, 0)
        rest = slice(IN_PIX, IN_PAD)
        none = jnp.zeros((IN_PAD - IN_PIX, C), BF16)
        self.scaled[rest] = none
        self.cot[rest] = none
        self.hid[rest] = none
        for h in range(4):
            self.pg[rest, 256 * h : 256 * h + 256] = none
        self.scaled_t[...] = self.scaled[...].T
        self.cot_t[...] = self.cot[...].T

    def hidden(self, h, gacc, iacc):
        w = self.w
        part = slice(256 * h, 256 * h + 256)
        self.pre[...] = dot(self.scaled[0:IN_PIX], w.w_in[:, part])
        self.hg[...] = dot(self.branch[...], w.w_out_t[:, part])

        def act(q, carry):
            rows = pl.ds(pl.multiple_of(q * 32, 32), 32)
            value, slope = gelu_and_slope(self.pre[rows])
            self.hid[rows] = value.astype(BF16)
            self.pg[rows, part] = (self.hg[rows] * slope).astype(BF16)
            return carry

        lax.fori_loop(0, IN_PIX // 32, act, 0)
        gacc[:, part] = dot(self.cot_t[...], self.hid[...])
        iacc[:, part] = dot(self.scaled_t[...], self.pg[:, part])

    def backward(self, gain_acc):
        w = self.w
        self.sg[...] = dot(self.pg[0:IN_PIX], w.w_in_t[...])

        def step(q, total):
            rows = pl.ds(q * 2, 2)
            flat = pl.ds(pl.multiple_of(q * 64, 64), 64)
            normed = self.normed[rows].reshape(64, C)
            sg = self.sg[flat]
            grad = norm_backward(sg, normed, self.inv[flat], w.gain[...])
            self.normed[rows] = grad.reshape(2, S, C)
            return total + jnp.sum((sg * normed).reshape(8, 8, C), axis=0)

        gain_acc[...] = lax.fori_loop(0, INNER // 2, step, jnp.zeros((8, C), F32))

    def kernel_grad(self, kg):
        def step(g, carry):
            cols, chans = lanes(g)
            d = [self.normed[i, cols, chans] for i in range(INNER)]
            correlate(lambda b, i: self.fb[b, 3 + i, cols, chans], d, kg, chans)
            return carry

        lax.fori_loop(0, 8, step, 0)


class Border:
    def __init__(self, w, fb, fs, bufs):
        self.w, self.fb, self.fs = w, fb, fs
        (self.normed, self.inv, self.scaled, self.cot, self.branch, self.scaled_t, self.cot_t,
         self.pre, self.hg, self.hid, self.pg, self.sg, self.cf) = bufs

    def cotangent(self):
        w = self.w
        self.cf[...] = jnp.zeros_like(self.cf)
        self.cf[0:EDGE] = w.cot[0:EDGE].astype(F32)
        self.cf[EDGE : 2 * EDGE] = w.cot[PIX - EDGE : PIX].astype(F32)
        for i in range(INNER):
            row = w.cot[(3 + i) * S : (4 + i) * S].astype(F32)
            at = SIDE_AT + 8 * i
            self.cf[at : at + 3] = row[0:3]
            self.cf[at + 3 : at + 6] = row[29:32]
        self.cot[...] = self.cf[...].astype(BF16)
        self.branch[...] = (self.cf[...] * w.layer[...]).astype(BF16)
        self.cot_t[...] = self.cot[...].T
        rest = slice(OUT_PIX, OUT_PAD)
        none = jnp.zeros((OUT_PAD - OUT_PIX, C), BF16)
        self.scaled[rest] = none
        for h in range(4):
            self.hid[rest, 256 * h : 256 * h + 256] = none
            self.pg[rest, 256 * h : 256 * h + 256] = none

    def depthwise(self):
        for chans in (slice(0, 128), slice(128, 256)):

            def put_side(i, value):
                self.normed[SIDE_AT + 8 * i : SIDE_AT + 8 * i + 8, chans] = value

            convolve(lambda b, i: self.fs[b, i, :, chans], self.w.taps, chans, INNER, put_side)
            for first, at in ((0, 0), (S - 3, EDGE)):
                for j in range(0, S, 8):

                    def put(i, value):
                        self.normed[at + S * i + j : at + S * i + j + 8, chans] = value

                    convolve(
                        lambda b, i: self.fb[b, first + i, j : j + 8, chans],
                        self.w.taps, chans, 3, put,
                    )

    def norm(self):
        w = self.w
        for at in range(0, OUT_PIX, 80):
            rows = slice(at, at + 80)
            normed, inverse = normalise(self.normed[rows])
            self.inv[rows] = jnp.broadcast_to(inverse, (80, 128))
            self.normed[rows] = normed
            self.scaled[rows] = (normed * w.gain[...]).astype(BF16)
        self.scaled_t[...] = self.scaled[...].T

    def products(self, h):
        part = slice(256 * h, 256 * h + 256)
        self.pre[h % 2] = dot(self.scaled[0:OUT_PIX], self.w.w_in[:, part])
        self.hg[h % 2] = dot(self.branch[0:OUT_PIX], self.w.w_out_t[:, part])

    def hidden(self):
        self.products(0)
        for h in range(4):
            if h < 3:
                self.products(h + 1)
            part = slice(256 * h, 256 * h + 256)
            for at in range(0, OUT_PIX, 16):
                rows = slice(at, at + 16)
                value, slope = gelu_and_slope(self.pre[h % 2, rows])
                self.hid[rows, part] = value.astype(BF16)
                self.pg[rows, part] = (self.hg[h % 2, rows] * slope).astype(BF16)

    def out_grad(self, gacc, big):
        w = self.w
        scale = jnp.zeros((1, C), F32)
        for h in range(4):
            part = slice(256 * h, 256 * h + 256)
            g = (gacc[:, part] + dot(self.cot_t[...], self.hid[:, part])).T
            big[part] = (g * w.layer[...]).astype(BF16)
            scale += jnp.sum(g * w.w_out[part].astype(F32), axis=0, keepdims=True)
        return scale

    def in_grad(self, iacc, big):
        for h in range(4):
            part = slice(256 * h, 256 * h + 256)
            total = iacc[:, part] + dot(self.scaled_t[...], self.pg[:, part])
            big[HID + 256 * h : HID + 256 * h + 256] = total.astype(BF16)

    def scaled_grad(self):
        self.sg[...] = dot(self.pg[0:OUT_PIX], self.w.w_in_t[...])

    def backward(self, gain_acc):
        total = gain_acc[...]
        for at in range(0, OUT_PIX, 80):
            rows = slice(at, at + 80)
            normed = self.normed[rows]
            sg = self.sg[rows]
            total += jnp.sum((sg * normed).reshape(10, 8, C), axis=0)
            self.normed[rows] = norm_backward(sg, normed, self.inv[rows], self.w.gain[...])
        return jnp.sum(total, axis=0, keepdims=True)

    def kernel_grad(self, kg):
        for chans in (slice(0, 128), slice(128, 256)):
            d = [self.normed[SIDE_AT + 8 * i : SIDE_AT + 8 * i + 8, chans] for i in range(INNER)]
            correlate(lambda b, i: self.fs[b, i, :, chans], d, kg, chans)
            for b in range(7):
                acc = [None] * 7
                for first, at in ((0, 0), (S - 3, EDGE)):
                    for j in range(0, S, 8):
                        d = [
                            self.normed[at + S * i + j : at + S * i + j + 8, chans]
                            for i in range(3)
                        ]
                        for i in range(9):
                            f = self.fb[b, first + i, j : j + 8, chans]
                            for a in range(7):
                                if 0 <= i - a < 3:
                                    term = f * d[i - a]
                                    acc[a] = term if acc[a] is None else acc[a] + term
                for a in range(7):
                    kg[7 * a + b, :, chans] += acc[a]


class Weights:
    def __init__(self, bufs):
        (self.taps, self.taps_in, self.gain, self.layer, self.w_in, self.w_in_t, self.w_out,
         self.w_out_t, self.cot) = bufs


def weight_scratch():
    return [
        pltpu.VMEM((49, C), F32),
        pltpu.VMEM((49, C), BF16),
        pltpu.VMEM((1, C), F32),
        pltpu.VMEM((1, C), F32),
        pltpu.VMEM((C, HID), BF16),
        pltpu.VMEM((HID, C), BF16),
        pltpu.VMEM((HID, C), BF16),
        pltpu.VMEM((C, HID), BF16),
        pltpu.VMEM((PIX, C), BF16),
    ]


def inside_scratch():
    return [
        pltpu.VMEM((INNER, S, C), F32),
        pltpu.VMEM((IN_PIX, 128), F32),
        pltpu.VMEM((IN_PAD, C), BF16),
        pltpu.VMEM((IN_PAD, C), BF16),
        pltpu.VMEM((IN_PIX, C), BF16),
        pltpu.VMEM((C, IN_PAD), BF16),
        pltpu.VMEM((C, IN_PAD), BF16),
        pltpu.VMEM((IN_PIX, 256), F32),
        pltpu.VMEM((IN_PIX, 256), F32),
        pltpu.VMEM((IN_PAD, 256), BF16),
        pltpu.VMEM((IN_PAD, HID), BF16),
        pltpu.VMEM((IN_PIX, C), F32),
    ]


def border_scratch():
    return [
        pltpu.VMEM((OUT_PIX, C), F32),
        pltpu.VMEM((OUT_PIX, 128), F32),
        pltpu.VMEM((OUT_PAD, C), BF16),
        pltpu.VMEM((OUT_PAD, C), BF16),
        pltpu.VMEM((OUT_PAD, C), BF16),
        pltpu.VMEM((C, OUT_PAD), BF16),
        pltpu.VMEM((C, OUT_PAD), BF16),
        pltpu.VMEM((2, OUT_PIX, 256), F32),
        pltpu.VMEM((2, OUT_PIX, 256), F32),
        pltpu.VMEM((OUT_PAD, HID), BF16),
        pltpu.VMEM((OUT_PAD, HID), BF16),
        pltpu.VMEM((OUT_PIX, C), F32),
        pltpu.VMEM((OUT_PAD, C), F32),
    ]


FAR_FIRST = (4, 3, 5, 2, 6, 1, 7)


def added(first, rest, count):
    total = first.astype(F32)
    for k in range(count):
        total += rest[k].astype(F32)
    return total


class OutSum:
    def __init__(self, net, me, peers, big, bufs):
        self.net, self.me, self.peers, self.big = net, me, peers, big
        self.r0, self.s1, self.r1, self.s2, self.r2, self.s3, self.r3, self.fin = bufs

    def start(self):
        half = pl.ds(pl.multiple_of((1 - self.me.core) * 512, 512), 512)
        self.c0 = self.net.send(self.big.at[half], self.r0, self.peers.mate)

    def over_z(self):
        self.c0.wait_recv()
        own = self.big[pl.ds(pl.multiple_of(self.me.core * 512, 512), 512)]
        self.s1[...] = added(own, [self.r0[...]], 1).astype(BF16).reshape(NZ, 64, C)
        z = self.me.z
        self.c1 = [
            self.net.send(self.s1.at[lax.rem(z + k, NZ)], self.r1.at[k - 1], self.peers.z[k - 1])
            for k in FAR_FIRST
        ]

    def over_x(self):
        for copy in self.c1:
            copy.wait_recv()
        total = added(self.s1[self.me.z], self.r1, NZ - 1)
        self.s2[...] = total.astype(BF16).reshape(NX, 16, C)
        x = self.me.x
        self.c2 = [
            self.net.send(self.s2.at[lax.rem(x + k, NX)], self.r2.at[k - 1], self.peers.x[k - 1])
            for k in (2, 1, 3)
        ]

    def over_y(self):
        for copy in self.c2:
            copy.wait_recv()
        self.s3[...] = added(self.s2[self.me.x], self.r2, NX - 1).astype(BF16)
        y = self.me.y
        self.r3[y] = self.s3[...]
        self.c3 = [self.net.send(self.s3, self.r3.at[y], self.peers.y[k - 1]) for k in FAR_FIRST]

    def back_x(self):
        for copy in self.c3:
            copy.wait_recv()
        me = self.me
        total = added(self.r3[0], [self.r3[k] for k in range(1, NY)], NY - 1)
        self.fin[me.core, me.z, me.x] = total.astype(BF16)
        mine = self.fin.at[me.core, me.z, me.x]
        self.c4 = [self.net.send(mine, mine, self.peers.x[k - 1]) for k in (2, 1, 3)]

    def back_z(self):
        for copy in self.c4:
            copy.wait_recv()
        mine = self.fin.at[self.me.core, self.me.z]
        self.c5 = [self.net.send(mine, mine, self.peers.z[k - 1]) for k in FAR_FIRST]

    def back_core(self):
        for copy in self.c5:
            copy.wait_recv()
        mine = self.fin.at[self.me.core]
        self.c6 = self.net.send(mine, mine, self.peers.mate)

    def finish(self):
        self.c6.wait_recv()


class InSum:
    def __init__(self, net, me, peers, big, bufs):
        self.net, self.me, self.peers, self.big = net, me, peers, big
        self.r0, self.s1, self.r1, self.s2, self.r2, self.s3, self.r3, self.fin = bufs

    def start(self):
        half = pl.ds(pl.multiple_of(HID + (1 - self.me.core) * 512, 512), 512)
        self.c0 = self.net.send(self.big.at[half], self.r0, self.peers.mate)

    def over_x(self):
        self.c0.wait_recv()
        own = self.big[pl.ds(pl.multiple_of(HID + self.me.core * 512, 512), 512)]
        self.s1[...] = added(own, [self.r0[...]], 1).astype(BF16).reshape(NX, 128, C)
        x = self.me.x
        self.c1 = [
            self.net.send(self.s1.at[lax.rem(x + k, NX)], self.r1.at[k - 1], self.peers.x[k - 1])
            for k in (2, 1, 3)
        ]

    def over_y(self):
        for copy in self.c1:
            copy.wait_recv()
        total = added(self.s1[self.me.x], self.r1, NX - 1)
        self.s2[...] = total.astype(BF16).reshape(NY, 16, C)
        y = self.me.y
        self.c2 = [
            self.net.send(self.s2.at[lax.rem(y + k, NY)], self.r2.at[k - 1], self.peers.y[k - 1])
            for k in FAR_FIRST
        ]

    def over_z(self):
        for copy in self.c2:
            copy.wait_recv()
        self.s3[...] = added(self.s2[self.me.y], self.r2, NY - 1).astype(BF16)
        z = self.me.z
        self.r3[z] = self.s3[...]
        self.c3 = [self.net.send(self.s3, self.r3.at[z], self.peers.z[k - 1]) for k in FAR_FIRST]

    def back_y(self):
        for copy in self.c3:
            copy.wait_recv()
        me = self.me
        total = added(self.r3[0], [self.r3[k] for k in range(1, NZ)], NZ - 1)
        self.fin[me.core, me.x, me.y] = total.astype(BF16)
        mine = self.fin.at[me.core, me.x, me.y]
        self.c4 = [self.net.send(mine, mine, self.peers.y[k - 1]) for k in FAR_FIRST]

    def back_x(self):
        for copy in self.c4:
            copy.wait_recv()
        mine = self.fin.at[self.me.core, self.me.x]
        self.c5 = [self.net.send(mine, mine, self.peers.x[k - 1]) for k in (2, 1, 3)]

    def back_core(self):
        for copy in self.c5:
            copy.wait_recv()
        mine = self.fin.at[self.me.core]
        self.c6 = self.net.send(mine, mine, self.peers.mate)

    def finish(self):
        self.c6.wait_recv()


class SmallSum:
    def __init__(self, net, me, peers, small, bufs):
        self.net, self.me, self.peers, self.small = net, me, peers, small
        self.r0, self.s1, self.r1, self.s2, self.r2, self.s3, self.r3, self.fin = bufs

    def start(self):
        half = pl.ds(pl.multiple_of((1 - self.me.core) * 32, 32), 32)
        self.c0 = self.net.send(self.small.at[half], self.r0, self.peers.mate)

    def over_x(self):
        self.c0.wait_recv()
        own = self.small[pl.ds(pl.multiple_of(self.me.core * 32, 32), 32)]
        self.s1[...] = (own + self.r0[...]).reshape(NX, 8, C)
        x = self.me.x
        self.c1 = [
            self.net.send(self.s1.at[lax.rem(x + k, NX)], self.r1.at[k - 1], self.peers.x[k - 1])
            for k in (2, 1, 3)
        ]

    def over_y(self):
        for copy in self.c1:
            copy.wait_recv()
        self.s2[...] = added(self.s1[self.me.x], self.r1, NX - 1)
        y = self.me.y
        self.r2[y] = self.s2[...]
        self.c2 = [self.net.send(self.s2, self.r2.at[y], self.peers.y[k - 1]) for k in FAR_FIRST]

    def over_z(self):
        for copy in self.c2:
            copy.wait_recv()
        self.s3[...] = jnp.sum(self.r2[...], axis=0)
        z = self.me.z
        self.r3[z] = self.s3[...]
        self.c3 = [self.net.send(self.s3, self.r3.at[z], self.peers.z[k - 1]) for k in FAR_FIRST]

    def back_x(self):
        for copy in self.c3:
            copy.wait_recv()
        me = self.me
        self.fin[me.core, me.x] = jnp.sum(self.r3[...], axis=0)
        mine = self.fin.at[me.core, me.x]
        self.c4 = [self.net.send(mine, mine, self.peers.x[k - 1]) for k in (2, 1, 3)]

    def back_core(self):
        for copy in self.c4:
            copy.wait_recv()
        mine = self.fin.at[self.me.core]
        self.c5 = self.net.send(mine, mine, self.peers.mate)

    def finish(self):
        self.c5.wait_recv()


class Peers:
    def __init__(self, me):
        self.mate = me.at(core=1 - me.core)
        self.x = [me.at(x=lax.rem(me.x + k, NX)) for k in range(1, NX)]
        self.y = [me.at(y=lax.rem(me.y + k, NY)) for k in range(1, NY)]
        self.z = [me.at(z=lax.rem(me.z + k, NZ)) for k in range(1, NZ)]

    def all(self):
        return [self.mate] + self.x + self.y + self.z


SUM_COPIES = (1 + 7 + 3 + 7 + 3 + 7 + 1) + (1 + 3 + 7 + 7 + 7 + 3 + 1) + (1 + 3 + 7 + 7 + 3 + 1)


def sum_scratch():
    return [
        pltpu.VMEM((512, C), BF16),
        pltpu.VMEM((NZ, 64, C), BF16),
        pltpu.VMEM((NZ - 1, 64, C), BF16),
        pltpu.VMEM((NX, 16, C), BF16),
        pltpu.VMEM((NX - 1, 16, C), BF16),
        pltpu.VMEM((16, C), BF16),
        pltpu.VMEM((NY, 16, C), BF16),
        pltpu.VMEM((512, C), BF16),
        pltpu.VMEM((NX, 128, C), BF16),
        pltpu.VMEM((NX - 1, 128, C), BF16),
        pltpu.VMEM((NY, 16, C), BF16),
        pltpu.VMEM((NY - 1, 16, C), BF16),
        pltpu.VMEM((16, C), BF16),
        pltpu.VMEM((NZ, 16, C), BF16),
        pltpu.VMEM((32, C), F32),
        pltpu.VMEM((NX, 8, C), F32),
        pltpu.VMEM((NX - 1, 8, C), F32),
        pltpu.VMEM((8, C), F32),
        pltpu.VMEM((NY, 8, C), F32),
        pltpu.VMEM((8, C), F32),
        pltpu.VMEM((NZ, 8, C), F32),
    ]


def sum_sums(outs, ins, smalls):
    smalls.over_x()
    smalls.over_y()
    ins.over_y()
    outs.over_x()
    smalls.over_z()
    ins.over_z()
    outs.over_y()
    smalls.back_x()
    ins.back_y()
    outs.back_x()
    smalls.back_core()
    outs.back_z()
    ins.back_x()
    smalls.finish()
    ins.back_core()
    outs.back_core()
    ins.finish()
    outs.finish()


def shared_scratch():
    return [
        pltpu.SMEM((8, 16), jnp.int32),
        pltpu.SMEM((8, 16), jnp.int32),
        pltpu.VMEM((S, S, C), BF16),
        pltpu.VMEM((S, S, C), F32),
        pltpu.VMEM((ROWS, PITCH, C), F32),
        pltpu.VMEM((7, ROWS, S, C), F32),
        pltpu.VMEM((7, S, 8, C), F32),
        pltpu.VMEM((4, 3, S, C), BF16),
        pltpu.VMEM((4, 16, C), BF16),
        pltpu.VMEM((4, 16, C), F32),
        pltpu.VMEM((C, HID), F32),
        pltpu.VMEM((C, HID), F32),
        pltpu.VMEM((49, 8, C), F32),
        pltpu.VMEM((8, C), F32),
        pltpu.VMEM((2 * HID, C), BF16),
        pltpu.VMEM((64, C), F32),
    ]


def split_refs(refs, *lists):
    refs = list(refs)
    parts = []
    for scratch in lists:
        parts.append(refs[: len(scratch)])
        refs = refs[len(scratch) :]
    return parts + [refs]


def block_kernel(
    ids_in, codes_in, x_in, cot_in, taps_in, gain_in, layer_in, w_in_in, w_out_in,
    out_fin, in_fin, small_fin, *rest,
):
    shared, weights, rims, inner, outer, sums, sems = split_refs(
        rest, shared_scratch(), weight_scratch(), rim_scratch(), inside_scratch(),
        border_scratch(), sum_scratch(),
    )
    ids, codes, xb, xf, fr, fb, fs, sides, corners, cf, gacc, iacc, kg, gain_acc, big, small = shared
    ss, rs, ls = sems
    w = Weights(weights)
    me = Place()
    peers = Peers(me)
    along_y, along_x = rim_partners(me)
    partners = peers.all() + along_y

    barrier = pltpu.get_barrier_semaphore()
    for device in partners:
        pl.semaphore_signal(barrier, inc=1, device_id=device, device_id_type=MESH)
    loads = [
        pltpu.make_async_copy(src, dst, ls.at[i])
        for i, (src, dst) in enumerate(
            (
                (x_in, xb), (ids_in, ids), (codes_in, codes), (taps_in, w.taps_in),
                (gain_in, w.gain), (layer_in, w.layer), (w_in_in, w.w_in), (w_out_in, w.w_out),
                (cot_in, w.cot),
            )
        )
    ]
    for load in loads:
        load.start()
    loads[0].wait()
    own_strips(xb, xf, rims[0], rims[6], me)
    pl.semaphore_wait(barrier, len(partners))

    net = Copies(ss, rs)
    by_y, by_x = both_rims(net, me, ids, codes, along_y, along_x, rims[:6], rims[6:])
    by_y.gather()
    by_x.gather()
    for load in loads[1:]:
        load.wait()

    inside = Inside(w, fb, inner)
    border = Border(w, fb, fs, outer)
    frame_inside(xf, fr)
    shift_rows(fr, fb, 3, S)
    w.taps[...] = w.taps_in[...].astype(F32)
    inside.depthwise()
    w.w_out_t[...] = w.w_out[...].T
    w.w_in_t[...] = w.w_in[...].T
    by_x.choose()
    inside.norm()
    border.cotangent()
    inside.hidden(0, gacc, iacc)
    by_y.choose()
    for h in range(1, 4):
        inside.hidden(h, gacc, iacc)
    inside.backward(gain_acc)
    kg[...] = jnp.zeros_like(kg)
    inside.kernel_grad(kg)

    by_y.take(sides, corners, slice(0, HALF), me.space)
    by_x.take(sides, corners, slice(HALF, C), me.space)
    frame_rims(sides, corners, fr, cf)
    shift_rows(fr, fb, 0, 9)
    shift_rows(fr, fb, S - 3, 9)
    shift_sides(fr, fs)
    border.depthwise()
    border.norm()
    border.hidden()
    outs = OutSum(net, me, peers, big, sums[0:7] + [out_fin])
    ins = InSum(net, me, peers, big, sums[7:14] + [in_fin])
    smalls = SmallSum(net, me, peers, small, sums[14:21] + [small_fin])
    scale = border.out_grad(gacc, big)
    outs.start()
    border.in_grad(iacc, big)
    ins.start()
    border.scaled_grad()
    outs.over_z()
    ins.over_x()
    gain = border.backward(gain_acc)
    border.kernel_grad(kg)
    small[0:49] = jnp.sum(kg[...], axis=1)
    small[49:50] = gain
    small[50:51] = scale
    small[51:64] = jnp.zeros((13, C), F32)
    smalls.start()
    sum_sums(outs, ins, smalls)
    net.finish()


def block_grads(neighbours, codes, tile, cot, kernel, ln_gain, layer_scale, w_in, w_out):
    vmem = pl.BlockSpec(memory_space=pltpu.VMEM)
    copies = RIM_COPIES + SUM_COPIES
    return pl.pallas_call(
        block_kernel,
        out_shape=(
            pltpu.VMEM((2, NZ, NX, 16, C), BF16),
            pltpu.VMEM((2, NX, NY, 16, C), BF16),
            pltpu.VMEM((2, NX, 8, C), F32),
        ),
        in_specs=[pl.BlockSpec(memory_space=pl.ANY)] * 9,
        out_specs=(vmem,) * 3,
        scratch_shapes=shared_scratch() + weight_scratch() + rim_scratch() + inside_scratch()
        + border_scratch() + sum_scratch()
        + [pltpu.SemaphoreType.DMA((copies,))] * 2 + [pltpu.SemaphoreType.DMA((9,))],
        compiler_params=pltpu.CompilerParams(
            collective_id=0, has_side_effects=True, vmem_limit_bytes=60 * 2**20
        ),
    )(
        neighbours, codes, tile, cot, kernel, ln_gain.reshape(1, C), layer_scale.reshape(1, C),
        w_in, w_out,
    )


def hand_over_kernel(
    out_fin, in_fin, small, kg_out, gain_out, scale_out, in_out, out_out, kg, gain, scale, sems
):
    def move(pairs, first):
        copies = [
            pltpu.make_async_copy(src, dst, sems.at[first + i])
            for i, (src, dst) in enumerate(pairs)
        ]
        for copy in copies:
            copy.start()
        return copies

    parts = [
        (in_fin.at[pl.ds(256 * q, 256)], in_out.at[:, pl.ds(256 * q, 256)])
        for q in range(HID // C)
    ]
    copies = move([(out_fin, out_out)] + parts, 0)
    kg[...] = small[0:49]
    gain[...] = small[49:50]
    scale[...] = small[50:51]
    copies += move([(kg, kg_out), (gain, gain_out), (scale, scale_out)], 5)
    for copy in copies:
        copy.wait()


def hand_over(out_fin, in_fin, small_fin):
    return pl.pallas_call(
        hand_over_kernel,
        out_shape=(
            jax.ShapeDtypeStruct((49, C), F32),
            jax.ShapeDtypeStruct((1, C), F32),
            jax.ShapeDtypeStruct((1, C), F32),
            jax.ShapeDtypeStruct((C, HID), BF16),
            jax.ShapeDtypeStruct((HID, C), BF16),
        ),
        in_specs=[pl.BlockSpec(memory_space=pltpu.VMEM)] * 3,
        out_specs=(pl.BlockSpec(memory_space=pl.ANY),) * 5,
        scratch_shapes=[
            pltpu.VMEM((49, C), F32),
            pltpu.VMEM((1, C), F32),
            pltpu.VMEM((1, C), F32),
            pltpu.SemaphoreType.DMA((8,)),
        ],
        compiler_params=pltpu.CompilerParams(has_side_effects=True),
    )(
        pltpu.with_memory_space_constraint(out_fin.reshape(HID, C), pltpu.VMEM),
        pltpu.with_memory_space_constraint(in_fin.reshape(HID, C), pltpu.VMEM),
        pltpu.with_memory_space_constraint(small_fin.reshape(64, C), pltpu.VMEM),
    )


def on_device(state, cotangent, kernel, ln_gain, w_in, w_out, layer_scale, neighbours, codes):
    sums = block_grads(
        neighbours.T, codes.T, state.reshape(S, S, C), cotangent.reshape(PIX, C), kernel, ln_gain,
        layer_scale, w_in, w_out,
    )
    kernel_grad, gain_grad, scale_grad, in_grad, out_grad = hand_over(*sums)
    return (kernel_grad, gain_grad.reshape(C), scale_grad.reshape(C), in_grad, out_grad)


def solution(mesh):
    placed = (P("dp", "space", None, None, None),) * 2 + (P(),) * 7
    return jax.shard_map(
        on_device, mesh=mesh, in_specs=placed, out_specs=(P(),) * 5, check_vma=False
    )
```

```python
import jax
import jax.numpy as jnp
from jax import lax
from jax.experimental import pallas as pl
from jax.experimental.pallas import tpu as pltpu
from jax.sharding import PartitionSpec as P

EPSILON = 1e-06
MESH = pl.DeviceIdType.MESH
F32 = jnp.float32
BF16 = jnp.bfloat16

CORES, NX, NY_LO, NY_HI, NZ = 2, 4, 4, 2, 8
NY = NY_LO * NY_HI

S = 32
C = 256
HID = 1024
PIX = S * S
PITCH = 40
ROWS = 38


class Place:
    def __init__(self):
        dp = lax.axis_index("dp")
        space = lax.axis_index("space")
        self.core = lax.rem(dp, CORES)
        self.y_hi = lax.rem(dp // CORES, NY_HI)
        self.z = dp // (CORES * NY_HI)
        self.x = lax.rem(space, NX)
        self.y_lo = space // NX
        self.y = self.y_hi * NY_LO + self.y_lo
        self.dp = dp
        self.space = space

    def at(self, core=None, x=None, y=None, z=None):
        core = self.core if core is None else core
        x = self.x if x is None else x
        y = self.y if y is None else y
        z = self.z if z is None else z
        dp = (z * NY_HI + y // NY_LO) * CORES + core
        return {"dp": dp, "space": lax.rem(y, NY_LO) * NX + x}


def greet(devices):
    barrier = pltpu.get_barrier_semaphore()
    for device in devices:
        pl.semaphore_signal(barrier, inc=1, device_id=device, device_id_type=MESH)
    pl.semaphore_wait(barrier, len(devices))


class Copies:
    def __init__(self, send_sems, recv_sems):
        self.send_sems = send_sems
        self.recv_sems = recv_sems
        self.used = 0
        self.started = []

    def send(self, src, dst, device):
        copy = pltpu.make_async_remote_copy(
            src_ref=src,
            dst_ref=dst,
            send_sem=self.send_sems.at[self.used],
            recv_sem=self.recv_sems.at[self.used],
            device_id=device,
            device_id_type=MESH,
        )
        copy.start()
        self.used += 1
        self.started.append(copy)
        return copy

    def finish(self):
        for copy in self.started:
            copy.wait_send()


HALF = C // 2


def own_strips(x_ref, xf, gath_y, gath_x, me):
    turn = reversal()
    xf[...] = x_ref[...].astype(F32)

    def put(side, r, rows):
        gath_y[me.y_lo, side, r] = rows[:, :HALF]
        gath_x[me.x, side, r] = rows[:, HALF:]

    for r in range(3):
        put(0, r, x_ref[r])
        put(2, r, flip(turn, x_ref[S - 1 - r]))
        put(1, r, xf[:, S - 1 - r, :].astype(BF16))
        put(3, r, flip(turn, xf[:, r, :].astype(BF16)))


class Rims:
    def __init__(self, net, ids, codes, gath, out_s, out_c, in_s, in_c, cf, gather_at, choose_at, gather_to, choose_to, tile_at, split):
        self.net = net
        self.ids, self.codes = ids, codes
        self.gath, self.out_s, self.out_c, self.in_s, self.in_c, self.cf = gath, out_s, out_c, in_s, in_c, cf
        self.gather_at, self.choose_at = gather_at, choose_at
        self.gather_to, self.choose_to = gather_to, choose_to
        self.tile_at, self.split = tile_at, split

    def gather(self):
        at = self.gather_at
        self.first = [
            self.net.send(self.gath.at[at], self.gath.at[at], self.gather_to[k - 1])
            for k in (2, 1, 3)
        ]

    def choose(self):
        for copy in self.first:
            copy.wait_recv()
        self.second = []
        at = self.choose_at
        for k in (2, 1, 3, 0):
            target = self.tile_at(lax.rem(at + k, 4))
            for s in range(8):
                row, _ = self.split(jnp.maximum(self.ids[s, target], 0))
                e = self.codes[s, target]
                if s < 4:
                    piece = self.gath[row, e]
                    if k:
                        self.out_s[k - 1, s] = piece
                    else:
                        self.in_s[at, s] = piece
                else:
                    piece = self.gath[row, e, :, 0:16, :].astype(F32)
                    for r in range(3):
                        self.cf[pl.ds(16 * (s - 4) + 4 * r, 4), :] = piece[r, 0:4]
            packed = self.cf[...].astype(BF16)
            if k:
                self.out_c[k - 1] = packed
                to = self.choose_to[k - 1]
                self.second.append(self.net.send(self.out_s.at[k - 1], self.in_s.at[at], to))
                self.second.append(self.net.send(self.out_c.at[k - 1], self.in_c.at[at], to))
            else:
                self.in_c[at] = packed

    def take(self, sides, corners, chans, space):
        for copy in self.second:
            copy.wait_recv()
        for s in range(8):
            n = self.ids[s, space]
            _, col = self.split(jnp.maximum(n, 0))
            if s < 4:
                sides[s, :, :, chans] = self.in_s[col, s]
            else:
                piece = self.in_c[col, pl.ds(16 * (s - 4), 16)]
                corners[s - 4, :, chans] = jnp.where(n >= 0, piece, jnp.zeros_like(piece))


def both_rims(net, me, ids, codes, along_y, along_x, bufs_y, bufs_x):
    by_y = Rims(
        net, ids, codes, *bufs_y, me.y_lo, me.x, along_y, along_x,
        lambda x: me.y_lo * NX + x, lambda n: (n // NX, lax.rem(n, NX)),
    )
    by_x = Rims(
        net, ids, codes, *bufs_x, me.x, me.y_lo, along_x, along_y,
        lambda y: y * NX + me.x, lambda n: (lax.rem(n, NX), n // NX),
    )
    return by_y, by_x


def rim_partners(me):
    base = me.y_hi * NY_LO
    along_y = [me.at(y=base + lax.rem(me.y_lo + k, NY_LO)) for k in range(1, NY_LO)]
    along_x = [me.at(x=lax.rem(me.x + k, NX)) for k in range(1, NX)]
    return along_y, along_x


RIM_COPIES = 2 * 9


def rim_scratch():
    half = [
        pltpu.VMEM((4, 4, 3, S, HALF), BF16),
        pltpu.VMEM((3, 4, 3, S, HALF), BF16),
        pltpu.VMEM((3, 64, HALF), BF16),
        pltpu.VMEM((4, 4, 3, S, HALF), BF16),
        pltpu.VMEM((4, 64, HALF), BF16),
        pltpu.VMEM((64, HALF), F32),
    ]
    return half * 2


def reversal():
    row = lax.broadcasted_iota(jnp.int32, (S, S), 0)
    col = lax.broadcasted_iota(jnp.int32, (S, S), 1)
    return jnp.where(row + col == S - 1, 1.0, 0.0).astype(BF16)


def flip(turn, rows):
    return jnp.dot(turn, rows, preferred_element_type=F32).astype(rows.dtype)


INNER = S - 6
NORM_ROWS = 13
NORM_PIX = NORM_ROWS * S
ACT_ROWS = 208
IN_PIX = INNER * S
IN_PAD = 896
EDGE = 3 * S
SIDE_AT = 2 * EDGE
OUT_PIX = SIDE_AT + INNER * 8
OUT_PAD = 512


def frame_inside(xf, fr):
    fr[...] = jnp.zeros_like(fr)

    def one_row(i, carry):
        fr[3 + i, 3 : 3 + S, :] = xf[i]
        return carry

    lax.fori_loop(0, S, one_row, 0)


def frame_rims(sides, corners, fr, cf, chans):
    turn = reversal()
    for r in range(3):
        fr[r, 3 : 3 + S, chans] = flip(turn, sides[0, 2 - r, :, chans]).astype(F32)
        fr[3 : 3 + S, 35 + r, chans] = flip(turn, sides[1, r, :, chans]).astype(F32)
        fr[35 + r, 3 : 3 + S, chans] = sides[2, r, :, chans].astype(F32)
        fr[3 : 3 + S, r, chans] = sides[3, 2 - r, :, chans].astype(F32)
    cf[:, :, chans] = corners[:, :, chans].astype(F32)
    for i in range(3):
        for j in range(3):
            fr[i, j, chans] = cf[0, 4 * (2 - i) + 2 - j, chans]
            fr[i, 35 + j, chans] = cf[1, 4 * j + 2 - i, chans]
            fr[35 + i, 35 + j, chans] = cf[2, 4 * i + j, chans]
            fr[35 + i, j, chans] = cf[3, 4 * (2 - j) + i, chans]


def shift_rows(fr, fb, first, count, chans=slice(0, C)):
    def one_row(i, carry):
        for b in range(7):
            fb[b, first + i, :, chans] = fr[first + i, b : b + S, chans]
        return carry

    lax.fori_loop(0, count, one_row, 0)


def shift_sides(fr, fs, chans):
    fs[:, :, :, chans] = jnp.zeros((7, S, 8, HALF), F32)

    def one_row(i, carry):
        for b in range(7):
            fs[b, i, 0:3, chans] = fr[3 + i, b : b + 3, chans]
            fs[b, i, 3:6, chans] = fr[3 + i, 29 + b : 32 + b, chans]
        return carry

    lax.fori_loop(0, S, one_row, 0)


def lanes(g):
    return (
        pl.ds(pl.multiple_of((g // 2) * 8, 8), 8),
        pl.ds(pl.multiple_of(lax.rem(g, 2) * 128, 128), 128),
    )


def convolve(load, taps, chans, count, put):
    acc = [None] * count
    for b in range(7):
        k = [jnp.broadcast_to(taps[pl.ds(7 * a + b, 1), chans], (8, 128)) for a in range(7)]
        for i in range(count + 6):
            f = load(b, i)
            for a in range(7):
                at = i - a
                if 0 <= at < count:
                    term = f * k[a]
                    acc[at] = term if acc[at] is None else acc[at] + term
    for i in range(count):
        put(i, acc[i])


def correlate(load, d, kg, chans):
    count = len(d)
    for b in range(7):
        acc = [None] * 7
        for i in range(count + 6):
            f = load(b, i)
            for a in range(7):
                at = i - a
                if 0 <= at < count:
                    term = f * d[at]
                    acc[a] = term if acc[a] is None else acc[a] + term
        for a in range(7):
            kg[7 * a + b, :, chans] += acc[a]


def normalise(v):
    mean = jnp.mean(v, axis=-1, keepdims=True)
    v = v - mean
    inverse = lax.rsqrt(jnp.mean(v * v, axis=-1, keepdims=True) + EPSILON)
    return v * inverse, inverse


def norm_backward(sg, normed, inverse, gain):
    g = sg * gain
    mean = jnp.mean(g, axis=-1, keepdims=True)
    along = jnp.mean(g * normed, axis=-1, keepdims=True)
    return (g - mean - normed * along) * jnp.concatenate([inverse, inverse], axis=1)


def gelu_and_slope(v):
    root = 0.7978845608028654
    square = v * v
    inner = v * (root + (root * 0.044715) * square)
    t = jnp.tanh(inner)
    half = 0.5 * (1.0 + t)
    slope = half + (0.5 * v) * (1.0 - t * t) * (root + (3.0 * root * 0.044715) * square)
    return v * half, slope


def dot(left, right):
    return jnp.dot(left, right, preferred_element_type=F32)


class Inside:
    def __init__(self, w, fb, bufs):
        self.w, self.fb = w, fb
        (self.normed, self.inv, self.scaled, self.cot, self.branch, self.scaled_t, self.cot_t,
         self.pre, self.hg, self.hid, self.pg, self.sg) = bufs

    def depthwise(self):
        def step(g, carry):
            cols, chans = lanes(g)

            def put(i, value):
                self.normed[i, cols, chans] = value

            convolve(lambda b, i: self.fb[b, 3 + i, cols, chans], self.w.taps, chans, INNER, put)
            return carry

        lax.fori_loop(0, 8, step, 0)

    def norm(self):
        w = self.w
        col = lax.rem(lax.broadcasted_iota(jnp.int32, (S, C), 0), S)
        here = ((col >= 3) & (col < S - 3))[None]

        def step(q, carry):
            rows = pl.ds(q * NORM_ROWS, NORM_ROWS)
            flat = pl.ds(pl.multiple_of(q * NORM_PIX, 32), NORM_PIX)
            normed, inverse = normalise(self.normed[rows].reshape(NORM_PIX, C))
            self.inv[flat] = jnp.broadcast_to(inverse, (NORM_PIX, 128))
            self.normed[rows] = normed.reshape(NORM_ROWS, S, C)
            self.scaled[flat] = (normed * w.gain[...]).astype(BF16)
            cot = w.cot[pl.ds(pl.multiple_of(3 * S + q * NORM_PIX, 32), NORM_PIX)].astype(F32)
            cot = cot.reshape(NORM_ROWS, S, C)
            cot = jnp.where(here, cot, jnp.zeros_like(cot)).reshape(NORM_PIX, C)
            self.cot[flat] = cot.astype(BF16)
            self.branch[flat] = (cot * w.layer[...]).astype(BF16)
            return carry

        lax.fori_loop(0, INNER // NORM_ROWS, step, 0)
        rest = slice(IN_PIX, IN_PAD)
        none = jnp.zeros((IN_PAD - IN_PIX, C), BF16)
        self.scaled[rest] = none
        self.cot[rest] = none
        self.hid[rest] = none
        for h in range(4):
            self.pg[rest, 256 * h : 256 * h + 256] = none
        self.scaled_t[...] = self.scaled[...].T
        self.cot_t[...] = self.cot[...].T

    def hidden(self, h, gacc, iacc):
        w = self.w
        part = slice(256 * h, 256 * h + 256)
        self.pre[...] = dot(self.scaled[0:IN_PIX], w.w_in[:, part])
        self.hg[...] = dot(self.branch[...], w.w_out_t[:, part])

        def act(q, carry):
            rows = pl.ds(pl.multiple_of(q * ACT_ROWS, 16), ACT_ROWS)
            value, slope = gelu_and_slope(self.pre[rows])
            self.hid[rows] = value.astype(BF16)
            self.pg[rows, part] = (self.hg[rows] * slope).astype(BF16)
            return carry

        lax.fori_loop(0, IN_PIX // ACT_ROWS, act, 0)
        gacc[:, part] = dot(self.cot_t[...], self.hid[...])
        iacc[:, part] = dot(self.scaled_t[...], self.pg[:, part])

    def backward(self, gain_acc):
        w = self.w
        self.sg[...] = dot(self.pg[0:IN_PIX], w.w_in_t[...])

        def step(q, total):
            rows = pl.ds(q * NORM_ROWS, NORM_ROWS)
            flat = pl.ds(pl.multiple_of(q * NORM_PIX, 32), NORM_PIX)
            normed = self.normed[rows].reshape(NORM_PIX, C)
            sg = self.sg[flat]
            grad = norm_backward(sg, normed, self.inv[flat], w.gain[...])
            self.normed[rows] = grad.reshape(NORM_ROWS, S, C)
            return total + jnp.sum((sg * normed).reshape(NORM_PIX // 8, 8, C), axis=0)

        gain_acc[...] = lax.fori_loop(0, INNER // NORM_ROWS, step, jnp.zeros((8, C), F32))

    def kernel_grad(self, kg):
        def step(g, carry):
            cols, chans = lanes(g)
            d = [self.normed[i, cols, chans] for i in range(INNER)]
            correlate(lambda b, i: self.fb[b, 3 + i, cols, chans], d, kg, chans)
            return carry

        lax.fori_loop(0, 8, step, 0)


class Border:
    def __init__(self, w, fb, fs, bufs):
        self.w, self.fb, self.fs = w, fb, fs
        (self.normed, self.inv, self.scaled, self.cot, self.branch, self.scaled_t, self.cot_t,
         self.pre, self.hg, self.hid, self.pg, self.sg, self.cf) = bufs

    def cotangent(self):
        w = self.w
        self.cf[...] = jnp.zeros_like(self.cf)
        self.cf[0:EDGE] = w.cot[0:EDGE].astype(F32)
        self.cf[EDGE : 2 * EDGE] = w.cot[PIX - EDGE : PIX].astype(F32)
        for i in range(INNER):
            row = w.cot[(3 + i) * S : (4 + i) * S].astype(F32)
            at = SIDE_AT + 8 * i
            self.cf[at : at + 3] = row[0:3]
            self.cf[at + 3 : at + 6] = row[29:32]
        self.cot[...] = self.cf[...].astype(BF16)
        self.branch[...] = (self.cf[...] * w.layer[...]).astype(BF16)
        self.cot_t[...] = self.cot[...].T
        rest = slice(OUT_PIX, OUT_PAD)
        none = jnp.zeros((OUT_PAD - OUT_PIX, C), BF16)
        self.scaled[rest] = none
        for h in range(4):
            self.hid[rest, 256 * h : 256 * h + 256] = none
            self.pg[rest, 256 * h : 256 * h + 256] = none

    def depthwise(self, chans):
        def put_side(i, value):
            self.normed[SIDE_AT + 8 * i : SIDE_AT + 8 * i + 8, chans] = value

        convolve(lambda b, i: self.fs[b, i, :, chans], self.w.taps, chans, INNER, put_side)
        for first, at in ((0, 0), (S - 3, EDGE)):
            for j in range(0, S, 8):

                def put(i, value):
                    self.normed[at + S * i + j : at + S * i + j + 8, chans] = value

                convolve(
                    lambda b, i: self.fb[b, first + i, j : j + 8, chans],
                    self.w.taps, chans, 3, put,
                )

    def norm(self):
        w = self.w
        for at in range(0, OUT_PIX, 80):
            rows = slice(at, at + 80)
            normed, inverse = normalise(self.normed[rows])
            self.inv[rows] = jnp.broadcast_to(inverse, (80, 128))
            self.normed[rows] = normed
            self.scaled[rows] = (normed * w.gain[...]).astype(BF16)
        self.scaled_t[...] = self.scaled[...].T

    def hidden_grad(self):
        for h in range(4):
            part = slice(256 * h, 256 * h + 256)
            self.hg[h] = dot(self.branch[0:OUT_PIX], self.w.w_out_t[:, part])

    def products(self, h):
        part = slice(256 * h, 256 * h + 256)
        self.pre[h % 2] = dot(self.scaled[0:OUT_PIX], self.w.w_in[:, part])

    def hidden(self):
        self.products(0)
        for h in range(4):
            if h < 3:
                self.products(h + 1)
            part = slice(256 * h, 256 * h + 256)
            for at in range(0, OUT_PIX, 16):
                rows = slice(at, at + 16)
                value, slope = gelu_and_slope(self.pre[h % 2, rows])
                self.hid[rows, part] = value.astype(BF16)
                self.pg[rows, part] = (self.hg[h, rows] * slope).astype(BF16)

    def out_grad(self, gacc, big):
        w = self.w
        scale = jnp.zeros((1, C), F32)
        for h in range(4):
            part = slice(256 * h, 256 * h + 256)
            g = (gacc[:, part] + dot(self.cot_t[...], self.hid[:, part])).T
            big[part] = (g * w.layer[...]).astype(BF16)
            scale += jnp.sum(g * w.w_out[part].astype(F32), axis=0, keepdims=True)
        return scale

    def in_grad(self, iacc, big):
        for h in range(4):
            part = slice(256 * h, 256 * h + 256)
            total = iacc[:, part] + dot(self.scaled_t[...], self.pg[:, part])
            big[HID + 256 * h : HID + 256 * h + 256] = total.astype(BF16)

    def scaled_grad(self):
        self.sg[...] = dot(self.pg[0:OUT_PIX], self.w.w_in_t[...])

    def backward(self, gain_acc):
        total = gain_acc[...]
        for at in range(0, OUT_PIX, 80):
            rows = slice(at, at + 80)
            normed = self.normed[rows]
            sg = self.sg[rows]
            total += jnp.sum((sg * normed).reshape(10, 8, C), axis=0)
            self.normed[rows] = norm_backward(sg, normed, self.inv[rows], self.w.gain[...])
        return jnp.sum(total, axis=0, keepdims=True)

    def kernel_grad(self, kg):
        for chans in (slice(0, 128), slice(128, 256)):
            d = [self.normed[SIDE_AT + 8 * i : SIDE_AT + 8 * i + 8, chans] for i in range(INNER)]
            correlate(lambda b, i: self.fs[b, i, :, chans], d, kg, chans)
            for b in range(7):
                acc = [None] * 7
                for first, at in ((0, 0), (S - 3, EDGE)):
                    for j in range(0, S, 8):
                        d = [
                            self.normed[at + S * i + j : at + S * i + j + 8, chans]
                            for i in range(3)
                        ]
                        for i in range(9):
                            f = self.fb[b, first + i, j : j + 8, chans]
                            for a in range(7):
                                if 0 <= i - a < 3:
                                    term = f * d[i - a]
                                    acc[a] = term if acc[a] is None else acc[a] + term
                for a in range(7):
                    kg[7 * a + b, :, chans] += acc[a]


class Weights:
    def __init__(self, bufs):
        (self.taps, self.taps_in, self.gain, self.layer, self.w_in, self.w_in_t, self.w_out,
         self.w_out_t, self.cot) = bufs


def weight_scratch():
    return [
        pltpu.VMEM((49, C), F32),
        pltpu.VMEM((49, C), BF16),
        pltpu.VMEM((1, C), F32),
        pltpu.VMEM((1, C), F32),
        pltpu.VMEM((C, HID), BF16),
        pltpu.VMEM((HID, C), BF16),
        pltpu.VMEM((HID, C), BF16),
        pltpu.VMEM((C, HID), BF16),
        pltpu.VMEM((PIX, C), BF16),
    ]


def inside_scratch():
    return [
        pltpu.VMEM((INNER, S, C), F32),
        pltpu.VMEM((IN_PIX, 128), F32),
        pltpu.VMEM((IN_PAD, C), BF16),
        pltpu.VMEM((IN_PAD, C), BF16),
        pltpu.VMEM((IN_PIX, C), BF16),
        pltpu.VMEM((C, IN_PAD), BF16),
        pltpu.VMEM((C, IN_PAD), BF16),
        pltpu.VMEM((IN_PIX, 256), F32),
        pltpu.VMEM((IN_PIX, 256), F32),
        pltpu.VMEM((IN_PAD, 256), BF16),
        pltpu.VMEM((IN_PAD, HID), BF16),
        pltpu.VMEM((IN_PIX, C), F32),
    ]


def border_scratch():
    return [
        pltpu.VMEM((OUT_PIX, C), F32),
        pltpu.VMEM((OUT_PIX, 128), F32),
        pltpu.VMEM((OUT_PAD, C), BF16),
        pltpu.VMEM((OUT_PAD, C), BF16),
        pltpu.VMEM((OUT_PAD, C), BF16),
        pltpu.VMEM((C, OUT_PAD), BF16),
        pltpu.VMEM((C, OUT_PAD), BF16),
        pltpu.VMEM((2, OUT_PIX, 256), F32),
        pltpu.VMEM((4, OUT_PIX, 256), F32),
        pltpu.VMEM((OUT_PAD, HID), BF16),
        pltpu.VMEM((OUT_PAD, HID), BF16),
        pltpu.VMEM((OUT_PIX, C), F32),
        pltpu.VMEM((OUT_PAD, C), F32),
    ]


FAR_FIRST = (4, 3, 5, 2, 6, 1, 7)


def added(first, rest, count):
    total = first.astype(F32)
    for k in range(count):
        total += rest[k].astype(F32)
    return total


CROSS = 384
CHUNK = CROSS // 8
PLANE = 256
PLANE_AT = 2 * CROSS


class CrossSum:
    def __init__(self, net, me, peers, big, base, first, bufs):
        self.net, self.me, self.big, self.base = net, me, big, base
        self.peers = peers
        self.at, self.to = (me.z, peers.z) if first == "z" else (me.y, peers.y)
        self.other_at, self.other_to = (me.y, peers.y) if first == "z" else (me.z, peers.z)
        self.r0, self.s1, self.r1, self.s2, self.r2, self.s3, self.r3, self.fin = bufs

    def half(self, core):
        return pl.ds(pl.multiple_of(self.base + core * CROSS, 128), CROSS)

    def start(self):
        self.c0 = self.net.send(self.big.at[self.half(1 - self.me.core)], self.r0, self.peers.mate)

    def over_first(self):
        self.c0.wait_recv()
        own = self.big[self.half(self.me.core)]
        self.s1[...] = added(own, [self.r0[...]], 1).astype(BF16).reshape(8, CHUNK, C)
        self.c1 = [
            self.net.send(self.s1.at[lax.rem(self.at + k, 8)], self.r1.at[k - 1], self.to[k - 1])
            for k in FAR_FIRST
        ]

    def over_x(self):
        for copy in self.c1:
            copy.wait_recv()
        self.s2[...] = added(self.s1[self.at], self.r1, 7).astype(BF16)
        x = self.me.x
        self.r2[x] = self.s2[...]
        self.c2 = [self.net.send(self.s2, self.r2.at[x], self.peers.x[k - 1]) for k in (2, 1, 3)]

    def over_other(self):
        for copy in self.c2:
            copy.wait_recv()
        total = added(self.r2[0], [self.r2[k] for k in range(1, NX)], NX - 1)
        self.s3[...] = total.astype(BF16)
        at = self.other_at
        self.r3[at] = self.s3[...]
        self.c3 = [self.net.send(self.s3, self.r3.at[at], self.other_to[k - 1]) for k in FAR_FIRST]

    def back_first(self):
        for copy in self.c3:
            copy.wait_recv()
        total = added(self.r3[0], [self.r3[k] for k in range(1, 8)], 7)
        core = self.me.core
        self.fin[core, self.at] = total.astype(BF16)
        mine = self.fin.at[core, self.at]
        self.c4 = [self.net.send(mine, mine, self.to[k - 1]) for k in FAR_FIRST]

    def back_core(self):
        for copy in self.c4:
            copy.wait_recv()
        mine = self.fin.at[self.me.core]
        self.c5 = self.net.send(mine, mine, self.peers.mate)

    def finish(self):
        self.c5.wait_recv()


class PlaneSum:
    def __init__(self, net, me, peers, big, bufs):
        self.net, self.me, self.peers, self.big = net, me, peers, big
        self.r0, self.s1, self.r1, self.s2, self.r2, self.s3, self.r3, self.fin = bufs

    def half(self, core):
        return pl.ds(pl.multiple_of(PLANE_AT + core * PLANE, 256), PLANE)

    def start(self):
        self.c0 = self.net.send(self.big.at[self.half(1 - self.me.core)], self.r0, self.peers.mate)

    def over_x(self):
        self.c0.wait_recv()
        own = self.big[self.half(self.me.core)]
        self.s1[...] = added(own, [self.r0[...]], 1).astype(BF16).reshape(NX, 64, C)
        x = self.me.x
        self.c1 = [
            self.net.send(self.s1.at[lax.rem(x + k, NX)], self.r1.at[k - 1], self.peers.x[k - 1])
            for k in (2, 1, 3)
        ]

    def over_y(self):
        for copy in self.c1:
            copy.wait_recv()
        total = added(self.s1[self.me.x], self.r1, NX - 1).astype(BF16)
        for t in range(NY):
            rows, cols = 16 * (t // 2), 128 * (t % 2)
            self.s2[t] = total[rows : rows + 16, cols : cols + 128]
        y = self.me.y
        self.c2 = [
            self.net.send(self.s2.at[lax.rem(y + k, NY)], self.r2.at[k - 1], self.peers.y[k - 1])
            for k in FAR_FIRST
        ]

    def over_z(self):
        for copy in self.c2:
            copy.wait_recv()
        self.s3[...] = added(self.s2[self.me.y], self.r2, NY - 1).astype(BF16)
        z = self.me.z
        self.r3[z] = self.s3[...]
        self.c3 = [self.net.send(self.s3, self.r3.at[z], self.peers.z[k - 1]) for k in FAR_FIRST]

    def back_y(self):
        for copy in self.c3:
            copy.wait_recv()
        me = self.me
        total = added(self.r3[0], [self.r3[k] for k in range(1, NZ)], NZ - 1)
        at = (lax.rem(me.y, 2), me.core, me.x, me.y // 2)
        self.fin[at] = total.astype(BF16)
        mine = self.fin.at[at]
        self.c4 = [self.net.send(mine, mine, self.peers.y[k - 1]) for k in FAR_FIRST]

    def back_x(self):
        for copy in self.c4:
            copy.wait_recv()
        self.c5 = []
        for k in (2, 1, 3):
            for half in range(2):
                mine = self.fin.at[half, self.me.core, self.me.x]
                self.c5.append(self.net.send(mine, mine, self.peers.x[k - 1]))

    def back_core(self):
        for copy in self.c5:
            copy.wait_recv()
        self.c6 = []
        for half in range(2):
            mine = self.fin.at[half, self.me.core]
            self.c6.append(self.net.send(mine, mine, self.peers.mate))

    def finish(self):
        for copy in self.c6:
            copy.wait_recv()


class SmallSum:
    def __init__(self, net, me, peers, small, bufs):
        self.net, self.me, self.peers, self.small = net, me, peers, small
        self.r0, self.s1, self.r1, self.s2, self.r2, self.s3, self.r3, self.fin = bufs

    def start(self):
        half = pl.ds(pl.multiple_of((1 - self.me.core) * 32, 32), 32)
        self.c0 = self.net.send(self.small.at[half], self.r0, self.peers.mate)

    def over_x(self):
        self.c0.wait_recv()
        own = self.small[pl.ds(pl.multiple_of(self.me.core * 32, 32), 32)]
        self.s1[...] = (own + self.r0[...]).reshape(NX, 8, C)
        x = self.me.x
        self.c1 = [
            self.net.send(self.s1.at[lax.rem(x + k, NX)], self.r1.at[k - 1], self.peers.x[k - 1])
            for k in (2, 1, 3)
        ]

    def over_y(self):
        for copy in self.c1:
            copy.wait_recv()
        self.s2[...] = added(self.s1[self.me.x], self.r1, NX - 1)
        y = self.me.y
        self.r2[y] = self.s2[...]
        self.c2 = [self.net.send(self.s2, self.r2.at[y], self.peers.y[k - 1]) for k in FAR_FIRST]

    def over_z(self):
        for copy in self.c2:
            copy.wait_recv()
        self.s3[...] = jnp.sum(self.r2[...], axis=0)
        z = self.me.z
        self.r3[z] = self.s3[...]
        self.c3 = [self.net.send(self.s3, self.r3.at[z], self.peers.z[k - 1]) for k in FAR_FIRST]

    def back_x(self):
        for copy in self.c3:
            copy.wait_recv()
        me = self.me
        self.fin[me.core, me.x] = jnp.sum(self.r3[...], axis=0)
        mine = self.fin.at[me.core, me.x]
        self.c4 = [self.net.send(mine, mine, self.peers.x[k - 1]) for k in (2, 1, 3)]

    def back_core(self):
        for copy in self.c4:
            copy.wait_recv()
        mine = self.fin.at[self.me.core]
        self.c5 = self.net.send(mine, mine, self.peers.mate)

    def finish(self):
        self.c5.wait_recv()


class Peers:
    def __init__(self, me):
        self.mate = me.at(core=1 - me.core)
        self.x = [me.at(x=lax.rem(me.x + k, NX)) for k in range(1, NX)]
        self.y = [me.at(y=lax.rem(me.y + k, NY)) for k in range(1, NY)]
        self.z = [me.at(z=lax.rem(me.z + k, NZ)) for k in range(1, NZ)]

    def all(self):
        return [self.mate] + self.x + self.y + self.z


SUM_COPIES = (1 + 3 + 7 + 7 + 7 + 6 + 2) + 2 * (1 + 7 + 3 + 7 + 7 + 1) + (1 + 3 + 7 + 7 + 3 + 1)


def sum_scratch():
    cross = [
        pltpu.VMEM((CROSS, C), BF16),
        pltpu.VMEM((8, CHUNK, C), BF16),
        pltpu.VMEM((7, CHUNK, C), BF16),
        pltpu.VMEM((CHUNK, C), BF16),
        pltpu.VMEM((NX, CHUNK, C), BF16),
        pltpu.VMEM((CHUNK, C), BF16),
        pltpu.VMEM((8, CHUNK, C), BF16),
    ]
    return cross * 2 + [
        pltpu.VMEM((PLANE, C), BF16),
        pltpu.VMEM((NX, 64, C), BF16),
        pltpu.VMEM((NX - 1, 64, C), BF16),
        pltpu.VMEM((NY, 16, 128), BF16),
        pltpu.VMEM((NY - 1, 16, 128), BF16),
        pltpu.VMEM((16, 128), BF16),
        pltpu.VMEM((NZ, 16, 128), BF16),
        pltpu.VMEM((32, C), F32),
        pltpu.VMEM((NX, 8, C), F32),
        pltpu.VMEM((NX - 1, 8, C), F32),
        pltpu.VMEM((8, C), F32),
        pltpu.VMEM((NY, 8, C), F32),
        pltpu.VMEM((8, C), F32),
        pltpu.VMEM((NZ, 8, C), F32),
    ]


def sum_sums(by_z, plane, by_y, smalls):
    plane.over_y()
    smalls.over_x()
    by_z.over_x()
    by_y.over_x()
    smalls.over_y()
    plane.over_z()
    by_z.over_other()
    by_y.over_other()
    smalls.over_z()
    plane.back_y()
    by_z.back_first()
    by_y.back_first()
    smalls.back_x()
    plane.back_x()
    by_z.back_core()
    smalls.back_core()
    by_y.back_core()
    plane.back_core()
    smalls.finish()
    by_z.finish()
    by_y.finish()
    plane.finish()


def shared_scratch():
    return [
        pltpu.SMEM((8, 16), jnp.int32),
        pltpu.SMEM((8, 16), jnp.int32),
        pltpu.VMEM((S, S, C), BF16),
        pltpu.VMEM((S, S, C), F32),
        pltpu.VMEM((ROWS, PITCH, C), F32),
        pltpu.VMEM((7, ROWS, S, C), F32),
        pltpu.VMEM((7, S, 8, C), F32),
        pltpu.VMEM((4, 3, S, C), BF16),
        pltpu.VMEM((4, 16, C), BF16),
        pltpu.VMEM((4, 16, C), F32),
        pltpu.VMEM((C, HID), F32),
        pltpu.VMEM((C, HID), F32),
        pltpu.VMEM((49, 8, C), F32),
        pltpu.VMEM((8, C), F32),
        pltpu.VMEM((2 * HID, C), BF16),
        pltpu.VMEM((64, C), F32),
    ]


def split_refs(refs, *lists):
    refs = list(refs)
    parts = []
    for scratch in lists:
        parts.append(refs[: len(scratch)])
        refs = refs[len(scratch) :]
    return parts + [refs]


def block_kernel(
    ids_in, codes_in, x_in, cot_in, taps_in, gain_in, layer_in, w_in_in, w_out_in,
    fin_z, fin_plane, fin_y, fin_small, *rest,
):
    shared, weights, rims, inner, outer, sums, sems = split_refs(
        rest, shared_scratch(), weight_scratch(), rim_scratch(), inside_scratch(),
        border_scratch(), sum_scratch(),
    )
    ids, codes, xb, xf, fr, fb, fs, sides, corners, cf, gacc, iacc, kg, gain_acc, big, small = shared
    ss, rs, ls = sems
    w = Weights(weights)
    me = Place()
    peers = Peers(me)
    along_y, along_x = rim_partners(me)
    partners = peers.all() + along_y

    barrier = pltpu.get_barrier_semaphore()
    for device in partners:
        pl.semaphore_signal(barrier, inc=1, device_id=device, device_id_type=MESH)
    loads = [
        pltpu.make_async_copy(src, dst, ls.at[i])
        for i, (src, dst) in enumerate(
            (
                (x_in, xb), (ids_in, ids), (codes_in, codes), (taps_in, w.taps_in),
                (gain_in, w.gain), (layer_in, w.layer), (w_in_in, w.w_in), (w_out_in, w.w_out),
                (cot_in, w.cot),
            )
        )
    ]
    for load in loads:
        load.start()
    loads[0].wait()
    own_strips(xb, xf, rims[0], rims[6], me)
    pl.semaphore_wait(barrier, len(partners))

    net = Copies(ss, rs)
    by_y, by_x = both_rims(net, me, ids, codes, along_y, along_x, rims[:6], rims[6:])
    by_y.gather()
    by_x.gather()
    for load in loads[1:]:
        load.wait()

    inside = Inside(w, fb, inner)
    border = Border(w, fb, fs, outer)
    frame_inside(xf, fr)
    shift_rows(fr, fb, 3, S)
    w.taps[...] = w.taps_in[...].astype(F32)
    inside.depthwise()
    w.w_out_t[...] = w.w_out[...].T
    w.w_in_t[...] = w.w_in[...].T
    inside.norm()
    by_x.choose()
    border.cotangent()
    border.hidden_grad()
    for h in range(3):
        inside.hidden(h, gacc, iacc)
    by_y.choose()
    for h in range(3, 4):
        inside.hidden(h, gacc, iacc)
    inside.backward(gain_acc)
    kg[...] = jnp.zeros_like(kg)
    inside.kernel_grad(kg)

    for rim, chans in ((by_y, slice(0, HALF)), (by_x, slice(HALF, C))):
        rim.take(sides, corners, chans, me.space)
        frame_rims(sides, corners, fr, cf, chans)
        shift_rows(fr, fb, 0, 9, chans)
        shift_rows(fr, fb, S - 3, 9, chans)
        shift_sides(fr, fs, chans)
        border.depthwise(chans)
    border.norm()
    border.hidden()
    sum_z = CrossSum(net, me, peers, big, 0, "z", sums[0:7] + [fin_z])
    sum_y = CrossSum(net, me, peers, big, PLANE_AT + 2 * PLANE, "y", sums[7:14] + [fin_y])
    plane = PlaneSum(net, me, peers, big, sums[14:21] + [fin_plane])
    smalls = SmallSum(net, me, peers, small, sums[21:28] + [fin_small])
    scale = border.out_grad(gacc, big)
    sum_z.start()
    border.in_grad(iacc, big)
    plane.start()
    sum_y.start()
    border.scaled_grad()
    sum_z.over_first()
    plane.over_x()
    sum_y.over_first()
    gain = border.backward(gain_acc)
    border.kernel_grad(kg)
    small[0:49] = jnp.sum(kg[...], axis=1)
    small[49:50] = gain
    small[50:51] = scale
    small[51:64] = jnp.zeros((13, C), F32)
    smalls.start()
    sum_sums(sum_z, plane, sum_y, smalls)
    net.finish()


def block_grads(neighbours, codes, tile, cot, kernel, ln_gain, layer_scale, w_in, w_out):
    vmem = pl.BlockSpec(memory_space=pltpu.VMEM)
    copies = RIM_COPIES + SUM_COPIES
    return pl.pallas_call(
        block_kernel,
        out_shape=(
            pltpu.VMEM((2, NZ, CHUNK, C), BF16),
            pltpu.VMEM((2, 2, NX, 4, 16, 128), BF16),
            pltpu.VMEM((2, NY, CHUNK, C), BF16),
            pltpu.VMEM((2, NX, 8, C), F32),
        ),
        in_specs=[pl.BlockSpec(memory_space=pl.ANY)] * 9,
        out_specs=(vmem,) * 4,
        scratch_shapes=shared_scratch() + weight_scratch() + rim_scratch() + inside_scratch()
        + border_scratch() + sum_scratch()
        + [pltpu.SemaphoreType.DMA((copies,))] * 2 + [pltpu.SemaphoreType.DMA((9,))],
        compiler_params=pltpu.CompilerParams(
            collective_id=0, has_side_effects=True, vmem_limit_bytes=60 * 2**20
        ),
    )(
        neighbours, codes, tile, cot, kernel, ln_gain.reshape(1, C), layer_scale.reshape(1, C),
        w_in, w_out,
    )


def hand_over_kernel(
    fin_z, fin_plane, fin_y, small, kg_out, gain_out, scale_out, in_out, out_out, kg, gain, scale, sems
):
    def move(pairs, first):
        copies = [
            pltpu.make_async_copy(src, dst, sems.at[first + i])
            for i, (src, dst) in enumerate(pairs)
        ]
        for copy in copies:
            copy.start()
        return copies

    rest = HID - PLANE_AT
    parts = [(fin_z, out_out.at[pl.ds(0, PLANE_AT)])]
    for q in range(1, HID // C):
        parts.append((fin_y.at[pl.ds(256 * (q - 1), 256)], in_out.at[:, pl.ds(256 * q, 256)]))
    for half in range(2):
        cols = pl.ds(128 * half, 128)
        parts.append((fin_plane.at[half, pl.ds(0, rest)], out_out.at[pl.ds(PLANE_AT, rest), cols]))
        parts.append((fin_plane.at[half, pl.ds(rest, C)], in_out.at[:, cols]))
    copies = move(parts, 0)
    kg[...] = small[0:49]
    gain[...] = small[49:50]
    scale[...] = small[50:51]
    copies += move([(kg, kg_out), (gain, gain_out), (scale, scale_out)], len(parts))
    for copy in copies:
        copy.wait()


def hand_over(fin_z, fin_plane, fin_y, fin_small):
    fins = (
        fin_z.reshape(2 * CROSS, C),
        fin_plane.reshape(2, 2 * PLANE, 128),
        fin_y.reshape(2 * CROSS, C),
        fin_small.reshape(64, C),
    )
    return pl.pallas_call(
        hand_over_kernel,
        out_shape=(
            jax.ShapeDtypeStruct((49, C), F32),
            jax.ShapeDtypeStruct((1, C), F32),
            jax.ShapeDtypeStruct((1, C), F32),
            jax.ShapeDtypeStruct((C, HID), BF16),
            jax.ShapeDtypeStruct((HID, C), BF16),
        ),
        in_specs=[pl.BlockSpec(memory_space=pltpu.VMEM)] * 4,
        out_specs=(pl.BlockSpec(memory_space=pl.ANY),) * 5,
        scratch_shapes=[
            pltpu.VMEM((49, C), F32),
            pltpu.VMEM((1, C), F32),
            pltpu.VMEM((1, C), F32),
            pltpu.SemaphoreType.DMA((11,)),
        ],
        compiler_params=pltpu.CompilerParams(has_side_effects=True),
    )(*[pltpu.with_memory_space_constraint(fin, pltpu.VMEM) for fin in fins])


def on_device(state, cotangent, kernel, ln_gain, w_in, w_out, layer_scale, neighbours, codes):
    sums = block_grads(
        neighbours.T, codes.T, state.reshape(S, S, C), cotangent.reshape(PIX, C), kernel, ln_gain,
        layer_scale, w_in, w_out,
    )
    kernel_grad, gain_grad, scale_grad, in_grad, out_grad = hand_over(*sums)
    return (kernel_grad, gain_grad.reshape(C), scale_grad.reshape(C), in_grad, out_grad)


def solution(mesh):
    placed = (P("dp", "space", None, None, None),) * 2 + (P(),) * 7
    return jax.shard_map(
        on_device, mesh=mesh, in_specs=placed, out_specs=(P(),) * 5, check_vma=False
    )
```

```python
import jax
import jax.numpy as jnp
from jax import lax
from jax.experimental import pallas as pl
from jax.experimental.pallas import tpu as pltpu
from jax.sharding import PartitionSpec as P

EPSILON = 1e-06
MESH = pl.DeviceIdType.MESH
F32 = jnp.float32
BF16 = jnp.bfloat16

CORES, NX, NY_LO, NY_HI, NZ = 2, 4, 4, 2, 8
NY = NY_LO * NY_HI

S = 32
C = 256
HID = 1024
PIX = S * S
PITCH = 40
ROWS = 38


class Place:
    def __init__(self):
        dp = lax.axis_index("dp")
        space = lax.axis_index("space")
        self.core = lax.rem(dp, CORES)
        self.y_hi = lax.rem(dp // CORES, NY_HI)
        self.z = dp // (CORES * NY_HI)
        self.x = lax.rem(space, NX)
        self.y_lo = space // NX
        self.y = self.y_hi * NY_LO + self.y_lo
        self.dp = dp
        self.space = space

    def at(self, core=None, x=None, y=None, z=None):
        core = self.core if core is None else core
        x = self.x if x is None else x
        y = self.y if y is None else y
        z = self.z if z is None else z
        dp = (z * NY_HI + y // NY_LO) * CORES + core
        return {"dp": dp, "space": lax.rem(y, NY_LO) * NX + x}


def greet(devices):
    barrier = pltpu.get_barrier_semaphore()
    for device in devices:
        pl.semaphore_signal(barrier, inc=1, device_id=device, device_id_type=MESH)
    pl.semaphore_wait(barrier, len(devices))


class Copies:
    def __init__(self, send_sems, recv_sems):
        self.send_sems = send_sems
        self.recv_sems = recv_sems
        self.used = 0
        self.started = []

    def send(self, src, dst, device):
        copy = pltpu.make_async_remote_copy(
            src_ref=src,
            dst_ref=dst,
            send_sem=self.send_sems.at[self.used],
            recv_sem=self.recv_sems.at[self.used],
            device_id=device,
            device_id_type=MESH,
        )
        copy.start()
        self.used += 1
        self.started.append(copy)
        return copy

    def settle(self, keep):
        at = len(self.started) - keep
        for copy in self.started[:at]:
            copy.wait_send()
        self.started = self.started[at:]

    def finish(self):
        self.settle(0)


HALF = C // 2


def own_strips(x_ref, xf, gath_y, gath_x, me):
    turn = reversal()
    xf[...] = x_ref[...].astype(F32)

    def put(side, r, rows):
        gath_y[me.y_lo, side, r] = rows[:, :HALF]
        gath_x[me.x, side, r] = rows[:, HALF:]

    for r in range(3):
        put(0, r, x_ref[r])
        put(2, r, flip(turn, x_ref[S - 1 - r]))
        put(1, r, xf[:, S - 1 - r, :].astype(BF16))
        put(3, r, flip(turn, xf[:, r, :].astype(BF16)))


class Rims:
    def __init__(self, net, ids, codes, gath, out_s, out_c, in_s, in_c, cf, gather_at, choose_at, gather_to, choose_to, tile_at, split):
        self.net = net
        self.ids, self.codes = ids, codes
        self.gath, self.out_s, self.out_c, self.in_s, self.in_c, self.cf = gath, out_s, out_c, in_s, in_c, cf
        self.gather_at, self.choose_at = gather_at, choose_at
        self.gather_to, self.choose_to = gather_to, choose_to
        self.tile_at, self.split = tile_at, split

    def gather(self):
        at = self.gather_at
        self.first = [
            self.net.send(self.gath.at[at], self.gath.at[at], self.gather_to[k - 1])
            for k in (2, 1, 3)
        ]

    def choose(self):
        for copy in self.first:
            copy.wait_recv()
        self.second = []
        at = self.choose_at
        for k in (2, 1, 3, 0):
            target = self.tile_at(lax.rem(at + k, 4))
            for s in range(8):
                row, _ = self.split(jnp.maximum(self.ids[s, target], 0))
                e = self.codes[s, target]
                if s < 4:
                    piece = self.gath[row, e]
                    if k:
                        self.out_s[k - 1, s] = piece
                    else:
                        self.in_s[at, s] = piece
                else:
                    piece = self.gath[row, e, :, 0:16, :].astype(F32)
                    for r in range(3):
                        self.cf[pl.ds(12 * (s - 4) + 4 * r, 4), :] = piece[r, 0:4]
            packed = self.cf[...].astype(BF16)
            if k:
                self.out_c[k - 1] = packed
                to = self.choose_to[k - 1]
                self.second.append(self.net.send(self.out_s.at[k - 1], self.in_s.at[at], to))
                self.second.append(self.net.send(self.out_c.at[k - 1], self.in_c.at[at], to))
            else:
                self.in_c[at] = packed

    def take(self, sides, corners, chans, space):
        for copy in self.second:
            copy.wait_recv()
        for s in range(8):
            n = self.ids[s, space]
            _, col = self.split(jnp.maximum(n, 0))
            if s < 4:
                sides[s, :, :, chans] = self.in_s[col, s]
            else:
                at = 12 * (s - 4)
                piece = self.in_c[col].astype(F32)[at : at + 12]
                corners[s - 4, 0:12, chans] = jnp.where(n >= 0, piece, jnp.zeros_like(piece))


def both_rims(net, me, ids, codes, along_y, along_x, bufs_y, bufs_x):
    by_y = Rims(
        net, ids, codes, *bufs_y, me.y_lo, me.x, along_y, along_x,
        lambda x: me.y_lo * NX + x, lambda n: (n // NX, lax.rem(n, NX)),
    )
    by_x = Rims(
        net, ids, codes, *bufs_x, me.x, me.y_lo, along_x, along_y,
        lambda y: y * NX + me.x, lambda n: (lax.rem(n, NX), n // NX),
    )
    return by_y, by_x


def rim_partners(me):
    base = me.y_hi * NY_LO
    along_y = [me.at(y=base + lax.rem(me.y_lo + k, NY_LO)) for k in range(1, NY_LO)]
    along_x = [me.at(x=lax.rem(me.x + k, NX)) for k in range(1, NX)]
    return along_y, along_x


RIM_COPIES = 2 * 9


def rim_scratch():
    half = [
        pltpu.VMEM((4, 4, 3, S, HALF), BF16),
        pltpu.VMEM((3, 4, 3, S, HALF), BF16),
        pltpu.VMEM((3, 48, HALF), BF16),
        pltpu.VMEM((4, 4, 3, S, HALF), BF16),
        pltpu.VMEM((4, 48, HALF), BF16),
        pltpu.VMEM((48, HALF), F32),
    ]
    return half * 2


def reversal():
    row = lax.broadcasted_iota(jnp.int32, (S, S), 0)
    col = lax.broadcasted_iota(jnp.int32, (S, S), 1)
    return jnp.where(row + col == S - 1, 1.0, 0.0).astype(BF16)


def flip(turn, rows):
    return jnp.dot(turn, rows, preferred_element_type=F32).astype(rows.dtype)


INNER = S - 6
NORM_ROWS = 13
NORM_PIX = NORM_ROWS * S
ACT_ROWS = 208
IN_PIX = INNER * S
IN_PAD = 896
EDGE = 3 * S
SIDE_AT = 2 * EDGE
OUT_PIX = SIDE_AT + INNER * 8
OUT_PAD = 512


def frame_inside(xf, fr):
    fr[...] = jnp.zeros_like(fr)

    def one_row(i, carry):
        fr[3 + i, 3 : 3 + S, :] = xf[i]
        return carry

    lax.fori_loop(0, S, one_row, 0)


def frame_rims(sides, cf, fr, chans):
    turn = reversal()
    for r in range(3):
        fr[r, 3 : 3 + S, chans] = flip(turn, sides[0, 2 - r, :, chans]).astype(F32)
        fr[3 : 3 + S, 35 + r, chans] = flip(turn, sides[1, r, :, chans]).astype(F32)
        fr[35 + r, 3 : 3 + S, chans] = sides[2, r, :, chans].astype(F32)
        fr[3 : 3 + S, r, chans] = sides[3, 2 - r, :, chans].astype(F32)
    for i in range(3):
        for j in range(3):
            fr[i, j, chans] = cf[0, 4 * (2 - i) + 2 - j, chans]
            fr[i, 35 + j, chans] = cf[1, 4 * j + 2 - i, chans]
            fr[35 + i, 35 + j, chans] = cf[2, 4 * i + j, chans]
            fr[35 + i, j, chans] = cf[3, 4 * (2 - j) + i, chans]


def shift_rows(fr, fb, first, count, chans=slice(0, C)):
    def one_row(i, carry):
        for b in range(7):
            fb[b, first + i, :, chans] = fr[first + i, b : b + S, chans]
        return carry

    lax.fori_loop(0, count, one_row, 0, unroll=3 if count % 3 == 0 else 4)


def shift_sides(fr, fs, chans):
    fs[:, :, :, chans] = jnp.zeros((7, S, 8, HALF), F32)

    def one_row(i, carry):
        for b in range(7):
            fs[b, i, 0:3, chans] = fr[3 + i, b : b + 3, chans]
            fs[b, i, 3:6, chans] = fr[3 + i, 29 + b : 32 + b, chans]
        return carry

    lax.fori_loop(0, S, one_row, 0, unroll=4)


def lanes(g):
    return (
        pl.ds(pl.multiple_of((g // 2) * 8, 8), 8),
        pl.ds(pl.multiple_of(lax.rem(g, 2) * 128, 128), 128),
    )


def convolve(load, taps, chans, count, put):
    acc = [None] * count
    for b in range(7):
        k = [jnp.broadcast_to(taps[pl.ds(7 * a + b, 1), chans], (8, 128)) for a in range(7)]
        for i in range(count + 6):
            f = load(b, i)
            for a in range(7):
                at = i - a
                if 0 <= at < count:
                    term = f * k[a]
                    acc[at] = term if acc[at] is None else acc[at] + term
    for i in range(count):
        put(i, acc[i])


def correlate(load, d, kg, chans):
    count = len(d)
    for b in range(7):
        acc = [None] * 7
        for i in range(count + 6):
            f = load(b, i)
            for a in range(7):
                at = i - a
                if 0 <= at < count:
                    term = f * d[at]
                    acc[a] = term if acc[a] is None else acc[a] + term
        for a in range(7):
            kg[7 * a + b, :, chans] += acc[a]


def normalise(v):
    mean = jnp.mean(v, axis=-1, keepdims=True)
    v = v - mean
    inverse = lax.rsqrt(jnp.mean(v * v, axis=-1, keepdims=True) + EPSILON)
    return v * inverse, inverse


def norm_backward(sg, normed, inverse, gain):
    g = sg * gain
    mean = jnp.mean(g, axis=-1, keepdims=True)
    along = jnp.mean(g * normed, axis=-1, keepdims=True)
    return (g - mean - normed * along) * jnp.concatenate([inverse, inverse], axis=1)


def gelu_and_slope(v):
    root = 0.7978845608028654
    square = v * v
    inner = v * (root + (root * 0.044715) * square)
    t = jnp.tanh(inner)
    half = 0.5 + 0.5 * t
    value = v * half
    slope = half + value * (1.0 - half) * (2.0 * root + (6.0 * root * 0.044715) * square)
    return value, slope


def dot(left, right):
    return jnp.dot(left, right, preferred_element_type=F32)


class Inside:
    def __init__(self, w, fb, bufs):
        self.w, self.fb = w, fb
        (self.normed, self.inv, self.scaled, self.cot, self.branch, self.scaled_t, self.cot_t,
         self.pre, self.hg, self.hid, self.pg, self.sg) = bufs

    def depthwise(self):
        def step(g, carry):
            cols, chans = lanes(g)

            def put(i, value):
                self.normed[i, cols, chans] = value

            convolve(lambda b, i: self.fb[b, 3 + i, cols, chans], self.w.taps, chans, INNER, put)
            return carry

        lax.fori_loop(0, 8, step, 0)

    def norm(self):
        w = self.w
        col = lax.rem(lax.broadcasted_iota(jnp.int32, (S, C), 0), S)
        here = ((col >= 3) & (col < S - 3))[None]

        def step(q, carry):
            rows = pl.ds(q * NORM_ROWS, NORM_ROWS)
            flat = pl.ds(pl.multiple_of(q * NORM_PIX, 32), NORM_PIX)
            normed, inverse = normalise(self.normed[rows].reshape(NORM_PIX, C))
            self.inv[flat] = jnp.broadcast_to(inverse, (NORM_PIX, 128))
            self.normed[rows] = normed.reshape(NORM_ROWS, S, C)
            self.scaled[flat] = (normed * w.gain[...]).astype(BF16)
            cot = w.cot[pl.ds(pl.multiple_of(3 * S + q * NORM_PIX, 32), NORM_PIX)].astype(F32)
            cot = cot.reshape(NORM_ROWS, S, C)
            cot = jnp.where(here, cot, jnp.zeros_like(cot)).reshape(NORM_PIX, C)
            self.cot[flat] = cot.astype(BF16)
            self.branch[flat] = (cot * w.layer[...]).astype(BF16)
            return carry

        lax.fori_loop(0, INNER // NORM_ROWS, step, 0)
        rest = slice(IN_PIX, IN_PAD)
        none = jnp.zeros((IN_PAD - IN_PIX, C), BF16)
        self.scaled[rest] = none
        self.cot[rest] = none
        self.hid[rest] = none
        for h in range(4):
            self.pg[rest, 256 * h : 256 * h + 256] = none
        self.scaled_t[...] = self.scaled[...].T
        self.cot_t[...] = self.cot[...].T

    def hidden(self, h, gacc, iacc):
        w = self.w
        part = slice(256 * h, 256 * h + 256)
        self.pre[...] = dot(self.scaled[0:IN_PIX], w.w_in[:, part])
        self.hg[...] = dot(self.branch[...], w.w_out_t[:, part])

        def act(q, carry):
            rows = pl.ds(pl.multiple_of(q * ACT_ROWS, 16), ACT_ROWS)
            value, slope = gelu_and_slope(self.pre[rows])
            self.hid[rows] = value.astype(BF16)
            self.pg[rows, part] = (self.hg[rows] * slope).astype(BF16)
            return carry

        lax.fori_loop(0, IN_PIX // ACT_ROWS, act, 0)
        gacc[:, part] = dot(self.cot_t[...], self.hid[...])
        iacc[:, part] = dot(self.scaled_t[...], self.pg[:, part])

    def backward(self, gain_acc):
        w = self.w
        self.sg[...] = dot(self.pg[0:IN_PIX], w.w_in_t[...])

        def step(q, total):
            rows = pl.ds(q * NORM_ROWS, NORM_ROWS)
            flat = pl.ds(pl.multiple_of(q * NORM_PIX, 32), NORM_PIX)
            normed = self.normed[rows].reshape(NORM_PIX, C)
            sg = self.sg[flat]
            grad = norm_backward(sg, normed, self.inv[flat], w.gain[...])
            self.normed[rows] = grad.reshape(NORM_ROWS, S, C)
            return total + jnp.sum((sg * normed).reshape(NORM_PIX // 8, 8, C), axis=0)

        gain_acc[...] = lax.fori_loop(0, INNER // NORM_ROWS, step, jnp.zeros((8, C), F32))

    def kernel_grad(self, kg):
        def step(g, carry):
            cols, chans = lanes(g)
            d = [self.normed[i, cols, chans] for i in range(INNER)]
            correlate(lambda b, i: self.fb[b, 3 + i, cols, chans], d, kg, chans)
            return carry

        lax.fori_loop(0, 8, step, 0)


class Border:
    def __init__(self, w, fb, fs, bufs):
        self.w, self.fb, self.fs = w, fb, fs
        (self.normed, self.inv, self.scaled, self.cot, self.branch, self.scaled_t, self.cot_t,
         self.pre, self.hg, self.hid, self.pg, self.sg, self.cf) = bufs

    def cotangent(self):
        w = self.w
        self.cf[...] = jnp.zeros_like(self.cf)
        self.cf[0:EDGE] = w.cot[0:EDGE].astype(F32)
        self.cf[EDGE : 2 * EDGE] = w.cot[PIX - EDGE : PIX].astype(F32)
        for i in range(INNER):
            row = w.cot[(3 + i) * S : (4 + i) * S].astype(F32)
            at = SIDE_AT + 8 * i
            self.cf[at : at + 3] = row[0:3]
            self.cf[at + 3 : at + 6] = row[29:32]
        self.cot[...] = self.cf[...].astype(BF16)
        self.branch[...] = (self.cf[...] * w.layer[...]).astype(BF16)
        self.cot_t[...] = self.cot[...].T
        rest = slice(OUT_PIX, OUT_PAD)
        none = jnp.zeros((OUT_PAD - OUT_PIX, C), BF16)
        self.scaled[rest] = none
        for h in range(4):
            self.hid[rest, 256 * h : 256 * h + 256] = none
            self.pg[rest, 256 * h : 256 * h + 256] = none

    def depthwise(self, chans):
        def put_side(i, value):
            self.normed[SIDE_AT + 8 * i : SIDE_AT + 8 * i + 8, chans] = value

        convolve(lambda b, i: self.fs[b, i, :, chans], self.w.taps, chans, INNER, put_side)
        for first, at in ((0, 0), (S - 3, EDGE)):
            for j in range(0, S, 8):

                def put(i, value):
                    self.normed[at + S * i + j : at + S * i + j + 8, chans] = value

                convolve(
                    lambda b, i: self.fb[b, first + i, j : j + 8, chans],
                    self.w.taps, chans, 3, put,
                )

    def norm(self):
        w = self.w
        for at in range(0, OUT_PIX, 80):
            rows = slice(at, at + 80)
            normed, inverse = normalise(self.normed[rows])
            self.inv[rows] = jnp.broadcast_to(inverse, (80, 128))
            self.normed[rows] = normed
            self.scaled[rows] = (normed * w.gain[...]).astype(BF16)
        self.scaled_t[...] = self.scaled[...].T

    def hidden_grad(self):
        for h in range(4):
            part = slice(256 * h, 256 * h + 256)
            self.hg[h] = dot(self.branch[0:OUT_PIX], self.w.w_out_t[:, part])

    def products(self, h):
        part = slice(256 * h, 256 * h + 256)
        self.pre[h % 2] = dot(self.scaled[0:OUT_PIX], self.w.w_in[:, part])

    def hidden(self):
        self.products(0)
        for h in range(4):
            if h < 3:
                self.products(h + 1)
            part = slice(256 * h, 256 * h + 256)
            for at in range(0, OUT_PIX, 16):
                rows = slice(at, at + 16)
                value, slope = gelu_and_slope(self.pre[h % 2, rows])
                self.hid[rows, part] = value.astype(BF16)
                self.pg[rows, part] = (self.hg[h, rows] * slope).astype(BF16)

    def out_grad(self, gacc, big):
        w = self.w
        scale = jnp.zeros((1, C), F32)
        for h in range(4):
            part = slice(256 * h, 256 * h + 256)
            g = (gacc[:, part] + dot(self.cot_t[...], self.hid[:, part])).T
            big[part] = (g * w.layer[...]).astype(BF16)
            scale += jnp.sum(g * w.w_out[part].astype(F32), axis=0, keepdims=True)
        return scale

    def in_grad(self, iacc, big):
        for h in range(4):
            part = slice(256 * h, 256 * h + 256)
            total = iacc[:, part] + dot(self.scaled_t[...], self.pg[:, part])
            big[HID + 256 * h : HID + 256 * h + 256] = total.astype(BF16)

    def scaled_grad(self):
        self.sg[...] = dot(self.pg[0:OUT_PIX], self.w.w_in_t[...])

    def backward(self, gain_acc):
        total = gain_acc[...]
        for at in range(0, OUT_PIX, 80):
            rows = slice(at, at + 80)
            normed = self.normed[rows]
            sg = self.sg[rows]
            total += jnp.sum((sg * normed).reshape(10, 8, C), axis=0)
            self.normed[rows] = norm_backward(sg, normed, self.inv[rows], self.w.gain[...])
        return jnp.sum(total, axis=0, keepdims=True)

    def kernel_grad(self, kg):
        for chans in (slice(0, 128), slice(128, 256)):
            d = [self.normed[SIDE_AT + 8 * i : SIDE_AT + 8 * i + 8, chans] for i in range(INNER)]
            correlate(lambda b, i: self.fs[b, i, :, chans], d, kg, chans)
            for b in range(7):
                acc = [None] * 7
                for first, at in ((0, 0), (S - 3, EDGE)):
                    for j in range(0, S, 8):
                        d = [
                            self.normed[at + S * i + j : at + S * i + j + 8, chans]
                            for i in range(3)
                        ]
                        for i in range(9):
                            f = self.fb[b, first + i, j : j + 8, chans]
                            for a in range(7):
                                if 0 <= i - a < 3:
                                    term = f * d[i - a]
                                    acc[a] = term if acc[a] is None else acc[a] + term
                for a in range(7):
                    kg[7 * a + b, :, chans] += acc[a]


class Weights:
    def __init__(self, bufs):
        (self.taps, self.taps_in, self.gain, self.layer, self.w_in, self.w_in_t, self.w_out,
         self.w_out_t, self.cot) = bufs


def weight_scratch():
    return [
        pltpu.VMEM((49, C), F32),
        pltpu.VMEM((49, C), BF16),
        pltpu.VMEM((1, C), F32),
        pltpu.VMEM((1, C), F32),
        pltpu.VMEM((C, HID), BF16),
        pltpu.VMEM((HID, C), BF16),
        pltpu.VMEM((HID, C), BF16),
        pltpu.VMEM((C, HID), BF16),
        pltpu.VMEM((PIX, C), BF16),
    ]


def inside_scratch():
    return [
        pltpu.VMEM((INNER, S, C), F32),
        pltpu.VMEM((IN_PIX, 128), F32),
        pltpu.VMEM((IN_PAD, C), BF16),
        pltpu.VMEM((IN_PAD, C), BF16),
        pltpu.VMEM((IN_PIX, C), BF16),
        pltpu.VMEM((C, IN_PAD), BF16),
        pltpu.VMEM((C, IN_PAD), BF16),
        pltpu.VMEM((IN_PIX, 256), F32),
        pltpu.VMEM((IN_PIX, 256), F32),
        pltpu.VMEM((IN_PAD, 256), BF16),
        pltpu.VMEM((IN_PAD, HID), BF16),
        pltpu.VMEM((IN_PIX, C), F32),
    ]


def border_scratch():
    return [
        pltpu.VMEM((OUT_PIX, C), F32),
        pltpu.VMEM((OUT_PIX, 128), F32),
        pltpu.VMEM((OUT_PAD, C), BF16),
        pltpu.VMEM((OUT_PAD, C), BF16),
        pltpu.VMEM((OUT_PAD, C), BF16),
        pltpu.VMEM((C, OUT_PAD), BF16),
        pltpu.VMEM((C, OUT_PAD), BF16),
        pltpu.VMEM((2, OUT_PIX, 256), F32),
        pltpu.VMEM((4, OUT_PIX, 256), F32),
        pltpu.VMEM((OUT_PAD, HID), BF16),
        pltpu.VMEM((OUT_PAD, HID), BF16),
        pltpu.VMEM((OUT_PIX, C), F32),
        pltpu.VMEM((OUT_PAD, C), F32),
    ]


FAR_FIRST = (4, 3, 5, 2, 6, 1, 7)


def added(first, rest, count):
    total = first.astype(F32)
    for k in range(count):
        total += rest[k].astype(F32)
    return total


CROSS = 384
CHUNK = CROSS // 8
PLANE = 256
PLANE_AT = 2 * CROSS


class CrossSum:
    def __init__(self, net, me, peers, big, base, first, bufs):
        self.net, self.me, self.big, self.base = net, me, big, base
        self.peers = peers
        self.at, self.to = (me.z, peers.z) if first == "z" else (me.y, peers.y)
        self.other_at, self.other_to = (me.y, peers.y) if first == "z" else (me.z, peers.z)
        self.r0, self.s1, self.r1, self.s2, self.r2, self.s3, self.r3, self.fin = bufs

    def half(self, core):
        return pl.ds(pl.multiple_of(self.base + core * CROSS, 128), CROSS)

    def start(self):
        self.c0 = self.net.send(self.big.at[self.half(1 - self.me.core)], self.r0, self.peers.mate)

    def over_first(self):
        self.c0.wait_recv()
        own = self.big[self.half(self.me.core)]
        self.s1[...] = added(own, [self.r0[...]], 1).astype(BF16).reshape(8, CHUNK, C)
        self.c1 = [
            self.net.send(self.s1.at[lax.rem(self.at + k, 8)], self.r1.at[k - 1], self.to[k - 1])
            for k in FAR_FIRST
        ]

    def over_x(self):
        for copy in self.c1:
            copy.wait_recv()
        self.s2[...] = added(self.s1[self.at], self.r1, 7).astype(BF16)
        x = self.me.x
        self.r2[x] = self.s2[...]
        self.c2 = [self.net.send(self.s2, self.r2.at[x], self.peers.x[k - 1]) for k in (2, 1, 3)]

    def over_other(self):
        for copy in self.c2:
            copy.wait_recv()
        total = added(self.r2[0], [self.r2[k] for k in range(1, NX)], NX - 1)
        self.s3[...] = total.astype(BF16)
        at = self.other_at
        self.r3[at] = self.s3[...]
        self.c3 = [self.net.send(self.s3, self.r3.at[at], self.other_to[k - 1]) for k in FAR_FIRST]

    def back_first(self):
        for copy in self.c3:
            copy.wait_recv()
        total = added(self.r3[0], [self.r3[k] for k in range(1, 8)], 7)
        core = self.me.core
        self.fin[core, self.at] = total.astype(BF16)
        mine = self.fin.at[core, self.at]
        self.c4 = [self.net.send(mine, mine, self.to[k - 1]) for k in FAR_FIRST]

    def back_core(self):
        for copy in self.c4:
            copy.wait_recv()
        mine = self.fin.at[self.me.core]
        self.c5 = self.net.send(mine, mine, self.peers.mate)

    def finish(self):
        self.c5.wait_recv()


class PlaneSum:
    def __init__(self, net, me, peers, big, bufs):
        self.net, self.me, self.peers, self.big = net, me, peers, big
        self.r0, self.s1, self.r1, self.s2, self.r2, self.s3, self.r3, self.fin = bufs

    def half(self, core):
        return pl.ds(pl.multiple_of(PLANE_AT + core * PLANE, 256), PLANE)

    def start(self):
        self.c0 = self.net.send(self.big.at[self.half(1 - self.me.core)], self.r0, self.peers.mate)

    def over_x(self):
        self.c0.wait_recv()
        own = self.big[self.half(self.me.core)]
        self.s1[...] = added(own, [self.r0[...]], 1).astype(BF16).reshape(NX, 64, C)
        x = self.me.x
        self.c1 = [
            self.net.send(self.s1.at[lax.rem(x + k, NX)], self.r1.at[k - 1], self.peers.x[k - 1])
            for k in (2, 1, 3)
        ]

    def over_y(self):
        for copy in self.c1:
            copy.wait_recv()
        total = added(self.s1[self.me.x], self.r1, NX - 1).astype(BF16)
        for t in range(NY):
            rows, cols = 16 * (t // 2), 128 * (t % 2)
            self.s2[t] = total[rows : rows + 16, cols : cols + 128]
        y = self.me.y
        self.c2 = [
            self.net.send(self.s2.at[lax.rem(y + k, NY)], self.r2.at[k - 1], self.peers.y[k - 1])
            for k in FAR_FIRST
        ]

    def over_z(self):
        for copy in self.c2:
            copy.wait_recv()
        self.s3[...] = added(self.s2[self.me.y], self.r2, NY - 1).astype(BF16)
        z = self.me.z
        self.r3[z] = self.s3[...]
        self.c3 = [self.net.send(self.s3, self.r3.at[z], self.peers.z[k - 1]) for k in FAR_FIRST]

    def back_y(self):
        for copy in self.c3:
            copy.wait_recv()
        me = self.me
        total = added(self.r3[0], [self.r3[k] for k in range(1, NZ)], NZ - 1)
        at = (lax.rem(me.y, 2), me.core, me.x, me.y // 2)
        self.fin[at] = total.astype(BF16)
        mine = self.fin.at[at]
        self.c4 = [self.net.send(mine, mine, self.peers.y[k - 1]) for k in FAR_FIRST]

    def back_x(self):
        for copy in self.c4:
            copy.wait_recv()
        self.c5 = []
        for k in (2, 1, 3):
            for half in range(2):
                mine = self.fin.at[half, self.me.core, self.me.x]
                self.c5.append(self.net.send(mine, mine, self.peers.x[k - 1]))

    def back_core(self):
        for copy in self.c5:
            copy.wait_recv()
        self.c6 = []
        for half in range(2):
            mine = self.fin.at[half, self.me.core]
            self.c6.append(self.net.send(mine, mine, self.peers.mate))

    def finish(self):
        for copy in self.c6:
            copy.wait_recv()


class SmallSum:
    def __init__(self, net, me, peers, small, bufs):
        self.net, self.me, self.peers, self.small = net, me, peers, small
        self.r0, self.s1, self.r1, self.s2, self.r2, self.s3, self.r3, self.fin = bufs

    def start(self):
        half = pl.ds(pl.multiple_of((1 - self.me.core) * 32, 32), 32)
        self.c0 = self.net.send(self.small.at[half], self.r0, self.peers.mate)

    def over_x(self):
        self.c0.wait_recv()
        own = self.small[pl.ds(pl.multiple_of(self.me.core * 32, 32), 32)]
        self.s1[...] = (own + self.r0[...]).reshape(NX, 8, C)
        x = self.me.x
        self.c1 = [
            self.net.send(self.s1.at[lax.rem(x + k, NX)], self.r1.at[k - 1], self.peers.x[k - 1])
            for k in (2, 1, 3)
        ]

    def over_y(self):
        for copy in self.c1:
            copy.wait_recv()
        self.s2[...] = added(self.s1[self.me.x], self.r1, NX - 1)
        y = self.me.y
        self.r2[y] = self.s2[...]
        self.c2 = [self.net.send(self.s2, self.r2.at[y], self.peers.y[k - 1]) for k in FAR_FIRST]

    def over_z(self):
        for copy in self.c2:
            copy.wait_recv()
        self.s3[...] = jnp.sum(self.r2[...], axis=0)
        z = self.me.z
        self.r3[z] = self.s3[...]
        self.c3 = [self.net.send(self.s3, self.r3.at[z], self.peers.z[k - 1]) for k in FAR_FIRST]

    def back_x(self):
        for copy in self.c3:
            copy.wait_recv()
        me = self.me
        self.fin[me.core, me.x] = jnp.sum(self.r3[...], axis=0)
        mine = self.fin.at[me.core, me.x]
        self.c4 = [self.net.send(mine, mine, self.peers.x[k - 1]) for k in (2, 1, 3)]

    def back_core(self):
        for copy in self.c4:
            copy.wait_recv()
        mine = self.fin.at[self.me.core]
        self.c5 = self.net.send(mine, mine, self.peers.mate)

    def finish(self):
        self.c5.wait_recv()


class Peers:
    def __init__(self, me):
        self.mate = me.at(core=1 - me.core)
        self.x = [me.at(x=lax.rem(me.x + k, NX)) for k in range(1, NX)]
        self.y = [me.at(y=lax.rem(me.y + k, NY)) for k in range(1, NY)]
        self.z = [me.at(z=lax.rem(me.z + k, NZ)) for k in range(1, NZ)]

    def all(self):
        return [self.mate] + self.x + self.y + self.z


SUM_COPIES = (1 + 3 + 7 + 7 + 7 + 6 + 2) + 2 * (1 + 7 + 3 + 7 + 7 + 1) + (1 + 3 + 7 + 7 + 3 + 1)


def sum_scratch():
    cross = [
        pltpu.VMEM((CROSS, C), BF16),
        pltpu.VMEM((8, CHUNK, C), BF16),
        pltpu.VMEM((7, CHUNK, C), BF16),
        pltpu.VMEM((CHUNK, C), BF16),
        pltpu.VMEM((NX, CHUNK, C), BF16),
        pltpu.VMEM((CHUNK, C), BF16),
        pltpu.VMEM((8, CHUNK, C), BF16),
    ]
    return cross * 2 + [
        pltpu.VMEM((PLANE, C), BF16),
        pltpu.VMEM((NX, 64, C), BF16),
        pltpu.VMEM((NX - 1, 64, C), BF16),
        pltpu.VMEM((NY, 16, 128), BF16),
        pltpu.VMEM((NY - 1, 16, 128), BF16),
        pltpu.VMEM((16, 128), BF16),
        pltpu.VMEM((NZ, 16, 128), BF16),
        pltpu.VMEM((32, C), F32),
        pltpu.VMEM((NX, 8, C), F32),
        pltpu.VMEM((NX - 1, 8, C), F32),
        pltpu.VMEM((8, C), F32),
        pltpu.VMEM((NY, 8, C), F32),
        pltpu.VMEM((8, C), F32),
        pltpu.VMEM((NZ, 8, C), F32),
    ]


def sum_sums(by_z, plane, by_y, smalls):
    plane.over_y()
    smalls.over_x()
    by_z.over_x()
    by_y.over_x()
    smalls.over_y()
    smalls.net.settle(20)
    plane.over_z()
    by_z.over_other()
    by_y.over_other()
    smalls.over_z()
    plane.back_y()
    by_z.back_first()
    by_y.back_first()
    smalls.back_x()
    plane.back_x()
    smalls.net.settle(30)
    by_z.back_core()
    smalls.back_core()
    by_y.back_core()
    smalls.net.settle(12)
    plane.back_core()
    smalls.finish()
    by_z.finish()
    by_y.finish()
    plane.finish()


def shared_scratch():
    return [
        pltpu.SMEM((8, 16), jnp.int32),
        pltpu.SMEM((8, 16), jnp.int32),
        pltpu.VMEM((S, S, C), BF16),
        pltpu.VMEM((S, S, C), F32),
        pltpu.VMEM((ROWS, PITCH, C), F32),
        pltpu.VMEM((7, ROWS, S, C), F32),
        pltpu.VMEM((7, S, 8, C), F32),
        pltpu.VMEM((4, 3, S, C), BF16),
        pltpu.VMEM((4, 16, C), F32),
        pltpu.VMEM((C, HID), F32),
        pltpu.VMEM((C, HID), F32),
        pltpu.VMEM((49, 8, C), F32),
        pltpu.VMEM((8, C), F32),
        pltpu.VMEM((2 * HID, C), BF16),
        pltpu.VMEM((64, C), F32),
    ]


def split_refs(refs, *lists):
    refs = list(refs)
    parts = []
    for scratch in lists:
        parts.append(refs[: len(scratch)])
        refs = refs[len(scratch) :]
    return parts + [refs]


def block_kernel(
    ids_in, codes_in, x_in, cot_in, taps_in, gain_in, layer_in, w_in_in, w_out_in,
    fin_z, fin_plane, fin_y, fin_small, *rest,
):
    shared, weights, rims, inner, outer, sums, sems = split_refs(
        rest, shared_scratch(), weight_scratch(), rim_scratch(), inside_scratch(),
        border_scratch(), sum_scratch(),
    )
    ids, codes, xb, xf, fr, fb, fs, sides, corners, gacc, iacc, kg, gain_acc, big, small = shared
    ss, rs, ls = sems
    w = Weights(weights)
    me = Place()
    peers = Peers(me)
    along_y, along_x = rim_partners(me)
    partners = peers.all() + along_y

    barrier = pltpu.get_barrier_semaphore()
    for device in partners:
        pl.semaphore_signal(barrier, inc=1, device_id=device, device_id_type=MESH)
    loads = [
        pltpu.make_async_copy(src, dst, ls.at[i])
        for i, (src, dst) in enumerate(
            (
                (x_in, xb), (ids_in, ids), (codes_in, codes), (taps_in, w.taps_in),
                (gain_in, w.gain), (layer_in, w.layer), (w_in_in, w.w_in), (w_out_in, w.w_out),
                (cot_in, w.cot),
            )
        )
    ]
    for load in loads:
        load.start()
    loads[0].wait()
    own_strips(xb, xf, rims[0], rims[6], me)
    pl.semaphore_wait(barrier, len(partners))

    net = Copies(ss, rs)
    by_y, by_x = both_rims(net, me, ids, codes, along_y, along_x, rims[:6], rims[6:])
    by_y.gather()
    by_x.gather()
    for load in loads[1:]:
        load.wait()

    inside = Inside(w, fb, inner)
    border = Border(w, fb, fs, outer)
    frame_inside(xf, fr)
    shift_rows(fr, fb, 3, S)
    w.taps[...] = w.taps_in[...].astype(F32)
    inside.depthwise()
    w.w_out_t[...] = w.w_out[...].T
    w.w_in_t[...] = w.w_in[...].T
    inside.norm()
    by_x.choose()
    border.cotangent()
    border.hidden_grad()
    for h in range(3):
        inside.hidden(h, gacc, iacc)
    by_y.choose()
    for h in range(3, 4):
        inside.hidden(h, gacc, iacc)
    inside.backward(gain_acc)
    kg[...] = jnp.zeros_like(kg)
    inside.kernel_grad(kg)

    for rim, chans in ((by_y, slice(0, HALF)), (by_x, slice(HALF, C))):
        rim.take(sides, corners, chans, me.space)
        frame_rims(sides, corners, fr, chans)
        shift_rows(fr, fb, 0, 9, chans)
        shift_rows(fr, fb, S - 3, 9, chans)
        shift_sides(fr, fs, chans)
        border.depthwise(chans)
    border.norm()
    border.hidden()
    sum_z = CrossSum(net, me, peers, big, 0, "z", sums[0:7] + [fin_z])
    sum_y = CrossSum(net, me, peers, big, PLANE_AT + 2 * PLANE, "y", sums[7:14] + [fin_y])
    plane = PlaneSum(net, me, peers, big, sums[14:21] + [fin_plane])
    smalls = SmallSum(net, me, peers, small, sums[21:28] + [fin_small])
    scale = border.out_grad(gacc, big)
    sum_z.start()
    border.in_grad(iacc, big)
    plane.start()
    sum_y.start()
    border.scaled_grad()
    sum_z.over_first()
    plane.over_x()
    sum_y.over_first()
    gain = border.backward(gain_acc)
    border.kernel_grad(kg)
    small[0:49] = jnp.sum(kg[...], axis=1)
    small[49:50] = gain
    small[50:51] = scale
    small[51:64] = jnp.zeros((13, C), F32)
    smalls.start()
    sum_sums(sum_z, plane, sum_y, smalls)
    net.finish()


def block_grads(neighbours, codes, tile, cot, kernel, ln_gain, layer_scale, w_in, w_out):
    vmem = pl.BlockSpec(memory_space=pltpu.VMEM)
    copies = RIM_COPIES + SUM_COPIES
    return pl.pallas_call(
        block_kernel,
        out_shape=(
            pltpu.VMEM((2, NZ, CHUNK, C), BF16),
            pltpu.VMEM((2, 2, NX, 4, 16, 128), BF16),
            pltpu.VMEM((2, NY, CHUNK, C), BF16),
            pltpu.VMEM((2, NX, 8, C), F32),
        ),
        in_specs=[pl.BlockSpec(memory_space=pl.ANY)] * 9,
        out_specs=(vmem,) * 4,
        scratch_shapes=shared_scratch() + weight_scratch() + rim_scratch() + inside_scratch()
        + border_scratch() + sum_scratch()
        + [pltpu.SemaphoreType.DMA((copies,))] * 2 + [pltpu.SemaphoreType.DMA((9,))],
        compiler_params=pltpu.CompilerParams(
            collective_id=0, has_side_effects=True, vmem_limit_bytes=60 * 2**20
        ),
    )(
        neighbours, codes, tile, cot, kernel, ln_gain.reshape(1, C), layer_scale.reshape(1, C),
        w_in, w_out,
    )


def hand_over_kernel(
    fin_z, fin_plane, fin_y, small, kg_out, gain_out, scale_out, in_out, out_out, kg, gain, scale, sems
):
    def move(pairs, first):
        copies = [
            pltpu.make_async_copy(src, dst, sems.at[first + i])
            for i, (src, dst) in enumerate(pairs)
        ]
        for copy in copies:
            copy.start()
        return copies

    rest = HID - PLANE_AT
    parts = [(fin_z, out_out.at[pl.ds(0, PLANE_AT)])]
    for q in range(1, HID // C):
        parts.append((fin_y.at[pl.ds(256 * (q - 1), 256)], in_out.at[:, pl.ds(256 * q, 256)]))
    for half in range(2):
        cols = pl.ds(128 * half, 128)
        parts.append((fin_plane.at[half, pl.ds(0, rest)], out_out.at[pl.ds(PLANE_AT, rest), cols]))
        parts.append((fin_plane.at[half, pl.ds(rest, C)], in_out.at[:, cols]))
    copies = move(parts, 0)
    kg[...] = small[0:49]
    gain[...] = small[49:50]
    scale[...] = small[50:51]
    copies += move([(kg, kg_out), (gain, gain_out), (scale, scale_out)], len(parts))
    for copy in copies:
        copy.wait()


def hand_over(fin_z, fin_plane, fin_y, fin_small):
    fins = (
        fin_z.reshape(2 * CROSS, C),
        fin_plane.reshape(2, 2 * PLANE, 128),
        fin_y.reshape(2 * CROSS, C),
        fin_small.reshape(64, C),
    )
    return pl.pallas_call(
        hand_over_kernel,
        out_shape=(
            jax.ShapeDtypeStruct((49, C), F32),
            jax.ShapeDtypeStruct((1, C), F32),
            jax.ShapeDtypeStruct((1, C), F32),
            jax.ShapeDtypeStruct((C, HID), BF16),
            jax.ShapeDtypeStruct((HID, C), BF16),
        ),
        in_specs=[pl.BlockSpec(memory_space=pltpu.VMEM)] * 4,
        out_specs=(pl.BlockSpec(memory_space=pl.ANY),) * 5,
        scratch_shapes=[
            pltpu.VMEM((49, C), F32),
            pltpu.VMEM((1, C), F32),
            pltpu.VMEM((1, C), F32),
            pltpu.SemaphoreType.DMA((11,)),
        ],
        compiler_params=pltpu.CompilerParams(has_side_effects=True),
    )(*[pltpu.with_memory_space_constraint(fin, pltpu.VMEM) for fin in fins])


def on_device(state, cotangent, kernel, ln_gain, w_in, w_out, layer_scale, neighbours, codes):
    sums = block_grads(
        neighbours.T, codes.T, state.reshape(S, S, C), cotangent.reshape(PIX, C), kernel, ln_gain,
        layer_scale, w_in, w_out,
    )
    kernel_grad, gain_grad, scale_grad, in_grad, out_grad = hand_over(*sums)
    return (kernel_grad, gain_grad.reshape(C), scale_grad.reshape(C), in_grad, out_grad)


def solution(mesh):
    placed = (P("dp", "space", None, None, None),) * 2 + (P(),) * 7
    return jax.shard_map(
        on_device, mesh=mesh, in_specs=placed, out_specs=(P(),) * 5, check_vma=False
    )
```

```python
import jax
import jax.numpy as jnp
from jax import lax
from jax.experimental import pallas as pl
from jax.experimental.pallas import tpu as pltpu
from jax.sharding import PartitionSpec as P

EPSILON = 1e-06
MESH = pl.DeviceIdType.MESH
F32 = jnp.float32
BF16 = jnp.bfloat16

CORES, NX, NY_LO, NY_HI, NZ = 2, 4, 4, 2, 8
NY = NY_LO * NY_HI

S = 32
C = 256
HID = 1024
PIX = S * S
PITCH = 40
ROWS = 38


class Place:
    def __init__(self):
        dp = lax.axis_index("dp")
        space = lax.axis_index("space")
        self.core = lax.rem(dp, CORES)
        self.y_hi = lax.rem(dp // CORES, NY_HI)
        self.z = dp // (CORES * NY_HI)
        self.x = lax.rem(space, NX)
        self.y_lo = space // NX
        self.y = self.y_hi * NY_LO + self.y_lo
        self.dp = dp
        self.space = space

    def at(self, core=None, x=None, y=None, z=None):
        core = self.core if core is None else core
        x = self.x if x is None else x
        y = self.y if y is None else y
        z = self.z if z is None else z
        dp = (z * NY_HI + y // NY_LO) * CORES + core
        return {"dp": dp, "space": lax.rem(y, NY_LO) * NX + x}


def greet(devices):
    barrier = pltpu.get_barrier_semaphore()
    for device in devices:
        pl.semaphore_signal(barrier, inc=1, device_id=device, device_id_type=MESH)
    pl.semaphore_wait(barrier, len(devices))


class Copies:
    def __init__(self, send_sems, recv_sems):
        self.send_sems = send_sems
        self.recv_sems = recv_sems
        self.used = 0
        self.started = []

    def send(self, src, dst, device):
        copy = pltpu.make_async_remote_copy(
            src_ref=src,
            dst_ref=dst,
            send_sem=self.send_sems.at[self.used],
            recv_sem=self.recv_sems.at[self.used],
            device_id=device,
            device_id_type=MESH,
        )
        copy.start()
        self.used += 1
        self.started.append(copy)
        return copy

    def settle(self, keep):
        at = len(self.started) - keep
        for copy in self.started[:at]:
            copy.wait_send()
        self.started = self.started[at:]

    def finish(self):
        self.settle(0)


HALF = C // 2


def own_strips(x_ref, xf, gath_y, gath_x, me):
    turn = reversal()
    xf[...] = x_ref[...].astype(F32)

    def put(side, r, rows):
        gath_y[me.y_lo, side, r] = rows[:, :HALF]
        gath_x[me.x, side, r] = rows[:, HALF:]

    for r in range(3):
        put(0, r, x_ref[r])
        put(2, r, flip(turn, x_ref[S - 1 - r]))
        put(1, r, xf[:, S - 1 - r, :].astype(BF16))
        put(3, r, flip(turn, xf[:, r, :].astype(BF16)))


class Rims:
    def __init__(self, net, ids, codes, gath, out_s, out_c, in_s, in_c, cf, gather_at, choose_at, gather_to, choose_to, tile_at, split):
        self.net = net
        self.ids, self.codes = ids, codes
        self.gath, self.out_s, self.out_c, self.in_s, self.in_c, self.cf = gath, out_s, out_c, in_s, in_c, cf
        self.gather_at, self.choose_at = gather_at, choose_at
        self.gather_to, self.choose_to = gather_to, choose_to
        self.tile_at, self.split = tile_at, split

    def gather(self):
        at = self.gather_at
        self.first = [
            self.net.send(self.gath.at[at], self.gath.at[at], self.gather_to[k - 1])
            for k in (2, 1, 3)
        ]

    def choose(self):
        for copy in self.first:
            copy.wait_recv()
        self.second = []
        at = self.choose_at
        for k in (2, 1, 3, 0):
            target = self.tile_at(lax.rem(at + k, 4))
            for s in range(8):
                row, _ = self.split(jnp.maximum(self.ids[s, target], 0))
                e = self.codes[s, target]
                if s < 4:
                    piece = self.gath[row, e]
                    if k:
                        self.out_s[k - 1, s] = piece
                    else:
                        self.in_s[at, s] = piece
                else:
                    piece = self.gath[row, e, :, 0:16, :].astype(F32)
                    for r in range(3):
                        self.cf[pl.ds(12 * (s - 4) + 4 * r, 4), :] = piece[r, 0:4]
            packed = self.cf[...].astype(BF16)
            if k:
                self.out_c[k - 1] = packed
                to = self.choose_to[k - 1]
                self.second.append(self.net.send(self.out_s.at[k - 1], self.in_s.at[at], to))
                self.second.append(self.net.send(self.out_c.at[k - 1], self.in_c.at[at], to))
            else:
                self.in_c[at] = packed

    def take(self, sides, corners, chans, space):
        for copy in self.second:
            copy.wait_recv()
        for s in range(8):
            n = self.ids[s, space]
            _, col = self.split(jnp.maximum(n, 0))
            if s < 4:
                sides[s, :, :, chans] = self.in_s[col, s]
            else:
                at = 12 * (s - 4)
                piece = self.in_c[col].astype(F32)[at : at + 12]
                corners[s - 4, 0:12, chans] = jnp.where(n >= 0, piece, jnp.zeros_like(piece))


def both_rims(net, me, ids, codes, along_y, along_x, bufs_y, bufs_x):
    by_y = Rims(
        net, ids, codes, *bufs_y, me.y_lo, me.x, along_y, along_x,
        lambda x: me.y_lo * NX + x, lambda n: (n // NX, lax.rem(n, NX)),
    )
    by_x = Rims(
        net, ids, codes, *bufs_x, me.x, me.y_lo, along_x, along_y,
        lambda y: y * NX + me.x, lambda n: (lax.rem(n, NX), n // NX),
    )
    return by_y, by_x


def rim_partners(me):
    base = me.y_hi * NY_LO
    along_y = [me.at(y=base + lax.rem(me.y_lo + k, NY_LO)) for k in range(1, NY_LO)]
    along_x = [me.at(x=lax.rem(me.x + k, NX)) for k in range(1, NX)]
    return along_y, along_x


RIM_COPIES = 2 * 9


def rim_scratch():
    half = [
        pltpu.VMEM((4, 4, 3, S, HALF), BF16),
        pltpu.VMEM((3, 4, 3, S, HALF), BF16),
        pltpu.VMEM((3, 48, HALF), BF16),
        pltpu.VMEM((4, 4, 3, S, HALF), BF16),
        pltpu.VMEM((4, 48, HALF), BF16),
        pltpu.VMEM((48, HALF), F32),
    ]
    return half * 2


def reversal():
    row = lax.broadcasted_iota(jnp.int32, (S, S), 0)
    col = lax.broadcasted_iota(jnp.int32, (S, S), 1)
    return jnp.where(row + col == S - 1, 1.0, 0.0).astype(BF16)


def flip(turn, rows):
    return jnp.dot(turn, rows, preferred_element_type=F32).astype(rows.dtype)


INNER = S - 6
NORM_ROWS = 13
NORM_PIX = NORM_ROWS * S
ACT_ROWS = 208
IN_PIX = INNER * S
IN_PAD = 896
EDGE = 3 * S
SIDE_AT = 2 * EDGE
OUT_PIX = SIDE_AT + INNER * 8
OUT_PAD = 512


def frame_inside(xf, fr):
    fr[...] = jnp.zeros_like(fr)

    def one_row(i, carry):
        fr[3 + i, 3 : 3 + S, :] = xf[i]
        return carry

    lax.fori_loop(0, S, one_row, 0)


def frame_rims(sides, cf, fr, chans):
    turn = reversal()
    for r in range(3):
        fr[r, 3 : 3 + S, chans] = flip(turn, sides[0, 2 - r, :, chans]).astype(F32)
        fr[3 : 3 + S, 35 + r, chans] = flip(turn, sides[1, r, :, chans]).astype(F32)
        fr[35 + r, 3 : 3 + S, chans] = sides[2, r, :, chans].astype(F32)
        fr[3 : 3 + S, r, chans] = sides[3, 2 - r, :, chans].astype(F32)
    for i in range(3):
        for j in range(3):
            fr[i, j, chans] = cf[0, 4 * (2 - i) + 2 - j, chans]
            fr[i, 35 + j, chans] = cf[1, 4 * j + 2 - i, chans]
            fr[35 + i, 35 + j, chans] = cf[2, 4 * i + j, chans]
            fr[35 + i, j, chans] = cf[3, 4 * (2 - j) + i, chans]


def shift_rows(fr, fb, first, count, chans=slice(0, C)):
    def one_row(i, carry):
        for b in range(7):
            fb[b, first + i, :, chans] = fr[first + i, b : b + S, chans]
        return carry

    lax.fori_loop(0, count, one_row, 0, unroll=3 if count % 3 == 0 else 4)


def shift_sides(fr, fs, chans):
    fs[:, :, :, chans] = jnp.zeros((7, S, 8, HALF), F32)

    def one_row(i, carry):
        for b in range(7):
            fs[b, i, 0:3, chans] = fr[3 + i, b : b + 3, chans]
            fs[b, i, 3:6, chans] = fr[3 + i, 29 + b : 32 + b, chans]
        return carry

    lax.fori_loop(0, S, one_row, 0, unroll=4)


def lanes(g):
    return (
        pl.ds(pl.multiple_of((g // 2) * 8, 8), 8),
        pl.ds(pl.multiple_of(lax.rem(g, 2) * 128, 128), 128),
    )


def convolve(load, taps, chans, count, put):
    acc = [None] * count
    for b in range(7):
        k = [jnp.broadcast_to(taps[pl.ds(7 * a + b, 1), chans], (8, 128)) for a in range(7)]
        for i in range(count + 6):
            f = load(b, i)
            for a in range(7):
                at = i - a
                if 0 <= at < count:
                    term = f * k[a]
                    acc[at] = term if acc[at] is None else acc[at] + term
    for i in range(count):
        put(i, acc[i])


def correlate(load, d, kg, chans):
    count = len(d)
    for b in range(7):
        acc = [None] * 7
        for i in range(count + 6):
            f = load(b, i)
            for a in range(7):
                at = i - a
                if 0 <= at < count:
                    term = f * d[at]
                    acc[a] = term if acc[a] is None else acc[a] + term
        for a in range(7):
            kg[7 * a + b, :, chans] += acc[a]


def normalise(v):
    mean = jnp.mean(v, axis=-1, keepdims=True)
    v = v - mean
    inverse = lax.rsqrt(jnp.mean(v * v, axis=-1, keepdims=True) + EPSILON)
    return v * inverse, inverse


def norm_backward(sg, normed, inverse, gain):
    g = sg * gain
    mean = jnp.mean(g, axis=-1, keepdims=True)
    along = jnp.mean(g * normed, axis=-1, keepdims=True)
    return (g - mean - normed * along) * jnp.concatenate([inverse, inverse], axis=1)


def gelu_and_slope(v):
    root = 0.7978845608028654
    square = v * v
    inner = v * (root + (root * 0.044715) * square)
    t = jnp.tanh(inner)
    half = 0.5 + 0.5 * t
    value = v * half
    slope = half + value * (1.0 - half) * (2.0 * root + (6.0 * root * 0.044715) * square)
    return value, slope


def dot(left, right):
    return jnp.dot(left, right, preferred_element_type=F32)


class Inside:
    def __init__(self, w, fb, bufs):
        self.w, self.fb = w, fb
        (self.normed, self.inv, self.scaled, self.cot, self.branch, self.scaled_t, self.cot_t,
         self.pre, self.hg, self.hid, self.pg, self.sg) = bufs

    def depthwise(self):
        def step(g, carry):
            cols, chans = lanes(g)

            def put(i, value):
                self.normed[i, cols, chans] = value

            convolve(lambda b, i: self.fb[b, 3 + i, cols, chans], self.w.taps, chans, INNER, put)
            return carry

        lax.fori_loop(0, 8, step, 0)

    def norm(self):
        w = self.w
        col = lax.rem(lax.broadcasted_iota(jnp.int32, (S, C), 0), S)
        here = ((col >= 3) & (col < S - 3))[None]

        def step(q, carry):
            rows = pl.ds(q * NORM_ROWS, NORM_ROWS)
            flat = pl.ds(pl.multiple_of(q * NORM_PIX, 32), NORM_PIX)
            normed, inverse = normalise(self.normed[rows].reshape(NORM_PIX, C))
            self.inv[flat] = jnp.broadcast_to(inverse, (NORM_PIX, 128))
            self.normed[rows] = normed.reshape(NORM_ROWS, S, C)
            self.scaled[flat] = (normed * w.gain[...]).astype(BF16)
            cot = w.cot[pl.ds(pl.multiple_of(3 * S + q * NORM_PIX, 32), NORM_PIX)].astype(F32)
            cot = cot.reshape(NORM_ROWS, S, C)
            cot = jnp.where(here, cot, jnp.zeros_like(cot)).reshape(NORM_PIX, C)
            self.cot[flat] = cot.astype(BF16)
            self.branch[flat] = (cot * w.layer[...]).astype(BF16)
            return carry

        lax.fori_loop(0, INNER // NORM_ROWS, step, 0)
        rest = slice(IN_PIX, IN_PAD)
        none = jnp.zeros((IN_PAD - IN_PIX, C), BF16)
        self.scaled[rest] = none
        self.cot[rest] = none
        self.hid[rest] = none
        for h in range(4):
            self.pg[rest, 256 * h : 256 * h + 256] = none
        self.scaled_t[...] = self.scaled[...].T
        self.cot_t[...] = self.cot[...].T

    def hidden(self, h, gacc, iacc):
        w = self.w
        part = slice(256 * h, 256 * h + 256)
        self.pre[...] = dot(self.scaled[0:IN_PIX], w.w_in[:, part])
        self.hg[...] = dot(self.branch[...], w.w_out_t[:, part])

        def act(q, carry):
            rows = pl.ds(pl.multiple_of(q * ACT_ROWS, 16), ACT_ROWS)
            value, slope = gelu_and_slope(self.pre[rows])
            self.hid[rows] = value.astype(BF16)
            self.pg[rows, part] = (self.hg[rows] * slope).astype(BF16)
            return carry

        lax.fori_loop(0, IN_PIX // ACT_ROWS, act, 0)
        gacc[:, part] = dot(self.cot_t[...], self.hid[...])
        iacc[:, part] = dot(self.scaled_t[...], self.pg[:, part])

    def backward(self, gain_acc):
        w = self.w
        self.sg[...] = dot(self.pg[0:IN_PIX], w.w_in_t[...])

        def step(q, total):
            rows = pl.ds(q * NORM_ROWS, NORM_ROWS)
            flat = pl.ds(pl.multiple_of(q * NORM_PIX, 32), NORM_PIX)
            normed = self.normed[rows].reshape(NORM_PIX, C)
            sg = self.sg[flat]
            grad = norm_backward(sg, normed, self.inv[flat], w.gain[...])
            self.normed[rows] = grad.reshape(NORM_ROWS, S, C)
            return total + jnp.sum((sg * normed).reshape(NORM_PIX // 8, 8, C), axis=0)

        gain_acc[...] = lax.fori_loop(0, INNER // NORM_ROWS, step, jnp.zeros((8, C), F32))

    def kernel_grad(self, kg):
        def step(g, carry):
            cols, chans = lanes(g)
            d = [self.normed[i, cols, chans] for i in range(INNER)]
            correlate(lambda b, i: self.fb[b, 3 + i, cols, chans], d, kg, chans)
            return carry

        lax.fori_loop(0, 8, step, 0)


class Border:
    def __init__(self, w, fb, fs, bufs):
        self.w, self.fb, self.fs = w, fb, fs
        (self.normed, self.inv, self.scaled, self.cot, self.branch, self.scaled_t, self.cot_t,
         self.pre, self.hg, self.hid, self.pg, self.sg, self.cf) = bufs

    def cotangent(self):
        w = self.w
        self.cf[...] = jnp.zeros_like(self.cf)
        self.cf[0:EDGE] = w.cot[0:EDGE].astype(F32)
        self.cf[EDGE : 2 * EDGE] = w.cot[PIX - EDGE : PIX].astype(F32)
        for i in range(INNER):
            row = w.cot[(3 + i) * S : (4 + i) * S].astype(F32)
            at = SIDE_AT + 8 * i
            self.cf[at : at + 3] = row[0:3]
            self.cf[at + 3 : at + 6] = row[29:32]
        self.cot[...] = self.cf[...].astype(BF16)
        self.branch[...] = (self.cf[...] * w.layer[...]).astype(BF16)
        self.cot_t[...] = self.cot[...].T
        rest = slice(OUT_PIX, OUT_PAD)
        none = jnp.zeros((OUT_PAD - OUT_PIX, C), BF16)
        self.scaled[rest] = none
        for h in range(4):
            self.hid[rest, 256 * h : 256 * h + 256] = none
            self.pg[rest, 256 * h : 256 * h + 256] = none

    def depthwise(self, chans):
        def put_side(i, value):
            self.normed[SIDE_AT + 8 * i : SIDE_AT + 8 * i + 8, chans] = value

        convolve(lambda b, i: self.fs[b, i, :, chans], self.w.taps, chans, INNER, put_side)
        for first, at in ((0, 0), (S - 3, EDGE)):
            for j in range(0, S, 8):

                def put(i, value):
                    self.normed[at + S * i + j : at + S * i + j + 8, chans] = value

                convolve(
                    lambda b, i: self.fb[b, first + i, j : j + 8, chans],
                    self.w.taps, chans, 3, put,
                )

    def norm(self):
        w = self.w
        for at in range(0, OUT_PIX, 80):
            rows = slice(at, at + 80)
            normed, inverse = normalise(self.normed[rows])
            self.inv[rows] = jnp.broadcast_to(inverse, (80, 128))
            self.normed[rows] = normed
            self.scaled[rows] = (normed * w.gain[...]).astype(BF16)
        self.scaled_t[...] = self.scaled[...].T

    def hidden_grad(self):
        for h in range(4):
            part = slice(256 * h, 256 * h + 256)
            self.hg[h] = dot(self.branch[0:OUT_PIX], self.w.w_out_t[:, part])

    def products(self, h):
        part = slice(256 * h, 256 * h + 256)
        self.pre[h % 2] = dot(self.scaled[0:OUT_PIX], self.w.w_in[:, part])

    def hidden(self):
        self.products(0)
        for h in range(4):
            if h < 3:
                self.products(h + 1)
            part = slice(256 * h, 256 * h + 256)
            for at in range(0, OUT_PIX, 16):
                rows = slice(at, at + 16)
                value, slope = gelu_and_slope(self.pre[h % 2, rows])
                self.hid[rows, part] = value.astype(BF16)
                self.pg[rows, part] = (self.hg[h, rows] * slope).astype(BF16)

    def out_grad(self, gacc, big):
        w = self.w
        scale = jnp.zeros((1, C), F32)
        for h in range(4):
            part = slice(256 * h, 256 * h + 256)
            g = (gacc[:, part] + dot(self.cot_t[...], self.hid[:, part])).T
            big[part] = (g * w.layer[...]).astype(BF16)
            scale += jnp.sum(g * w.w_out[part].astype(F32), axis=0, keepdims=True)
        return scale

    def in_grad(self, iacc, big):
        for h in range(4):
            part = slice(256 * h, 256 * h + 256)
            total = iacc[:, part] + dot(self.scaled_t[...], self.pg[:, part])
            big[HID + 256 * h : HID + 256 * h + 256] = total.astype(BF16)

    def scaled_grad(self):
        self.sg[...] = dot(self.pg[0:OUT_PIX], self.w.w_in_t[...])

    def backward(self, gain_acc):
        total = gain_acc[...]
        for at in range(0, OUT_PIX, 80):
            rows = slice(at, at + 80)
            normed = self.normed[rows]
            sg = self.sg[rows]
            total += jnp.sum((sg * normed).reshape(10, 8, C), axis=0)
            self.normed[rows] = norm_backward(sg, normed, self.inv[rows], self.w.gain[...])
        return jnp.sum(total, axis=0, keepdims=True)

    def kernel_grad(self, kg):
        for chans in (slice(0, 128), slice(128, 256)):
            d = [self.normed[SIDE_AT + 8 * i : SIDE_AT + 8 * i + 8, chans] for i in range(INNER)]
            correlate(lambda b, i: self.fs[b, i, :, chans], d, kg, chans)
            for b in range(7):
                acc = [None] * 7
                for first, at in ((0, 0), (S - 3, EDGE)):
                    for j in range(0, S, 8):
                        d = [
                            self.normed[at + S * i + j : at + S * i + j + 8, chans]
                            for i in range(3)
                        ]
                        for i in range(9):
                            f = self.fb[b, first + i, j : j + 8, chans]
                            for a in range(7):
                                if 0 <= i - a < 3:
                                    term = f * d[i - a]
                                    acc[a] = term if acc[a] is None else acc[a] + term
                for a in range(7):
                    kg[7 * a + b, :, chans] += acc[a]


class Weights:
    def __init__(self, bufs):
        (self.taps, self.taps_in, self.gain, self.layer, self.w_in, self.w_in_t, self.w_out,
         self.w_out_t, self.cot) = bufs


def weight_scratch():
    return [
        pltpu.VMEM((49, C), F32),
        pltpu.VMEM((49, C), BF16),
        pltpu.VMEM((1, C), F32),
        pltpu.VMEM((1, C), F32),
        pltpu.VMEM((C, HID), BF16),
        pltpu.VMEM((HID, C), BF16),
        pltpu.VMEM((HID, C), BF16),
        pltpu.VMEM((C, HID), BF16),
        pltpu.VMEM((PIX, C), BF16),
    ]


def inside_scratch():
    return [
        pltpu.VMEM((INNER, S, C), F32),
        pltpu.VMEM((IN_PIX, 128), F32),
        pltpu.VMEM((IN_PAD, C), BF16),
        pltpu.VMEM((IN_PAD, C), BF16),
        pltpu.VMEM((IN_PIX, C), BF16),
        pltpu.VMEM((C, IN_PAD), BF16),
        pltpu.VMEM((C, IN_PAD), BF16),
        pltpu.VMEM((IN_PIX, 256), F32),
        pltpu.VMEM((IN_PIX, 256), F32),
        pltpu.VMEM((IN_PAD, 256), BF16),
        pltpu.VMEM((IN_PAD, HID), BF16),
        pltpu.VMEM((IN_PIX, C), F32),
    ]


def border_scratch():
    return [
        pltpu.VMEM((OUT_PIX, C), F32),
        pltpu.VMEM((OUT_PIX, 128), F32),
        pltpu.VMEM((OUT_PAD, C), BF16),
        pltpu.VMEM((OUT_PAD, C), BF16),
        pltpu.VMEM((OUT_PAD, C), BF16),
        pltpu.VMEM((C, OUT_PAD), BF16),
        pltpu.VMEM((C, OUT_PAD), BF16),
        pltpu.VMEM((2, OUT_PIX, 256), F32),
        pltpu.VMEM((4, OUT_PIX, 256), F32),
        pltpu.VMEM((OUT_PAD, HID), BF16),
        pltpu.VMEM((OUT_PAD, HID), BF16),
        pltpu.VMEM((OUT_PIX, C), F32),
        pltpu.VMEM((OUT_PAD, C), F32),
    ]


FAR_FIRST = (4, 3, 5, 2, 6, 1, 7)


def added(first, rest, count):
    total = first.astype(F32)
    for k in range(count):
        total += rest[k].astype(F32)
    return total


CROSS = 384
CHUNK = CROSS // 8
PLANE = 256
PLANE_AT = 2 * CROSS


class CrossSum:
    def __init__(self, net, me, peers, big, base, first, bufs):
        self.net, self.me, self.big, self.base = net, me, big, base
        self.peers = peers
        self.at, self.to = (me.z, peers.z) if first == "z" else (me.y, peers.y)
        self.other_at, self.other_to = (me.y, peers.y) if first == "z" else (me.z, peers.z)
        self.r0, self.s1, self.r1, self.s2, self.r2, self.s3, self.r3, self.fin = bufs

    def half(self, core):
        return pl.ds(pl.multiple_of(self.base + core * CROSS, 128), CROSS)

    def start(self):
        self.c0 = self.net.send(self.big.at[self.half(1 - self.me.core)], self.r0, self.peers.mate)

    def over_first(self):
        self.c0.wait_recv()
        own = self.big[self.half(self.me.core)]
        self.s1[...] = added(own, [self.r0[...]], 1).astype(BF16).reshape(8, CHUNK, C)
        self.c1 = [
            self.net.send(self.s1.at[lax.rem(self.at + k, 8)], self.r1.at[k - 1], self.to[k - 1])
            for k in FAR_FIRST
        ]

    def over_x(self):
        for copy in self.c1:
            copy.wait_recv()
        self.s2[...] = added(self.s1[self.at], self.r1, 7).astype(BF16)
        x = self.me.x
        self.r2[x] = self.s2[...]
        self.c2 = [self.net.send(self.s2, self.r2.at[x], self.peers.x[k - 1]) for k in (2, 1, 3)]

    def over_other(self):
        for copy in self.c2:
            copy.wait_recv()
        total = added(self.r2[0], [self.r2[k] for k in range(1, NX)], NX - 1)
        self.s3[...] = total.astype(BF16)
        at = self.other_at
        self.r3[at] = self.s3[...]
        self.c3 = [self.net.send(self.s3, self.r3.at[at], self.other_to[k - 1]) for k in FAR_FIRST]

    def back_first(self):
        for copy in self.c3:
            copy.wait_recv()
        total = added(self.r3[0], [self.r3[k] for k in range(1, 8)], 7)
        core = self.me.core
        self.fin[core, self.at] = total.astype(BF16)
        mine = self.fin.at[core, self.at]
        self.c4 = [self.net.send(mine, mine, self.to[k - 1]) for k in FAR_FIRST]

    def back_core(self):
        for copy in self.c4:
            copy.wait_recv()
        mine = self.fin.at[self.me.core]
        self.c5 = self.net.send(mine, mine, self.peers.mate)

    def finish(self):
        self.c5.wait_recv()


class PlaneSum:
    def __init__(self, net, me, peers, big, bufs):
        self.net, self.me, self.peers, self.big = net, me, peers, big
        self.r0, self.s1, self.r1, self.s2, self.r2, self.s3, self.r3, self.fin = bufs

    def half(self, core):
        return pl.ds(pl.multiple_of(PLANE_AT + core * PLANE, 256), PLANE)

    def start(self):
        self.c0 = self.net.send(self.big.at[self.half(1 - self.me.core)], self.r0, self.peers.mate)

    def over_x(self):
        self.c0.wait_recv()
        own = self.big[self.half(self.me.core)]
        self.s1[...] = added(own, [self.r0[...]], 1).astype(BF16).reshape(NX, 64, C)
        x = self.me.x
        self.c1 = [
            self.net.send(self.s1.at[lax.rem(x + k, NX)], self.r1.at[k - 1], self.peers.x[k - 1])
            for k in (2, 1, 3)
        ]

    def over_y(self):
        for copy in self.c1:
            copy.wait_recv()
        total = added(self.s1[self.me.x], self.r1, NX - 1).astype(BF16)
        for t in range(NY):
            rows, cols = 16 * (t // 2), 128 * (t % 2)
            self.s2[t] = total[rows : rows + 16, cols : cols + 128]
        y = self.me.y
        self.c2 = [
            self.net.send(self.s2.at[lax.rem(y + k, NY)], self.r2.at[k - 1], self.peers.y[k - 1])
            for k in FAR_FIRST
        ]

    def over_z(self):
        for copy in self.c2:
            copy.wait_recv()
        self.s3[...] = added(self.s2[self.me.y], self.r2, NY - 1).astype(BF16)
        z = self.me.z
        self.r3[z] = self.s3[...]
        self.c3 = [self.net.send(self.s3, self.r3.at[z], self.peers.z[k - 1]) for k in FAR_FIRST]

    def back_y(self):
        for copy in self.c3:
            copy.wait_recv()
        me = self.me
        total = added(self.r3[0], [self.r3[k] for k in range(1, NZ)], NZ - 1)
        at = (lax.rem(me.y, 2), me.core, me.x, me.y // 2)
        self.fin[at] = total.astype(BF16)
        mine = self.fin.at[at]
        self.c4 = [self.net.send(mine, mine, self.peers.y[k - 1]) for k in FAR_FIRST]

    def back_x(self):
        for copy in self.c4:
            copy.wait_recv()
        self.c5 = []
        for k in (2, 1, 3):
            for half in range(2):
                mine = self.fin.at[half, self.me.core, self.me.x]
                self.c5.append(self.net.send(mine, mine, self.peers.x[k - 1]))

    def back_core(self):
        for copy in self.c5:
            copy.wait_recv()
        self.c6 = []
        for half in range(2):
            mine = self.fin.at[half, self.me.core]
            self.c6.append(self.net.send(mine, mine, self.peers.mate))

    def finish(self):
        for copy in self.c6:
            copy.wait_recv()


class SmallSum:
    def __init__(self, net, me, peers, small, bufs):
        self.net, self.me, self.peers, self.small = net, me, peers, small
        self.r0, self.s1, self.r1, self.s2, self.r2, self.s3, self.r3, self.fin = bufs

    def start(self):
        half = pl.ds(pl.multiple_of((1 - self.me.core) * 32, 32), 32)
        self.c0 = self.net.send(self.small.at[half], self.r0, self.peers.mate)

    def over_x(self):
        self.c0.wait_recv()
        own = self.small[pl.ds(pl.multiple_of(self.me.core * 32, 32), 32)]
        self.s1[...] = (own + self.r0[...]).reshape(NX, 8, C)
        x = self.me.x
        self.c1 = [
            self.net.send(self.s1.at[lax.rem(x + k, NX)], self.r1.at[k - 1], self.peers.x[k - 1])
            for k in (2, 1, 3)
        ]

    def over_y(self):
        for copy in self.c1:
            copy.wait_recv()
        self.s2[...] = added(self.s1[self.me.x], self.r1, NX - 1)
        y = self.me.y
        self.r2[y] = self.s2[...]
        self.c2 = [self.net.send(self.s2, self.r2.at[y], self.peers.y[k - 1]) for k in FAR_FIRST]

    def over_z(self):
        for copy in self.c2:
            copy.wait_recv()
        self.s3[...] = jnp.sum(self.r2[...], axis=0)
        z = self.me.z
        self.r3[z] = self.s3[...]
        self.c3 = [self.net.send(self.s3, self.r3.at[z], self.peers.z[k - 1]) for k in FAR_FIRST]

    def back_x(self):
        for copy in self.c3:
            copy.wait_recv()
        me = self.me
        self.fin[me.core, me.x] = jnp.sum(self.r3[...], axis=0)
        mine = self.fin.at[me.core, me.x]
        self.c4 = [self.net.send(mine, mine, self.peers.x[k - 1]) for k in (2, 1, 3)]

    def back_core(self):
        for copy in self.c4:
            copy.wait_recv()
        mine = self.fin.at[self.me.core]
        self.c5 = self.net.send(mine, mine, self.peers.mate)

    def finish(self):
        self.c5.wait_recv()


class Peers:
    def __init__(self, me):
        self.mate = me.at(core=1 - me.core)
        self.x = [me.at(x=lax.rem(me.x + k, NX)) for k in range(1, NX)]
        self.y = [me.at(y=lax.rem(me.y + k, NY)) for k in range(1, NY)]
        self.z = [me.at(z=lax.rem(me.z + k, NZ)) for k in range(1, NZ)]

    def all(self):
        return [self.mate] + self.x + self.y + self.z


SUM_COPIES = (1 + 3 + 7 + 7 + 7 + 6 + 2) + 2 * (1 + 7 + 3 + 7 + 7 + 1) + (1 + 3 + 7 + 7 + 3 + 1)


def sum_scratch():
    cross = [
        pltpu.VMEM((CROSS, C), BF16),
        pltpu.VMEM((8, CHUNK, C), BF16),
        pltpu.VMEM((7, CHUNK, C), BF16),
        pltpu.VMEM((CHUNK, C), BF16),
        pltpu.VMEM((NX, CHUNK, C), BF16),
        pltpu.VMEM((CHUNK, C), BF16),
        pltpu.VMEM((8, CHUNK, C), BF16),
    ]
    return cross * 2 + [
        pltpu.VMEM((PLANE, C), BF16),
        pltpu.VMEM((NX, 64, C), BF16),
        pltpu.VMEM((NX - 1, 64, C), BF16),
        pltpu.VMEM((NY, 16, 128), BF16),
        pltpu.VMEM((NY - 1, 16, 128), BF16),
        pltpu.VMEM((16, 128), BF16),
        pltpu.VMEM((NZ, 16, 128), BF16),
        pltpu.VMEM((32, C), F32),
        pltpu.VMEM((NX, 8, C), F32),
        pltpu.VMEM((NX - 1, 8, C), F32),
        pltpu.VMEM((8, C), F32),
        pltpu.VMEM((NY, 8, C), F32),
        pltpu.VMEM((8, C), F32),
        pltpu.VMEM((NZ, 8, C), F32),
    ]


def sum_sums(by_z, plane, by_y, smalls):
    plane.over_y()
    smalls.over_x()
    by_z.over_x()
    by_y.over_x()
    smalls.over_y()
    smalls.net.settle(20)
    plane.over_z()
    by_z.over_other()
    by_y.over_other()
    smalls.over_z()
    plane.back_y()
    by_z.back_first()
    by_y.back_first()
    smalls.back_x()
    plane.back_x()
    smalls.net.settle(30)
    by_z.back_core()
    smalls.back_core()
    by_y.back_core()
    smalls.net.settle(12)
    plane.back_core()
    smalls.finish()
    by_z.finish()
    by_y.finish()
    plane.finish()


def shared_scratch():
    return [
        pltpu.SMEM((8, 16), jnp.int32),
        pltpu.SMEM((8, 16), jnp.int32),
        pltpu.VMEM((S, S, C), BF16),
        pltpu.VMEM((S, S, C), F32),
        pltpu.VMEM((ROWS, PITCH, C), F32),
        pltpu.VMEM((7, ROWS, S, C), F32),
        pltpu.VMEM((7, S, 8, C), F32),
        pltpu.VMEM((4, 3, S, C), BF16),
        pltpu.VMEM((4, 16, C), F32),
        pltpu.VMEM((C, HID), F32),
        pltpu.VMEM((C, HID), F32),
        pltpu.VMEM((49, 8, C), F32),
        pltpu.VMEM((8, C), F32),
        pltpu.VMEM((2 * HID, C), BF16),
        pltpu.VMEM((64, C), F32),
    ]


def split_refs(refs, *lists):
    refs = list(refs)
    parts = []
    for scratch in lists:
        parts.append(refs[: len(scratch)])
        refs = refs[len(scratch) :]
    return parts + [refs]


def block_kernel(
    ids_in, codes_in, x_in, cot_in, taps_in, gain_in, layer_in, w_in_in, w_out_in,
    fin_z, fin_plane, fin_y, fin_small, *rest,
):
    shared, weights, rims, inner, outer, sums, sems = split_refs(
        rest, shared_scratch(), weight_scratch(), rim_scratch(), inside_scratch(),
        border_scratch(), sum_scratch(),
    )
    ids, codes, xb, xf, fr, fb, fs, sides, corners, gacc, iacc, kg, gain_acc, big, small = shared
    ss, rs, ls = sems
    w = Weights(weights)
    me = Place()
    peers = Peers(me)
    along_y, along_x = rim_partners(me)
    partners = peers.all() + along_y

    barrier = pltpu.get_barrier_semaphore()
    for device in partners:
        pl.semaphore_signal(barrier, inc=1, device_id=device, device_id_type=MESH)
    loads = [
        pltpu.make_async_copy(src, dst, ls.at[i])
        for i, (src, dst) in enumerate(
            (
                (x_in, xb), (ids_in, ids), (codes_in, codes), (taps_in, w.taps_in),
                (gain_in, w.gain), (layer_in, w.layer), (w_in_in, w.w_in), (w_out_in, w.w_out),
                (cot_in, w.cot),
            )
        )
    ]
    for load in loads:
        load.start()
    loads[0].wait()
    own_strips(xb, xf, rims[0], rims[6], me)
    pl.semaphore_wait(barrier, len(partners))

    net = Copies(ss, rs)
    by_y, by_x = both_rims(net, me, ids, codes, along_y, along_x, rims[:6], rims[6:])
    by_y.gather()
    by_x.gather()
    for load in loads[1:]:
        load.wait()

    inside = Inside(w, fb, inner)
    border = Border(w, fb, fs, outer)
    frame_inside(xf, fr)
    shift_rows(fr, fb, 3, S)
    w.taps[...] = w.taps_in[...].astype(F32)
    inside.depthwise()
    w.w_out_t[...] = w.w_out[...].T
    w.w_in_t[...] = w.w_in[...].T
    inside.norm()
    by_x.choose()
    border.cotangent()
    border.hidden_grad()
    for h in range(3):
        inside.hidden(h, gacc, iacc)
    by_y.choose()
    for h in range(3, 4):
        inside.hidden(h, gacc, iacc)
    inside.backward(gain_acc)
    kg[...] = jnp.zeros_like(kg)
    inside.kernel_grad(kg)

    for rim, chans in ((by_y, slice(0, HALF)), (by_x, slice(HALF, C))):
        rim.take(sides, corners, chans, me.space)
        frame_rims(sides, corners, fr, chans)
        shift_rows(fr, fb, 0, 9, chans)
        shift_rows(fr, fb, S - 3, 9, chans)
        shift_sides(fr, fs, chans)
        border.depthwise(chans)
    border.norm()
    border.hidden()
    sum_z = CrossSum(net, me, peers, big, 0, "z", sums[0:7] + [fin_z])
    sum_y = CrossSum(net, me, peers, big, PLANE_AT + 2 * PLANE, "y", sums[7:14] + [fin_y])
    plane = PlaneSum(net, me, peers, big, sums[14:21] + [fin_plane])
    smalls = SmallSum(net, me, peers, small, sums[21:28] + [fin_small])
    scale = border.out_grad(gacc, big)
    sum_z.start()
    border.in_grad(iacc, big)
    plane.start()
    sum_y.start()
    sum_z.over_first()
    border.scaled_grad()
    plane.over_x()
    sum_y.over_first()
    gain = border.backward(gain_acc)
    border.kernel_grad(kg)
    small[0:49] = jnp.sum(kg[...], axis=1)
    small[49:50] = gain
    small[50:51] = scale
    small[51:64] = jnp.zeros((13, C), F32)
    smalls.start()
    sum_sums(sum_z, plane, sum_y, smalls)
    net.finish()


def block_grads(neighbours, codes, tile, cot, kernel, ln_gain, layer_scale, w_in, w_out):
    vmem = pl.BlockSpec(memory_space=pltpu.VMEM)
    copies = RIM_COPIES + SUM_COPIES
    return pl.pallas_call(
        block_kernel,
        out_shape=(
            pltpu.VMEM((2, NZ, CHUNK, C), BF16),
            pltpu.VMEM((2, 2, NX, 4, 16, 128), BF16),
            pltpu.VMEM((2, NY, CHUNK, C), BF16),
            pltpu.VMEM((2, NX, 8, C), F32),
        ),
        in_specs=[pl.BlockSpec(memory_space=pl.ANY)] * 9,
        out_specs=(vmem,) * 4,
        scratch_shapes=shared_scratch() + weight_scratch() + rim_scratch() + inside_scratch()
        + border_scratch() + sum_scratch()
        + [pltpu.SemaphoreType.DMA((copies,))] * 2 + [pltpu.SemaphoreType.DMA((9,))],
        compiler_params=pltpu.CompilerParams(
            collective_id=0, has_side_effects=True, vmem_limit_bytes=60 * 2**20
        ),
    )(
        neighbours, codes, tile, cot, kernel, ln_gain.reshape(1, C), layer_scale.reshape(1, C),
        w_in, w_out,
    )


def hand_over_kernel(
    fin_z, fin_plane, fin_y, small, kg_out, gain_out, scale_out, in_out, out_out, kg, gain, scale, sems
):
    def move(pairs, first):
        copies = [
            pltpu.make_async_copy(src, dst, sems.at[first + i])
            for i, (src, dst) in enumerate(pairs)
        ]
        for copy in copies:
            copy.start()
        return copies

    rest = HID - PLANE_AT
    parts = [(fin_z, out_out.at[pl.ds(0, PLANE_AT)])]
    for q in range(1, HID // C):
        parts.append((fin_y.at[pl.ds(256 * (q - 1), 256)], in_out.at[:, pl.ds(256 * q, 256)]))
    for half in range(2):
        cols = pl.ds(128 * half, 128)
        parts.append((fin_plane.at[half, pl.ds(0, rest)], out_out.at[pl.ds(PLANE_AT, rest), cols]))
        parts.append((fin_plane.at[half, pl.ds(rest, C)], in_out.at[:, cols]))
    copies = move(parts, 0)
    kg[...] = small[0:49]
    gain[...] = small[49:50]
    scale[...] = small[50:51]
    copies += move([(kg, kg_out), (gain, gain_out), (scale, scale_out)], len(parts))
    for copy in copies:
        copy.wait()


def hand_over(fin_z, fin_plane, fin_y, fin_small):
    fins = (
        fin_z.reshape(2 * CROSS, C),
        fin_plane.reshape(2, 2 * PLANE, 128),
        fin_y.reshape(2 * CROSS, C),
        fin_small.reshape(64, C),
    )
    return pl.pallas_call(
        hand_over_kernel,
        out_shape=(
            jax.ShapeDtypeStruct((49, C), F32),
            jax.ShapeDtypeStruct((1, C), F32),
            jax.ShapeDtypeStruct((1, C), F32),
            jax.ShapeDtypeStruct((C, HID), BF16),
            jax.ShapeDtypeStruct((HID, C), BF16),
        ),
        in_specs=[pl.BlockSpec(memory_space=pltpu.VMEM)] * 4,
        out_specs=(pl.BlockSpec(memory_space=pl.ANY),) * 5,
        scratch_shapes=[
            pltpu.VMEM((49, C), F32),
            pltpu.VMEM((1, C), F32),
            pltpu.VMEM((1, C), F32),
            pltpu.SemaphoreType.DMA((11,)),
        ],
        compiler_params=pltpu.CompilerParams(has_side_effects=True),
    )(*[pltpu.with_memory_space_constraint(fin, pltpu.VMEM) for fin in fins])


def on_device(state, cotangent, kernel, ln_gain, w_in, w_out, layer_scale, neighbours, codes):
    sums = block_grads(
        neighbours.T, codes.T, state.reshape(S, S, C), cotangent.reshape(PIX, C), kernel, ln_gain,
        layer_scale, w_in, w_out,
    )
    kernel_grad, gain_grad, scale_grad, in_grad, out_grad = hand_over(*sums)
    return (kernel_grad, gain_grad.reshape(C), scale_grad.reshape(C), in_grad, out_grad)


def solution(mesh):
    placed = (P("dp", "space", None, None, None),) * 2 + (P(),) * 7
    return jax.shard_map(
        on_device, mesh=mesh, in_specs=placed, out_specs=(P(),) * 5, check_vma=False
    )
```
